128 devices in a mesh: frame: 128 (over z, x, y, core).
Axes of the slice: x: 4, y: 4, z: 4, core: 2. Of those that a mesh axis runs over, the one named last changes fastest.
Arguments:
- inputs: bfloat16 [24576, 3072], P('frame'), may hold values from -6 to 6
- queries: bfloat16 [24576, 1536], P('frame'), may hold values from -5 to 5
- keys: bfloat16 [24576, 1536], P('frame'), may hold values from -5 to 5
- values: bfloat16 [24576, 1536], P('frame'), may hold values from -6 to 6
- output_gradient: bfloat16 [24576, 1536], P('frame'), may hold values from -48 to 48
- radial_block_mask: int32 [128, 128], replicated, may hold values from 0 to 1, as said below
- adapter_down_weight: bfloat16 [3, 3072, 64], replicated, may hold values from -0.109375 to 0.109375
- adapter_up_weight: bfloat16 [3, 64, 1536], replicated, may hold values from -0.75 to 0.75
Outputs:
- grad_input: bfloat16 [24576, 3072], P('frame')
- down_gradient: float32 [3, 3072, 64], replicated
- up_gradient: float32 [3, 64, 1536], replicated
The draws below stay inside these ranges and needn't reach their ends.
Inputs may be any that keep to these rules, and one draw needn't show every extreme that they name: radial_block_mask[b, c] is 1 whenever |b - c| <= 1, and 0 unless |b - c| is 0 or a power of two below 128.
All inputs are finite; a program needn't handle non-finite values.
Results may differ from the reference program's by a relative error of at most 0.0099.
Values may be sent and summed in bfloat16 or wider, within the bound.
A program may use at most 192 MiB of HBM per device.

```python
import math
import jax
import jax.numpy as jnp
from jax import lax

MODEL_WIDTH = 3072
DH = 128
ADAPTER_RANK = 64
TOK_DEV = 192
HEAD_FEATURES = 1536
NB = 128
TOKENS = 24576
LEVELS = 7


def draw_queries(key, part):
    key = jax.random.fold_in(key, 11)
    drawn = jax.random.normal(key, (TOKENS, HEAD_FEATURES), jnp.float32)
    return jnp.clip(drawn, -5.0, 5.0).astype(jnp.bfloat16)


def draw_keys(key, part):
    key = jax.random.fold_in(key, 13)
    drawn = jax.random.normal(key, (TOKENS, HEAD_FEATURES), jnp.float32)
    return jnp.clip(drawn, -5.0, 5.0).astype(jnp.bfloat16)


def draw_radial_block_mask(key, part):
    key = jax.random.fold_in(key, 23)
    block_ids = jnp.arange(NB, dtype=jnp.int32)
    distance = jnp.abs(block_ids[:, None] - block_ids[None, :])
    power_two = jnp.bitwise_and(distance, distance - 1) == 0
    coin_flip = jax.random.randint(key, (NB, NB), 0, 2)
    kept = (distance <= 1) | (distance >= 2) & power_two & (coin_flip == 1)
    return kept.astype(jnp.int32)


def levels(key, extent, shards, low, top_value):
    def one(dim, blocks):
        steps = jax.random.uniform(jax.random.fold_in(jax.random.fold_in(key, 6), dim), (blocks,), jnp.float32, low / len(shards), top_value / len(shards))
        return jnp.repeat(jnp.exp(steps), extent[dim] // blocks).reshape((-1,) + (1,) * (len(extent) - dim - 1))

    level = one(*shards[0])
    for cut in shards[1:]:
        level = level * one(*cut)
    return level


def normal_values(stream_key, shape, scale, bound, shards=(), kind=jnp.bfloat16):
    gain = levels(stream_key, shape, shards, -0.22, 0.18) if shards else 1.0
    entries = jax.random.normal(stream_key, shape, jnp.float32) * scale * gain
    return jnp.minimum(jnp.maximum(entries, -bound), bound).astype(kind)


def setup_inputs(seed: int = 0) -> dict:
    splits = jax.random.split(jax.random.key(seed), 9)
    inputs = normal_values(splits[0], (TOKENS, MODEL_WIDTH), 1.0, 6.0, ((0, 128),))
    queries = draw_queries(jax.random.fold_in(splits[8], 71), 0)
    keys = draw_keys(jax.random.fold_in(splits[8], 71), 0)
    values = normal_values(splits[3], (TOKENS, HEAD_FEATURES), 1.0, 6.0, ((0, 128),))
    output_gradient = normal_values(splits[4], (TOKENS, HEAD_FEATURES), 8.0, 48.0, ((0, 128),))
    radial_block_mask = draw_radial_block_mask(jax.random.fold_in(splits[8], 71), 0)
    adapter_down_weight = normal_values(splits[6], (3, MODEL_WIDTH, ADAPTER_RANK), MODEL_WIDTH ** -0.5, 0.109375)
    adapter_up_weight = normal_values(splits[7], (3, ADAPTER_RANK, HEAD_FEATURES), ADAPTER_RANK ** -0.5, 0.75)
    return {"inputs": inputs, "queries": queries, "keys": keys, "values": values, "output_gradient": output_gradient, "radial_block_mask": radial_block_mask, "adapter_down_weight": adapter_down_weight, "adapter_up_weight": adapter_up_weight}


def block_grads(q_block, g_block, key_blocks, val_blocks, keep_bits):
    block_count, row_count, feat_width = key_blocks.shape
    head_count = feat_width // DH
    inv_root = 1.0 / math.sqrt(DH)
    flat_keys = key_blocks.reshape(block_count * row_count, feat_width)
    flat_vals = val_blocks.reshape(block_count * row_count, feat_width)
    live_cols = jnp.repeat(keep_bits, row_count, total_repeat_length=block_count * row_count) > 0.5

    def per_head(head_id, running):
        q_acc, k_acc, v_acc = running
        col_start = (head_id * DH).astype(jnp.int32)
        q_head = lax.dynamic_slice_in_dim(q_block, col_start, DH, 1)
        g_head = lax.dynamic_slice_in_dim(g_block, col_start, DH, 1)
        k_head = lax.dynamic_slice_in_dim(flat_keys, col_start, DH, 1)
        v_head = lax.dynamic_slice_in_dim(flat_vals, col_start, DH, 1)
        scores = jnp.dot(q_head, k_head.T, preferred_element_type=jnp.float32) * inv_root
        scores = jnp.where(live_cols[None, :], scores, -1e+30)
        row_max = lax.optimization_barrier(jnp.max(scores, axis=1, keepdims=True))
        row_sum = lax.optimization_barrier(jnp.sum(jnp.exp(scores - row_max), axis=1, keepdims=True))
        log_total = row_max + jnp.log(row_sum)
        probs = jnp.exp(scores - log_total)
        probs_b = probs.astype(jnp.bfloat16)
        attended = jnp.dot(probs_b, v_head, preferred_element_type=jnp.float32)
        row_dot = lax.optimization_barrier(jnp.sum(g_head.astype(jnp.float32) * attended, axis=1, keepdims=True))
        dprobs = jnp.dot(g_head, v_head.T, preferred_element_type=jnp.float32)
        dscores = (probs * (dprobs - row_dot)).astype(jnp.bfloat16)
        q_grad = jnp.dot(dscores, k_head, preferred_element_type=jnp.float32) * inv_root
        k_grad = (jnp.dot(dscores.T, q_head, preferred_element_type=jnp.float32) * inv_root).astype(jnp.bfloat16)
        v_grad = jnp.dot(probs_b.T, g_head, preferred_element_type=jnp.float32).astype(jnp.bfloat16)
        q_acc = lax.dynamic_update_slice_in_dim(q_acc, q_grad, col_start, 1)
        k_acc = lax.dynamic_update_slice_in_dim(k_acc, k_grad, col_start, 1)
        v_acc = lax.dynamic_update_slice_in_dim(v_acc, v_grad, col_start, 1)
        return (q_acc, k_acc, v_acc)
    start_state = (jnp.zeros((row_count, feat_width), jnp.float32), jnp.zeros((block_count * row_count, feat_width), jnp.bfloat16), jnp.zeros((block_count * row_count, feat_width), jnp.bfloat16))
    q_acc, k_acc, v_acc = lax.fori_loop(0, head_count, per_head, start_state)
    shaped = (block_count, row_count, feat_width)
    return (q_acc, k_acc.reshape(shaped), v_acc.reshape(shaped))

def adapter_gradient_list(inputs, projection_gradients, adapter_down_weight, adapter_up_weight, norm_scale_factor):
    input_gradient = jnp.zeros((inputs.shape[0], inputs.shape[1]), jnp.float32)
    downs = []
    ups = []
    for projection_choice in range(3):
        output_projection = projection_gradients[projection_choice].astype(jnp.bfloat16)
        lowrank_projection = jnp.dot(inputs, adapter_down_weight[projection_choice], preferred_element_type=jnp.float32).astype(jnp.bfloat16)
        ups.append(jnp.dot(lowrank_projection.T, output_projection, preferred_element_type=jnp.float32) * norm_scale_factor)
        backward_projection = jnp.dot(output_projection, adapter_up_weight[projection_choice].T, preferred_element_type=jnp.float32).astype(jnp.bfloat16)
        downs.append(jnp.dot(inputs.T, backward_projection, preferred_element_type=jnp.float32) * norm_scale_factor)
        input_gradient = input_gradient + jnp.dot(backward_projection, adapter_down_weight[projection_choice].T, preferred_element_type=jnp.float32)
    return (input_gradient, jnp.stack(downs), jnp.stack(ups))

def reference(inputs, queries, keys, values, output_gradient, radial_block_mask, adapter_down_weight, adapter_up_weight):
    offsets = [0] + [direction * 2 ** level for level in range(LEVELS) for direction in (1, -1)]

    def per_block(running, block_id):
        key_sum, val_sum = running
        row_start = (block_id * TOK_DEV).astype(jnp.int32)
        q_block = lax.dynamic_slice_in_dim(queries, row_start, TOK_DEV, 0)
        g_block = lax.dynamic_slice_in_dim(output_gradient, row_start, TOK_DEV, 0)
        mask_row = radial_block_mask[block_id]
        firsts = []
        key_list = []
        val_list = []
        keep_list = []
        for offset in offsets:
            target = block_id - offset
            inside = (target >= 0) & (target < NB)
            clipped = jnp.clip(target, 0, NB - 1).astype(jnp.int32)
            first_row = (clipped * TOK_DEV).astype(jnp.int32)
            firsts.append(first_row)
            key_list.append(lax.dynamic_slice_in_dim(keys, first_row, TOK_DEV, 0))
            val_list.append(lax.dynamic_slice_in_dim(values, first_row, TOK_DEV, 0))
            keep_list.append(jnp.where(inside, mask_row[clipped], 0).astype(jnp.float32))
        q_grad, key_parts, val_parts = block_grads(q_block, g_block, jnp.stack(key_list), jnp.stack(val_list), jnp.stack(keep_list))
        for position in range(len(offsets)):
            first_row = firsts[position]
            key_now = lax.dynamic_slice_in_dim(key_sum, first_row, TOK_DEV, 0)
            key_sum = lax.dynamic_update_slice_in_dim(key_sum, key_now + key_parts[position].astype(jnp.float32), first_row, 0)
            val_now = lax.dynamic_slice_in_dim(val_sum, first_row, TOK_DEV, 0)
            val_sum = lax.dynamic_update_slice_in_dim(val_sum, val_now + val_parts[position].astype(jnp.float32), first_row, 0)
        return ((key_sum, val_sum), q_grad)
    zeros_all = jnp.zeros((TOKENS, HEAD_FEATURES), jnp.float32)
    (key_gradient, value_gradient), q_blocks = lax.scan(per_block, (zeros_all, zeros_all), jnp.arange(NB, dtype=jnp.int32))
    query_gradient = q_blocks.reshape(TOKENS, HEAD_FEATURES)
    norm_scale_factor = 1.0 / math.sqrt(TOKENS)
    input_gradient, down_gradient, up_gradient = adapter_gradient_list(inputs, (query_gradient, key_gradient, value_gradient), adapter_down_weight, adapter_up_weight, norm_scale_factor)
    return (input_gradient.astype(jnp.bfloat16), down_gradient, up_gradient)
```

```python
import functools
import math

import jax
import jax.numpy as jnp
from jax import lax
from jax.experimental import pallas as pl
from jax.experimental.pallas import tpu as pltpu
from jax.sharding import PartitionSpec as P

MESH = pl.DeviceIdType.MESH
DH = 128
HEADS = 12
TOK = 192
RANK = 64
WIDTH = 3072
FEAT = HEADS * DH
OWN, PARTNER, SIDE = 0, 1, 2
SLOT = {1: 3, -1: 4, 2: 5, -2: 6, 4: 7, -4: 8, 8: 9, -8: 10, 16: 11, -16: 12, 32: 13, -32: 14}
SLOTS = 15
VIA_Y, VIA_Z = 15, 16
KEYS = SLOTS * TOK
PAD = 3072
TILES = [(0, 512), (512, 512), (1024, 512), (1536, 512), (2048, 512), (2560, 320)]
ROOT = 1.0 / math.sqrt(DH)
MASKED = -1e30


def nt(a, b):
    return lax.dot_general(a, b, (((1,), (1,)), ((), ())), preferred_element_type=jnp.float32)


def nn(a, b):
    return lax.dot_general(a, b, (((1,), (0,)), ((), ())), preferred_element_type=jnp.float32)


def pick(cond, a, b):
    return jnp.where(cond, a, b)


def hops(d, z, x, y):
    if abs(d) == 16:
        return 1
    if d == 4:
        return pick(x == 0, 2, 1)
    if d == -4:
        return pick(x == 3, 2, 1)
    if d == 1:
        return pick(y == 0, pick(x == 0, 3, 2), 1)
    if d == -1:
        return pick(y == 3, pick(x == 3, 3, 2), 1)
    if d == 8:
        return pick(x >= 2, 2, 3)
    if d == -8:
        return pick(x <= 1, 2, 3)
    if abs(d) == 32:
        return 2
    if d == 2:
        return pick(y >= 2, 2, pick(x == 0, 4, 3))
    return pick(y <= 1, 2, pick(x == 3, 4, 3))


def attention_kernel(
    mask_ref, x_ref, q_ref, g_ref, k_ref, v_ref, down_ref, up_ref,
    back_out, upgrad_out,
    buf, lowbuf, bias, s_ref, d_ref, acc, back0, lowt0, rsend, rrecv,
    load_sem, send_sem, recv_sem, lsend, lrecv, rs_send, rs_recv,
):
    me = lax.axis_index("frame")
    i = me // 2
    c = me % 2
    z = i // 16
    x = (i // 4) % 4
    y = i % 4

    def dev(zz, xx, yy, cc):
        return ((zz + 4) % 4) * 32 + ((xx + 4) % 4) * 8 + ((yy + 4) % 4) * 2 + cc

    yp, ym = dev(z, x, y + 1, c), dev(z, x, y - 1, c)
    xp, xm = dev(z, x + 1, y, c), dev(z, x - 1, y, c)
    zp, zm = dev(z + 1, x, y, c), dev(z - 1, x, y, c)
    pt = dev(z, x, y, 1 - c)
    side = pick(c == 0, me - 1, me + 1)
    side_ok = (side >= 0) & (side < 128)

    def valid(d):
        return (i - d >= 0) & (i - d < 64)

    def rows(s):
        return pl.ds(s * TOK, TOK)

    barrier = pltpu.get_barrier_semaphore()
    for d in (yp, ym, xp, xm, zp, zm, pt):
        pl.semaphore_signal(barrier, inc=1, device_id=(d,), device_id_type=MESH)
    count = jnp.int32(7)
    for d in SLOT:
        count = count + pick(valid(d), 1, 0)

        @pl.when(valid(d))
        def _(d=d):
            pl.semaphore_signal(barrier, inc=1, device_id=(me - 2 * d,), device_id_type=MESH)

    count = count + pick(side_ok, 1, 0)

    @pl.when(side_ok)
    def _():
        pl.semaphore_signal(barrier, inc=1, device_id=(side,), device_id_type=MESH)

    def load(h, a):
        ref = (k_ref, v_ref)[a]
        return pltpu.make_async_copy(
            ref.at[:, pl.ds(h * DH, DH)], buf.at[h, a, rows(OWN)], load_sem.at[h, a]
        )

    for h in range(HEADS):
        for a in range(2):
            load(h, a).start()

    every = [(d, SLOT[d]) for d in SLOT]
    for d, s in every:
        @pl.when(jnp.logical_not(valid(d)))
        def _(s=s):
            lowbuf[rows(s), :] = jnp.zeros((TOK, DH), jnp.bfloat16)
            rrecv[s] = jnp.zeros((2 * RANK, TOK), jnp.bfloat16)

            def zero(h, _):
                for a in range(2):
                    buf[h, a, rows(s), :] = jnp.zeros((TOK, DH), jnp.bfloat16)
                return 0

            lax.fori_loop(0, HEADS, zero, 0)

    @pl.when(jnp.logical_not(side_ok))
    def _():
        lowbuf[rows(SIDE), :] = jnp.zeros((TOK, DH), jnp.bfloat16)
        rrecv[SIDE] = jnp.zeros((2 * RANK, TOK), jnp.bfloat16)

        def zero(h, _):
            for a in range(2):
                buf[h, a, rows(SIDE), :] = jnp.zeros((TOK, DH), jnp.bfloat16)
            return 0

        lax.fori_loop(0, HEADS, zero, 0)

    lane = lax.broadcasted_iota(jnp.int32, (8, PAD), 1)
    total_bias = jnp.zeros((8, PAD), jnp.float32)
    for s, (block, ok) in enumerate(
        [(me, None), (pt, None), (side, side_ok)] + [(me - 2 * d, valid(d)) for d in SLOT]
    ):
        kept = mask_ref[me, jnp.clip(block, 0, 127)]
        value = jnp.where(kept > 0, 0.0, MASKED)
        if ok is not None:
            value = jnp.where(ok, value, MASKED)
        inside = (lane >= s * TOK) & (lane < (s + 1) * TOK)
        total_bias = jnp.where(inside, value, total_bias)
    bias[...] = total_bias

    low = nt(x_ref[...], down_ref[...]).astype(jnp.bfloat16)
    lowt0[...] = nt(down_ref[0:RANK, :], x_ref[...]).astype(jnp.bfloat16)
    lowbuf[rows(OWN), :] = low[:, RANK:]
    acc[...] = jnp.zeros_like(acc)
    back0[...] = jnp.zeros_like(back0)

    def low_copy(s, device):
        return pltpu.make_async_remote_copy(
            src_ref=lowbuf.at[rows(OWN)], dst_ref=lowbuf.at[rows(s)],
            send_sem=lsend.at[s], recv_sem=lrecv.at[s],
            device_id=(device,), device_id_type=MESH,
        )

    def back_copy(s, device):
        return pltpu.make_async_remote_copy(
            src_ref=rsend.at[s], dst_ref=rrecv.at[s],
            send_sem=rs_send.at[s], recv_sem=rs_recv.at[s],
            device_id=(device,), device_id_type=MESH,
        )

    direct = [(PARTNER, None, None, pt, pt), (SIDE, side_ok, side_ok, side, side)]
    direct += [(SLOT[d], valid(-d), valid(d), me + 2 * d, me - 2 * d) for d in SLOT]

    def guarded(cond, f):
        if cond is None:
            f()
        else:
            pl.when(cond)(f)

    def copy(kind, h, src, dst, device):
        return pltpu.make_async_remote_copy(
            src_ref=buf.at[h, :, rows(src)], dst_ref=buf.at[h, :, rows(dst)],
            send_sem=send_sem.at[kind, h], recv_sem=recv_sem.at[dst, h],
            device_id=(device,), device_id_type=MESH,
        )

    kinds = []

    def kind(cond, src, dst, device):
        kinds.append((cond, src, dst, device))
        return len(kinds) - 1

    mid = (x == 1) | (x == 2)

    def by_ring_up(xx, h):
        return (xx == 0) | (((xx == 1) | (xx == 2)) & (h % 2 == 0))

    def by_ring_down(xx, h):
        return (xx == 3) | (((xx == 1) | (xx == 2)) & (h % 2 == 1))

    def late(h):
        return (h // 2) % 2 == 0

    def up_here(h):
        return by_ring_up(x, h)

    def down_here(h):
        return by_ring_down(x, h)

    def always(cond):
        return lambda h: cond

    own = [
        kind(None, OWN, PARTNER, pt),
        kind(always(y < 3), OWN, SLOT[1], yp), kind(always(y > 0), OWN, SLOT[-1], ym),
        kind(always(x < 3), OWN, SLOT[4], xp), kind(always(x > 0), OWN, SLOT[-4], xm),
        kind(always(z < 3), OWN, SLOT[16], zp), kind(always(z > 0), OWN, SLOT[-16], zm),
        kind(always((z == 0) & (x == 0)), OWN, VIA_Z, zm),
        kind(always((z == 3) & (x == 3)), OWN, VIA_Z, zp),
    ]
    on = {}
    on[16] = [
        kind(always((z == 1) & (x != 0)), SLOT[16], SLOT[32], zp),
        kind(always(z == 3), SLOT[16], SLOT[-32], zp),
        kind(always((x == 3) & (z > 0)), SLOT[16], SLOT[4], xp),
    ]
    on[-16] = [
        kind(always((z == 2) & (x != 3)), SLOT[-16], SLOT[-32], zm),
        kind(always(z == 0), SLOT[-16], SLOT[32], zm),
        kind(always((x == 0) & (z < 3)), SLOT[-16], SLOT[-4], xm),
    ]
    on["z"] = [
        kind(always((z == 3) & (x == 0)), VIA_Z, SLOT[32], zm),
        kind(always((z == 0) & (x == 3)), VIA_Z, SLOT[-32], zp),
    ]
    on[4] = [
        kind(always((x < 2) & valid(4)), SLOT[4], SLOT[8], xp),
        kind(always(x == 3), SLOT[4], SLOT[-8], xp),
        kind(always((y == 3) & valid(4)), SLOT[4], SLOT[1], yp),
        kind(lambda h: (y == 2) & valid(4) & up_here(h), SLOT[4], VIA_Y, yp),
    ]
    on[-4] = [
        kind(always((x > 1) & valid(-4)), SLOT[-4], SLOT[-8], xm),
        kind(always(x == 0), SLOT[-4], SLOT[8], xm),
        kind(always((y == 0) & valid(-4)), SLOT[-4], SLOT[-1], ym),
        kind(lambda h: (y == 1) & valid(-4) & down_here(h), SLOT[-4], VIA_Y, ym),
    ]
    on[1] = [
        kind(lambda h: valid(1) & ((y < 2) | ((y == 2) & jnp.logical_not(up_here(h)))), SLOT[1], SLOT[2], yp),
        kind(lambda h: (y == 3) & jnp.logical_not(up_here(h)), SLOT[1], SLOT[-2], yp),
        kind(always((c == 1) & valid(1)), SLOT[1], SIDE, pt),
        kind(
            lambda h: (y == 3) & (x < 3) & jnp.logical_not(by_ring_up(x + 1, h)) & jnp.logical_not(late(h)),
            SLOT[1], VIA_Y, xp,
        ),
    ]
    on[-1] = [
        kind(lambda h: valid(-1) & ((y > 1) | ((y == 1) & up_here(h))), SLOT[-1], SLOT[-2], ym),
        kind(lambda h: (y == 0) & up_here(h), SLOT[-1], SLOT[2], ym),
        kind(always((c == 0) & valid(-1)), SLOT[-1], SIDE, pt),
        kind(
            lambda h: (y == 0) & (x > 0) & jnp.logical_not(by_ring_down(x - 1, h)) & jnp.logical_not(late(h)),
            SLOT[-1], VIA_Y, xm,
        ),
    ]

    def has_via_y(h):
        up = (y == 3) & ((z > 0) | (x > 0)) & (up_here(h) | jnp.logical_not(late(h)))
        down = (y == 0) & ((z < 3) | (x < 3)) & (down_here(h) | jnp.logical_not(late(h)))
        return up | down

    via_z = ((z == 3) & (x == 0)) | ((z == 0) & (x == 3))
    on["y"] = [
        kind(lambda h: (y == 3) & has_via_y(h), VIA_Y, SLOT[2], yp),
        kind(lambda h: (y == 0) & has_via_y(h), VIA_Y, SLOT[-2], ym),
    ]
    on[2] = [
        kind(lambda h: (y == 3) & (x > 0) & jnp.logical_not(by_ring_down(x - 1, h)) & late(h), SLOT[2], SLOT[-2], xm),
    ]
    on[-2] = [
        kind(lambda h: (y == 0) & (x < 3) & jnp.logical_not(by_ring_up(x + 1, h)) & late(h), SLOT[-2], SLOT[2], xp),
    ]
    on[8] = [kind(always((x == 3) & (z > 0)), SLOT[8], SLOT[-8], zm)]
    on[-8] = [kind(always((x == 0) & (z < 3)), SLOT[-8], SLOT[8], zp)]
    on[32] = []
    on[-32] = []

    def slot_of(d):
        return VIA_Y if d == "y" else VIA_Z if d == "z" else SLOT[d]

    def comes(d, h):
        return has_via_y(h) if d == "y" else via_z if d == "z" else valid(d)

    def lag(d):
        if d == "z":
            return 1
        if d == "y":
            return pick(((y == 3) & (x == 0)) | ((y == 0) & (x == 3)), 3, 2)
        return hops(d, z, x, y)

    def send(k, h):
        cond, src, dst, device = kinds[k]
        guarded(None if cond is None else cond(h), lambda: copy(k, h, src, dst, device).start())

    def arrived(s, h):
        copy(0, h, s, s, pt).wait_recv()

    def head(h):
        cols = pl.ds(pl.multiple_of(h * DH, DH), DH)
        q = q_ref[:, cols]
        g = g_ref[:, cols]
        top = None
        for t0, w in TILES:
            kt = buf[h, 0, pl.ds(t0, w), :]
            s = nt(q, kt) * (ROOT * math.log2(math.e)) + bias[0:1, t0:t0 + w]
            s_ref[:, t0:t0 + w] = s
            m = jnp.max(s, axis=1, keepdims=True)
            top = m if top is None else jnp.maximum(top, m)
        total = jnp.zeros((TOK, 1), jnp.float32)
        dot = jnp.zeros((TOK, 1), jnp.float32)
        for t0, w in TILES:
            e = jnp.exp2(s_ref[:, t0:t0 + w] - top)
            s_ref[:, t0:t0 + w] = e
            dp = nt(g, buf[h, 1, pl.ds(t0, w), :])
            d_ref[:, t0:t0 + w] = dp
            total = total + jnp.sum(e, axis=1, keepdims=True)
            dot = dot + jnp.sum(e * dp, axis=1, keepdims=True)
        inv = 1.0 / total
        dot = dot * inv
        qu = (nt(up_ref[1, :, cols], q) * ROOT).astype(jnp.bfloat16)
        gu = nt(up_ref[2, :, cols], g).astype(jnp.bfloat16)
        both = jnp.zeros((TOK, 2 * DH), jnp.float32)
        vlow = jnp.zeros((TOK, DH), jnp.float32)
        for t0, w in TILES:
            p = s_ref[:, t0:t0 + w] * inv
            pb = p.astype(jnp.bfloat16)
            ds = (p * (d_ref[:, t0:t0 + w] - dot)).astype(jnp.bfloat16)
            kt = buf[h, 0, pl.ds(t0, w), :]
            lt = lowbuf[pl.ds(t0, w), :]
            both = both + nn(ds, jnp.concatenate([kt, lt], axis=1))
            vlow = vlow + nn(pb, lt)
            acc[0:RANK, t0:t0 + w] += nn(qu, ds)
            acc[RANK:, t0:t0 + w] += nn(gu, pb)
        out0 = (both[:, 0:DH] * ROOT).astype(jnp.bfloat16)
        klow = both[:, DH:DH + RANK] * ROOT
        upgrad_out[0, :, cols] = nn(lowt0[...], out0)
        back0[...] += nt(up_ref[0, :, cols], out0)
        lows = jnp.concatenate([klow, vlow[:, RANK:]], axis=1).T.astype(jnp.bfloat16)
        upgrad_out[1, :, cols] = nn(lows[0:RANK], q)
        upgrad_out[2, :, cols] = nn(lows[RANK:], g)

    pl.semaphore_wait(barrier, count)

    last = 4
    order = [16, -16, 4, -4, 1, -1, "z", "y", 8, -8, 2, -2, 32, -32]

    def step(r, _):
        @pl.when(r < HEADS)
        def _():
            for a in range(2):
                load(r, a).wait()
            for k in own:
                send(k, r)

        for d in order:
            h = r - lag(d)

            @pl.when((h >= 0) & (h < HEADS) & comes(d, h))
            def _(d=d, h=h):
                arrived(slot_of(d), h)
                for k in on[d]:
                    send(k, h)

        @pl.when(r == 0)
        def _():
            for s, goes, _, to, _ in direct:
                guarded(goes, low_copy(s, to).start)

        @pl.when(r == last)
        def _():
            for s, _, comes_in, _, _ in direct:
                guarded(comes_in, low_copy(s, pt).wait_recv)

        h = r - last

        @pl.when((h >= 0) & (h < HEADS))
        def _():
            arrived(PARTNER, h)

            @pl.when(((c == 0) & valid(1)) | ((c == 1) & valid(-1)))
            def _():
                arrived(SIDE, h)

            head(h)

        return 0

    lax.fori_loop(0, HEADS + last, step, 0)

    for s, _, goes, _, to in direct:
        rsend[s] = acc[:, s * TOK:(s + 1) * TOK].astype(jnp.bfloat16)
        guarded(goes, back_copy(s, to).start)
    total = acc[:, 0:TOK]
    for s, comes_in, _, _, _ in direct:
        guarded(comes_in, back_copy(s, pt).wait_recv)
        total = total + rrecv[s].astype(jnp.float32)
    back_out[0:RANK, :] = back0[...].astype(jnp.bfloat16)
    back_out[RANK:, :] = total.astype(jnp.bfloat16)

    for s, goes, returns, to, owner in direct:
        guarded(goes, low_copy(s, to).wait_send)
        guarded(returns, back_copy(s, owner).wait_send)

    def drain(h, _):
        for k, (cond, src, dst, device) in enumerate(kinds):
            guarded(
                None if cond is None else cond(h),
                lambda: copy(k, h, src, dst, device).wait_send(),
            )
        return 0

    lax.fori_loop(0, HEADS, drain, 0)


def attention(mask, inputs, queries, output_gradient, keys, values, down_t, up):
    vm = pl.BlockSpec(memory_space=pltpu.VMEM)
    dma = pltpu.SemaphoreType.DMA
    return pl.pallas_call(
        attention_kernel,
        out_shape=(
            jax.ShapeDtypeStruct((3 * RANK, TOK), jnp.bfloat16),
            jax.ShapeDtypeStruct((3, RANK, FEAT), jnp.float32),
        ),
        in_specs=[pl.BlockSpec(memory_space=pltpu.SMEM), vm, vm, vm,
                  pl.BlockSpec(memory_space=pl.ANY), pl.BlockSpec(memory_space=pl.ANY), vm, vm],
        out_specs=(vm, vm),
        scratch_shapes=[
            pltpu.VMEM((HEADS, 2, (SLOTS + 2) * TOK, DH), jnp.bfloat16),
            pltpu.VMEM((KEYS, DH), jnp.bfloat16),
            pltpu.VMEM((8, PAD), jnp.float32),
            pltpu.VMEM((TOK, PAD), jnp.float32),
            pltpu.VMEM((TOK, PAD), jnp.float32),
            pltpu.VMEM((2 * RANK, PAD), jnp.float32),
            pltpu.VMEM((RANK, TOK), jnp.float32),
            pltpu.VMEM((RANK, TOK), jnp.bfloat16),
            pltpu.VMEM((SLOTS, 2 * RANK, TOK), jnp.bfloat16),
            pltpu.VMEM((SLOTS, 2 * RANK, TOK), jnp.bfloat16),
            dma((HEADS, 2)),
            dma((39, HEADS)),
            dma((SLOTS + 2, HEADS)),
            dma((SLOTS,)), dma((SLOTS,)), dma((SLOTS,)), dma((SLOTS,)),
        ],
        compiler_params=pltpu.CompilerParams(
            collective_id=0, has_side_effects=True, vmem_limit_bytes=56 * 2**20
        ),
        cost_estimate=pl.CostEstimate(flops=12 * 10**9, bytes_accessed=8 * 10**6, transcendentals=7 * 10**6),
        name="attention_gradients",
    )(mask, inputs, queries, output_gradient, keys, values, down_t, up)


def per_device(
    inputs, queries, keys, values, output_gradient, radial_block_mask,
    adapter_down_weight, adapter_up_weight,
):
    axis_size = lax.axis_size("frame")
    norm = 1.0 / math.sqrt(TOK * axis_size)
    down_t = jnp.swapaxes(adapter_down_weight, 1, 2).reshape(3 * RANK, WIDTH)
    back, up_terms = attention(
        radial_block_mask, inputs, queries, output_gradient, keys, values, down_t, adapter_up_weight
    )
    down_terms = nn(back, inputs) * norm
    input_gradient = lax.dot_general(
        back, down_t, (((0,), (0,)), ((), ())), preferred_element_type=jnp.float32
    )
    down, up = lax.psum((down_terms, up_terms * norm), "frame")
    down = jnp.swapaxes(down.reshape(3, RANK, WIDTH), 1, 2)
    return (input_gradient.astype(jnp.bfloat16), down, up)


def solution(mesh):
    return jax.shard_map(
        per_device,
        mesh=mesh,
        in_specs=(P("frame", None),) * 5 + (P(), P(), P()),
        out_specs=(P("frame", None), P(), P()),
        check_vma=False,
    )
```

```python
import functools
import math

import jax
import jax.numpy as jnp
from jax import lax
from jax.experimental import pallas as pl
from jax.experimental.pallas import tpu as pltpu
from jax.sharding import PartitionSpec as P

MESH = pl.DeviceIdType.MESH
DH = 128
HEADS = 12
TOK = 192
RANK = 64
WIDTH = 3072
FEAT = HEADS * DH
OWN, PARTNER, SIDE = 0, 1, 2
SLOT = {1: 3, -1: 4, 2: 5, -2: 6, 4: 7, -4: 8, 8: 9, -8: 10, 16: 11, -16: 12, 32: 13, -32: 14}
SLOTS = 15
VIA_Y, VIA_Z = 15, 16
KEYS = SLOTS * TOK
PAD = 3072
TILES = [(0, 512), (512, 512), (1024, 512), (1536, 512), (2048, 512), (2560, 320)]
ROOT = 1.0 / math.sqrt(DH)
MASKED = -1e30
CHIPS = 64
NORM = 1.0 / math.sqrt(128 * TOK)
EARLY = 3840
LATE = 3072
PIECE = (16, 256)


def nt(a, b):
    return lax.dot_general(a, b, (((1,), (1,)), ((), ())), preferred_element_type=jnp.float32)


def nn(a, b):
    return lax.dot_general(a, b, (((1,), (0,)), ((), ())), preferred_element_type=jnp.float32)


def pick(cond, a, b):
    return jnp.where(cond, a, b)


def hops(d, z, x, y):
    if abs(d) == 16:
        return 1
    if d == 4:
        return pick(x == 0, 2, 1)
    if d == -4:
        return pick(x == 3, 2, 1)
    if d == 1:
        return pick(y == 0, pick(x == 0, 3, 2), 1)
    if d == -1:
        return pick(y == 3, pick(x == 3, 3, 2), 1)
    if d == 8:
        return pick(x >= 2, 2, 3)
    if d == -8:
        return pick(x <= 1, 2, 3)
    if abs(d) == 32:
        return 2
    if d == 2:
        return pick(y >= 2, 2, pick(x == 0, 4, 3))
    return pick(y <= 1, 2, pick(x == 3, 4, 3))


def attention_kernel(
    mask_ref, x_ref, q_ref, g_ref, k_ref, v_ref, down_ref, up_ref,
    grad_out, down_out, up_out,
    buf, lowbuf, bias, s_ref, d_ref, acc, back0, lowt0, rsend, rrecv,
    x2, upart, upart2, backs, backs2, terms, result, result2, early_in, late_in, early_sum, late_sum,
    load_sem, send_sem, recv_sem, lsend, lrecv, rs_send, rs_recv,
    pair_send, pair_recv, red_send, red_recv, gat_send, gat_recv,
):
    me = lax.axis_index("frame")
    i = me // 2
    c = me % 2
    z = i // 16
    x = (i // 4) % 4
    y = i % 4

    def dev(zz, xx, yy, cc):
        return ((zz + 4) % 4) * 32 + ((xx + 4) % 4) * 8 + ((yy + 4) % 4) * 2 + cc

    yp, ym = dev(z, x, y + 1, c), dev(z, x, y - 1, c)
    xp, xm = dev(z, x + 1, y, c), dev(z, x - 1, y, c)
    zp, zm = dev(z + 1, x, y, c), dev(z - 1, x, y, c)
    pt = dev(z, x, y, 1 - c)
    side = pick(c == 0, me - 1, me + 1)
    side_ok = (side >= 0) & (side < 128)

    def valid(d):
        return (i - d >= 0) & (i - d < 64)

    def rows(s):
        return pl.ds(s * TOK, TOK)

    barrier = pltpu.get_barrier_semaphore()

    def greet(n, _):
        pl.semaphore_signal(barrier, inc=1, device_id=((me + n) % 128,), device_id_type=MESH)
        return 0

    lax.fori_loop(1, 128, greet, 0)

    def load(h, a):
        ref = (k_ref, v_ref)[a]
        return pltpu.make_async_copy(
            ref.at[:, pl.ds(h * DH, DH)], buf.at[h, a, rows(OWN)], load_sem.at[h, a]
        )

    for h in range(HEADS):
        for a in range(2):
            load(h, a).start()

    every = [(d, SLOT[d]) for d in SLOT]
    for d, s in every:
        @pl.when(jnp.logical_not(valid(d)))
        def _(s=s):
            lowbuf[rows(s), :] = jnp.zeros((TOK, DH), jnp.bfloat16)
            rrecv[s] = jnp.zeros((2 * RANK, TOK), jnp.bfloat16)

            def zero(h, _):
                for a in range(2):
                    buf[h, a, rows(s), :] = jnp.zeros((TOK, DH), jnp.bfloat16)
                return 0

            lax.fori_loop(0, HEADS, zero, 0)

    @pl.when(jnp.logical_not(side_ok))
    def _():
        lowbuf[rows(SIDE), :] = jnp.zeros((TOK, DH), jnp.bfloat16)
        rrecv[SIDE] = jnp.zeros((2 * RANK, TOK), jnp.bfloat16)

        def zero(h, _):
            for a in range(2):
                buf[h, a, rows(SIDE), :] = jnp.zeros((TOK, DH), jnp.bfloat16)
            return 0

        lax.fori_loop(0, HEADS, zero, 0)

    lane = lax.broadcasted_iota(jnp.int32, (8, PAD), 1)
    total_bias = jnp.zeros((8, PAD), jnp.float32)
    for s, (block, ok) in enumerate(
        [(me, None), (pt, None), (side, side_ok)] + [(me - 2 * d, valid(d)) for d in SLOT]
    ):
        kept = mask_ref[me, jnp.clip(block, 0, 127)]
        value = jnp.where(kept > 0, 0.0, MASKED)
        if ok is not None:
            value = jnp.where(ok, value, MASKED)
        inside = (lane >= s * TOK) & (lane < (s + 1) * TOK)
        total_bias = jnp.where(inside, value, total_bias)
    bias[...] = total_bias

    low = nt(x_ref[...], down_ref[...]).astype(jnp.bfloat16)
    lowt0[...] = nt(down_ref[0:RANK, :], x_ref[...]).astype(jnp.bfloat16)
    lowbuf[rows(OWN), :] = low[:, RANK:]
    acc[...] = jnp.zeros_like(acc)
    back0[...] = jnp.zeros_like(back0)

    def low_copy(s, device):
        return pltpu.make_async_remote_copy(
            src_ref=lowbuf.at[rows(OWN)], dst_ref=lowbuf.at[rows(s)],
            send_sem=lsend.at[s], recv_sem=lrecv.at[s],
            device_id=(device,), device_id_type=MESH,
        )

    def back_copy(s, device):
        return pltpu.make_async_remote_copy(
            src_ref=rsend.at[s], dst_ref=rrecv.at[s],
            send_sem=rs_send.at[s], recv_sem=rs_recv.at[s],
            device_id=(device,), device_id_type=MESH,
        )

    direct = [(PARTNER, None, None, pt, pt), (SIDE, side_ok, side_ok, side, side)]
    direct += [(SLOT[d], valid(-d), valid(d), me + 2 * d, me - 2 * d) for d in SLOT]

    def guarded(cond, f):
        if cond is None:
            f()
        else:
            pl.when(cond)(f)

    def copy(kind, h, src, dst, device):
        return pltpu.make_async_remote_copy(
            src_ref=buf.at[h, :, rows(src)], dst_ref=buf.at[h, :, rows(dst)],
            send_sem=send_sem.at[kind, h], recv_sem=recv_sem.at[dst, h],
            device_id=(device,), device_id_type=MESH,
        )

    kinds = []

    def kind(cond, src, dst, device):
        kinds.append((cond, src, dst, device))
        return len(kinds) - 1

    mid = (x == 1) | (x == 2)

    def by_ring_up(xx, h):
        return (xx == 0) | (((xx == 1) | (xx == 2)) & (h % 2 == 0))

    def by_ring_down(xx, h):
        return (xx == 3) | (((xx == 1) | (xx == 2)) & (h % 2 == 1))

    def late(h):
        return (h // 2) % 2 == 0

    def up_here(h):
        return by_ring_up(x, h)

    def down_here(h):
        return by_ring_down(x, h)

    def always(cond):
        return lambda h: cond

    own = [
        kind(None, OWN, PARTNER, pt),
        kind(always(y < 3), OWN, SLOT[1], yp), kind(always(y > 0), OWN, SLOT[-1], ym),
        kind(always(x < 3), OWN, SLOT[4], xp), kind(always(x > 0), OWN, SLOT[-4], xm),
        kind(always(z < 3), OWN, SLOT[16], zp), kind(always(z > 0), OWN, SLOT[-16], zm),
        kind(always((z == 0) & (x == 0)), OWN, VIA_Z, zm),
        kind(always((z == 3) & (x == 3)), OWN, VIA_Z, zp),
    ]
    on = {}
    on[16] = [
        kind(always((z == 1) & (x != 0)), SLOT[16], SLOT[32], zp),
        kind(always(z == 3), SLOT[16], SLOT[-32], zp),
        kind(always((x == 3) & (z > 0)), SLOT[16], SLOT[4], xp),
    ]
    on[-16] = [
        kind(always((z == 2) & (x != 3)), SLOT[-16], SLOT[-32], zm),
        kind(always(z == 0), SLOT[-16], SLOT[32], zm),
        kind(always((x == 0) & (z < 3)), SLOT[-16], SLOT[-4], xm),
    ]
    on["z"] = [
        kind(always((z == 3) & (x == 0)), VIA_Z, SLOT[32], zm),
        kind(always((z == 0) & (x == 3)), VIA_Z, SLOT[-32], zp),
    ]
    on[4] = [
        kind(always((x < 2) & valid(4)), SLOT[4], SLOT[8], xp),
        kind(always(x == 3), SLOT[4], SLOT[-8], xp),
        kind(always((y == 3) & valid(4)), SLOT[4], SLOT[1], yp),
        kind(lambda h: (y == 2) & valid(4) & up_here(h), SLOT[4], VIA_Y, yp),
    ]
    on[-4] = [
        kind(always((x > 1) & valid(-4)), SLOT[-4], SLOT[-8], xm),
        kind(always(x == 0), SLOT[-4], SLOT[8], xm),
        kind(always((y == 0) & valid(-4)), SLOT[-4], SLOT[-1], ym),
        kind(lambda h: (y == 1) & valid(-4) & down_here(h), SLOT[-4], VIA_Y, ym),
    ]
    on[1] = [
        kind(lambda h: valid(1) & ((y < 2) | ((y == 2) & jnp.logical_not(up_here(h)))), SLOT[1], SLOT[2], yp),
        kind(lambda h: (y == 3) & jnp.logical_not(up_here(h)), SLOT[1], SLOT[-2], yp),
        kind(always((c == 1) & valid(1)), SLOT[1], SIDE, pt),
        kind(
            lambda h: (y == 3) & (x < 3) & jnp.logical_not(by_ring_up(x + 1, h)) & jnp.logical_not(late(h)),
            SLOT[1], VIA_Y, xp,
        ),
    ]
    on[-1] = [
        kind(lambda h: valid(-1) & ((y > 1) | ((y == 1) & up_here(h))), SLOT[-1], SLOT[-2], ym),
        kind(lambda h: (y == 0) & up_here(h), SLOT[-1], SLOT[2], ym),
        kind(always((c == 0) & valid(-1)), SLOT[-1], SIDE, pt),
        kind(
            lambda h: (y == 0) & (x > 0) & jnp.logical_not(by_ring_down(x - 1, h)) & jnp.logical_not(late(h)),
            SLOT[-1], VIA_Y, xm,
        ),
    ]

    def has_via_y(h):
        up = (y == 3) & ((z > 0) | (x > 0)) & (up_here(h) | jnp.logical_not(late(h)))
        down = (y == 0) & ((z < 3) | (x < 3)) & (down_here(h) | jnp.logical_not(late(h)))
        return up | down

    via_z = ((z == 3) & (x == 0)) | ((z == 0) & (x == 3))
    on["y"] = [
        kind(lambda h: (y == 3) & has_via_y(h), VIA_Y, SLOT[2], yp),
        kind(lambda h: (y == 0) & has_via_y(h), VIA_Y, SLOT[-2], ym),
    ]
    on[2] = [
        kind(lambda h: (y == 3) & (x > 0) & jnp.logical_not(by_ring_down(x - 1, h)) & late(h), SLOT[2], SLOT[-2], xm),
    ]
    on[-2] = [
        kind(lambda h: (y == 0) & (x < 3) & jnp.logical_not(by_ring_up(x + 1, h)) & late(h), SLOT[-2], SLOT[2], xp),
    ]
    on[8] = [kind(always((x == 3) & (z > 0)), SLOT[8], SLOT[-8], zm)]
    on[-8] = [kind(always((x == 0) & (z < 3)), SLOT[-8], SLOT[8], zp)]
    on[32] = []
    on[-32] = []

    def slot_of(d):
        return VIA_Y if d == "y" else VIA_Z if d == "z" else SLOT[d]

    def comes(d, h):
        return has_via_y(h) if d == "y" else via_z if d == "z" else valid(d)

    def lag(d):
        if d == "z":
            return 1
        if d == "y":
            return pick(((y == 3) & (x == 0)) | ((y == 0) & (x == 3)), 3, 2)
        return hops(d, z, x, y)

    def send(k, h):
        cond, src, dst, device = kinds[k]
        guarded(None if cond is None else cond(h), lambda: copy(k, h, src, dst, device).start())

    def arrived(s, h):
        copy(0, h, s, s, pt).wait_recv()

    def head(h):
        cols = pl.ds(pl.multiple_of(h * DH, DH), DH)
        q = q_ref[:, cols]
        g = g_ref[:, cols]
        top = None
        for t0, w in TILES:
            kt = buf[h, 0, pl.ds(t0, w), :]
            s = nt(q, kt) * (ROOT * math.log2(math.e)) + bias[0:1, t0:t0 + w]
            s_ref[:, t0:t0 + w] = s
            m = jnp.max(s, axis=1, keepdims=True)
            top = m if top is None else jnp.maximum(top, m)
        total = jnp.zeros((TOK, 1), jnp.float32)
        dot = jnp.zeros((TOK, 1), jnp.float32)
        for t0, w in TILES:
            e = jnp.exp2(s_ref[:, t0:t0 + w] - top)
            s_ref[:, t0:t0 + w] = e
            dp = nt(g, buf[h, 1, pl.ds(t0, w), :])
            d_ref[:, t0:t0 + w] = dp
            total = total + jnp.sum(e, axis=1, keepdims=True)
            dot = dot + jnp.sum(e * dp, axis=1, keepdims=True)
        inv = 1.0 / total
        dot = dot * inv
        qu = (nt(up_ref[1, :, cols], q) * ROOT).astype(jnp.bfloat16)
        gu = nt(up_ref[2, :, cols], g).astype(jnp.bfloat16)
        both = jnp.zeros((TOK, 2 * DH), jnp.float32)
        vlow = jnp.zeros((TOK, DH), jnp.float32)
        for t0, w in TILES:
            p = s_ref[:, t0:t0 + w] * inv
            pb = p.astype(jnp.bfloat16)
            ds = (p * (d_ref[:, t0:t0 + w] - dot)).astype(jnp.bfloat16)
            kt = buf[h, 0, pl.ds(t0, w), :]
            lt = lowbuf[pl.ds(t0, w), :]
            both = both + nn(ds, jnp.concatenate([kt, lt], axis=1))
            vlow = vlow + nn(pb, lt)
            acc[0:RANK, t0:t0 + w] += nn(qu, ds)
            acc[RANK:, t0:t0 + w] += nn(gu, pb)
        out0 = (both[:, 0:DH] * ROOT).astype(jnp.bfloat16)
        klow = both[:, DH:DH + RANK] * ROOT
        upart[0:RANK, cols] = (nn(lowt0[...], out0) * NORM).astype(jnp.bfloat16)
        back0[...] += nt(up_ref[0, :, cols], out0)
        lows = jnp.concatenate([klow, vlow[:, RANK:]], axis=1).T.astype(jnp.bfloat16)
        upart[RANK:2 * RANK, cols] = (nn(lows[0:RANK], q) * NORM).astype(jnp.bfloat16)
        upart[2 * RANK:, cols] = (nn(lows[RANK:], g) * NORM).astype(jnp.bfloat16)

    pl.semaphore_wait(barrier, 127)

    def pair_copy(n, src, dst):
        return pltpu.make_async_remote_copy(
            src_ref=src, dst_ref=dst, send_sem=pair_send.at[n], recv_sem=pair_recv.at[n],
            device_id=(pt,), device_id_type=MESH,
        )

    last = 4
    order = [16, -16, 4, -4, 1, -1, "z", "y", 8, -8, 2, -2, 32, -32]

    def step(r, _):
        @pl.when(r < HEADS)
        def _():
            for a in range(2):
                load(r, a).wait()
            for k in own:
                send(k, r)

        for d in order:
            h = r - lag(d)

            @pl.when((h >= 0) & (h < HEADS) & comes(d, h))
            def _(d=d, h=h):
                arrived(slot_of(d), h)
                for k in on[d]:
                    send(k, h)

        @pl.when(r == 0)
        def _():
            for s, goes, _, to, _ in direct:
                guarded(goes, low_copy(s, to).start)
            pair_copy(0, x_ref, x2).start()

        @pl.when(r == last)
        def _():
            for s, _, comes_in, _, _ in direct:
                guarded(comes_in, low_copy(s, pt).wait_recv)

        h = r - last

        @pl.when((h >= 0) & (h < HEADS))
        def _():
            arrived(PARTNER, h)

            @pl.when(((c == 0) & valid(1)) | ((c == 1) & valid(-1)))
            def _():
                arrived(SIDE, h)

            head(h)

        return 0

    lax.fori_loop(0, HEADS + last, step, 0)

    for s, _, goes, _, to in direct:
        rsend[s] = acc[:, s * TOK:(s + 1) * TOK].astype(jnp.bfloat16)
        guarded(goes, back_copy(s, to).start)
    pair_copy(1, upart, upart2).start()
    backs[0:RANK, :] = back0[...].astype(jnp.bfloat16)
    pair_copy(2, backs.at[0:RANK], backs2.at[0:RANK]).start()
    pair_copy(0, x_ref, x2).wait_recv()
    pair_copy(1, upart, upart2).wait_recv()
    pair_copy(2, backs.at[0:RANK], backs2.at[0:RANK]).wait_recv()

    def both_up(p, lo, hi):
        r = slice(p * RANK, (p + 1) * RANK)
        return (upart[r, lo:hi].astype(jnp.float32) + upart2[r, lo:hi].astype(jnp.float32)).astype(jnp.bfloat16)

    def both_down(p, start):
        for t in range(0, WIDTH, 512):
            part = nn(backs[p * RANK:(p + 1) * RANK, :], x_ref[:, t:t + 512])
            part = part + nn(backs2[p * RANK:(p + 1) * RANK, :], x2[:, t:t + 512])
            terms[:, start + t:start + t + 512] = (part * NORM).astype(jnp.bfloat16)

    @pl.when(c == 0)
    def _():
        both_down(0, 0)
        terms[:, 3072:3840] = both_up(0, 0, 768)

    @pl.when(c == 1)
    def _():
        terms[:, 0:768] = both_up(0, 768, 1536)
        terms[:, 768:2304] = both_up(1, 0, 1536)
        terms[:, 2304:3840] = both_up(2, 0, 1536)

    def early_piece(o):
        return (o % 16) != 15, o - o // 16

    def late_piece(o):
        oz, ox, oy = o // 16, (o // 4) % 4, o % 4
        t = (oy - ox - oz + 8) % 4
        return t < 3, (oz * 4 + ox) * 3 + t

    def place(ref, start, piece):
        return ref.at[
            pl.ds(pl.multiple_of((piece % 4) * 16, 16), 16),
            pl.ds(pl.multiple_of(start + (piece // 4) * 256, 256), 256),
        ]

    def reduce_start(j, of, start, landing):
        def one(n, _):
            o = (i + n) % CHIPS
            owns, piece = of(o)

            @pl.when(owns)
            def _():
                pltpu.make_async_remote_copy(
                    src_ref=place(terms, start, piece), dst_ref=landing.at[63 - n],
                    send_sem=red_send.at[j], recv_sem=red_recv.at[j],
                    device_id=(2 * o + c,), device_id_type=MESH,
                ).start()

            return 0

        lax.fori_loop(1, CHIPS, one, 0)

    def reduce_finish(j, of, start, landing, sums):
        owns, piece = of(i)

        @pl.when(owns)
        def _():
            pltpu.make_async_copy(landing, landing, red_recv.at[j]).wait()
            mine = place(terms, start, piece)[...].astype(jnp.float32)

            def add(n, total):
                return total + landing[n].astype(jnp.float32)

            sums[...] = lax.fori_loop(0, CHIPS - 1, add, mine).astype(jnp.bfloat16)
            pltpu.make_async_copy(sums, place(result, start, piece), gat_recv.at[j]).start()

            def one(n, _):
                o = (i + n) % CHIPS
                pltpu.make_async_remote_copy(
                    src_ref=sums, dst_ref=place(result, start, piece),
                    send_sem=gat_send.at[j], recv_sem=gat_recv.at[j],
                    device_id=(2 * o + c,), device_id_type=MESH,
                ).start()
                return 0

            lax.fori_loop(1, CHIPS, one, 0)

    def gathered(j, start, width):
        part = result.at[:, start:start + width]
        pltpu.make_async_copy(part, part, gat_recv.at[j]).wait()
        pair_copy(4 + j, part, result2.at[:, start:start + width]).start()

    def sent(j, of, landing, pieces):
        owns, _ = of(i)

        @pl.when(owns)
        def _():
            part = landing.at[0:pieces - 1]
            pltpu.make_async_copy(part, part, red_send.at[j]).wait()
            pltpu.make_async_copy(landing, landing, gat_send.at[j]).wait()

        @pl.when(jnp.logical_not(owns))
        def _():
            part = landing.at[0:pieces]
            pltpu.make_async_copy(part, part, red_send.at[j]).wait()

    reduce_start(0, early_piece, 0, early_in)

    total = acc[:, 0:TOK]
    for s, comes_in, _, _, _ in direct:
        guarded(comes_in, back_copy(s, pt).wait_recv)
        total = total + rrecv[s].astype(jnp.float32)
    backs[RANK:, :] = total.astype(jnp.bfloat16)
    pair_copy(3, backs.at[RANK:3 * RANK], backs2.at[RANK:3 * RANK]).start()
    pair_copy(3, backs.at[RANK:3 * RANK], backs2.at[RANK:3 * RANK]).wait_recv()

    @pl.when(c == 0)
    def _():
        both_down(1, EARLY)

    @pl.when(c == 1)
    def _():
        both_down(2, EARLY)

    reduce_start(1, late_piece, EARLY, late_in)
    reduce_finish(0, early_piece, 0, early_in, early_sum)
    back = backs[...].T
    for t in range(0, WIDTH, 512):
        grad_out[:, t:t + 512] = nn(back, down_ref[:, t:t + 512]).astype(jnp.bfloat16)
    reduce_finish(1, late_piece, EARLY, late_in, late_sum)
    gathered(0, 0, EARLY)
    gathered(1, EARLY, LATE)
    for j, (start, width) in enumerate([(0, EARLY), (EARLY, LATE)]):
        pair_copy(4 + j, result.at[:, start:start + width], result2.at[:, start:start + width]).wait_recv()

    def finish(a, b):
        down_out[0:RANK, :] = a[:, 0:3072]
        down_out[RANK:2 * RANK, :] = a[:, 3840:6912]
        down_out[2 * RANK:, :] = b[:, 3840:6912]
        up_out[0:RANK, 0:768] = a[:, 3072:3840]
        up_out[0:RANK, 768:1536] = b[:, 0:768]
        up_out[RANK:2 * RANK, :] = b[:, 768:2304]
        up_out[2 * RANK:, :] = b[:, 2304:3840]

    @pl.when(c == 0)
    def _():
        finish(result, result2)

    @pl.when(c == 1)
    def _():
        finish(result2, result)

    sent(0, early_piece, early_in, 60)
    sent(1, late_piece, late_in, 48)
    pair_copy(0, x_ref, x2).wait_send()
    pair_copy(1, upart, upart2).wait_send()
    pair_copy(2, backs.at[0:RANK], backs2.at[0:RANK]).wait_send()
    pair_copy(3, backs.at[RANK:3 * RANK], backs2.at[RANK:3 * RANK]).wait_send()
    for j, (start, width) in enumerate([(0, EARLY), (EARLY, LATE)]):
        pair_copy(4 + j, result.at[:, start:start + width], result2.at[:, start:start + width]).wait_send()
    for s, goes, returns, to, owner in direct:
        guarded(goes, low_copy(s, to).wait_send)
        guarded(returns, back_copy(s, owner).wait_send)

    def drain(h, _):
        for k, (cond, src, dst, device) in enumerate(kinds):
            guarded(
                None if cond is None else cond(h),
                lambda: copy(k, h, src, dst, device).wait_send(),
            )
        return 0

    lax.fori_loop(0, HEADS, drain, 0)


def attention(mask, inputs, queries, output_gradient, keys, values, down_t, up):
    vm = pl.BlockSpec(memory_space=pltpu.VMEM)
    dma = pltpu.SemaphoreType.DMA
    return pl.pallas_call(
        attention_kernel,
        out_shape=(
            jax.ShapeDtypeStruct((TOK, WIDTH), jnp.bfloat16),
            jax.ShapeDtypeStruct((3 * RANK, WIDTH), jnp.bfloat16),
            jax.ShapeDtypeStruct((3 * RANK, FEAT), jnp.bfloat16),
        ),
        in_specs=[pl.BlockSpec(memory_space=pltpu.SMEM), vm, vm, vm,
                  pl.BlockSpec(memory_space=pl.ANY), pl.BlockSpec(memory_space=pl.ANY), vm, vm],
        out_specs=(vm, vm, vm),
        scratch_shapes=[
            pltpu.VMEM((HEADS, 2, (SLOTS + 2) * TOK, DH), jnp.bfloat16),
            pltpu.VMEM((KEYS, DH), jnp.bfloat16),
            pltpu.VMEM((8, PAD), jnp.float32),
            pltpu.VMEM((TOK, PAD), jnp.float32),
            pltpu.VMEM((TOK, PAD), jnp.float32),
            pltpu.VMEM((2 * RANK, PAD), jnp.float32),
            pltpu.VMEM((RANK, TOK), jnp.float32),
            pltpu.VMEM((RANK, TOK), jnp.bfloat16),
            pltpu.VMEM((SLOTS, 2 * RANK, TOK), jnp.bfloat16),
            pltpu.VMEM((SLOTS, 2 * RANK, TOK), jnp.bfloat16),
            pltpu.VMEM((TOK, WIDTH), jnp.bfloat16),
            pltpu.VMEM((3 * RANK, FEAT), jnp.bfloat16),
            pltpu.VMEM((3 * RANK, FEAT), jnp.bfloat16),
            pltpu.VMEM((3 * RANK, TOK), jnp.bfloat16),
            pltpu.VMEM((3 * RANK, TOK), jnp.bfloat16),
            pltpu.VMEM((RANK, EARLY + LATE), jnp.bfloat16),
            pltpu.VMEM((RANK, EARLY + LATE), jnp.bfloat16),
            pltpu.VMEM((RANK, EARLY + LATE), jnp.bfloat16),
            pltpu.VMEM((CHIPS - 1, *PIECE), jnp.bfloat16),
            pltpu.VMEM((CHIPS - 1, *PIECE), jnp.bfloat16),
            pltpu.VMEM(PIECE, jnp.bfloat16),
            pltpu.VMEM(PIECE, jnp.bfloat16),
            dma((HEADS, 2)),
            dma((39, HEADS)),
            dma((SLOTS + 2, HEADS)),
            dma((SLOTS,)), dma((SLOTS,)), dma((SLOTS,)), dma((SLOTS,)),
            dma((6,)), dma((6,)), dma((2,)), dma((2,)), dma((2,)), dma((2,)),
        ],
        compiler_params=pltpu.CompilerParams(
            collective_id=0, has_side_effects=True, vmem_limit_bytes=56 * 2**20
        ),
        cost_estimate=pl.CostEstimate(flops=12 * 10**9, bytes_accessed=8 * 10**6, transcendentals=7 * 10**6),
        name="attention_gradients",
    )(mask, inputs, queries, output_gradient, keys, values, down_t, up)


def per_device(
    inputs, queries, keys, values, output_gradient, radial_block_mask,
    adapter_down_weight, adapter_up_weight,
):
    down_t = jnp.swapaxes(adapter_down_weight, 1, 2).reshape(3 * RANK, WIDTH)
    input_gradient, down, up = attention(
        radial_block_mask, inputs, queries, output_gradient, keys, values, down_t, adapter_up_weight
    )
    down = jnp.swapaxes(down.reshape(3, RANK, WIDTH), 1, 2).astype(jnp.float32)
    up = up.reshape(3, RANK, FEAT).astype(jnp.float32)
    return (input_gradient, down, up)


def solution(mesh):
    return jax.shard_map(
        per_device,
        mesh=mesh,
        in_specs=(P("frame", None),) * 5 + (P(), P(), P()),
        out_specs=(P("frame", None), P(), P()),
        check_vma=False,
    )
```

```python
import functools
import math

import jax
import jax.numpy as jnp
from jax import lax
from jax.experimental import pallas as pl
from jax.experimental.pallas import tpu as pltpu
from jax.sharding import PartitionSpec as P

MESH = pl.DeviceIdType.MESH
DH = 128
HEADS = 12
TOK = 192
RANK = 64
WIDTH = 3072
FEAT = HEADS * DH
OWN, PARTNER, SIDE = 0, 1, 2
SLOT = {1: 3, -1: 4, 2: 5, -2: 6, 4: 7, -4: 8, 8: 9, -8: 10, 16: 11, -16: 12, 32: 13, -32: 14}
SLOTS = 15
VIA_Y, VIA_Z = 15, 16
KEYS = SLOTS * TOK
PAD = 3072
TILES = [(0, 512), (512, 512), (1024, 512), (1536, 512), (2048, 512), (2560, 320)]
ROOT = 1.0 / math.sqrt(DH)
MASKED = -1e30
LEAD = 1
CHIPS = 64
NORM = 1.0 / math.sqrt(128 * TOK)
EARLY = 3840
THIRD = EARLY // 3
LATE = 3072
PIECE = (16, 256)


def nt(a, b):
    return lax.dot_general(a, b, (((1,), (1,)), ((), ())), preferred_element_type=jnp.float32)


def nn(a, b):
    return lax.dot_general(a, b, (((1,), (0,)), ((), ())), preferred_element_type=jnp.float32)


def pick(cond, a, b):
    return jnp.where(cond, a, b)


def hops(d, z, x, y):
    if abs(d) == 16:
        return 1
    if d == 4:
        return pick(x == 0, 2, 1)
    if d == -4:
        return pick(x == 3, 2, 1)
    if d == 1:
        return pick(y == 0, pick(x == 0, 3, 2), 1)
    if d == -1:
        return pick(y == 3, pick(x == 3, 3, 2), 1)
    if d == 8:
        return pick(x >= 2, 2, 3)
    if d == -8:
        return pick(x <= 1, 2, 3)
    if abs(d) == 32:
        return 2
    if d == 2:
        return pick(y >= 2, 2, pick(x == 0, 4, 3))
    return pick(y <= 1, 2, pick(x == 3, 4, 3))


def attention_kernel(
    mask_ref, x_hbm, q_hbm, g_hbm, k_ref, v_ref, down_hbm, up_hbm,
    grad_out, down_out, up_out,
    x_ref, q_ref, g_ref, down_ref, up_ref,
    buf, lowbuf, bias, s_ref, d_ref, acc, back0, lowt0, rsend, rrecv,
    x2, upart, upart2, backs, backs2, terms, result, result2, late_in, late_sum, ring1, ring2, ring3, part1, part2, part3,
    in_sem, load_sem, send_sem, recv_sem, lsend, lrecv, rs_send, rs_recv,
    pair_send, pair_recv, red_send, red_recv, gat_send, gat_recv, ring_send, ring_recv,
):
    me = lax.axis_index("frame")
    i = me // 2
    c = me % 2
    z = i // 16
    x = (i // 4) % 4
    y = i % 4

    def dev(zz, xx, yy, cc):
        return ((zz + 4) % 4) * 32 + ((xx + 4) % 4) * 8 + ((yy + 4) % 4) * 2 + cc

    yp, ym = dev(z, x, y + 1, c), dev(z, x, y - 1, c)
    xp, xm = dev(z, x + 1, y, c), dev(z, x - 1, y, c)
    zp, zm = dev(z + 1, x, y, c), dev(z - 1, x, y, c)
    pt = dev(z, x, y, 1 - c)
    side = pick(c == 0, me - 1, me + 1)
    side_ok = (side >= 0) & (side < 128)

    def valid(d):
        return (i - d >= 0) & (i - d < 64)

    def rows(s):
        return pl.ds(s * TOK, TOK)

    def load(h, a):
        ref = (k_ref, v_ref)[a]
        return pltpu.make_async_copy(
            ref.at[:, pl.ds(h * DH, DH)], buf.at[h, a, rows(OWN)], load_sem.at[h, a]
        )

    for h in range(HEADS):
        for a in range(2):
            load(h, a).start()

    def arrays():
        pairs = [(x_hbm, x_ref), (down_hbm, down_ref), (q_hbm, q_ref), (g_hbm, g_ref), (up_hbm, up_ref)]
        return [pltpu.make_async_copy(src, dst, in_sem.at[n]) for n, (src, dst) in enumerate(pairs)]

    for one in arrays():
        one.start()

    barrier = pltpu.get_barrier_semaphore()

    def greet(n, _):
        pl.semaphore_signal(barrier, inc=1, device_id=((me + n) % 128,), device_id_type=MESH)
        return 0

    lax.fori_loop(1, 128, greet, 0)

    def low_copy(s, device):
        return pltpu.make_async_remote_copy(
            src_ref=lowbuf.at[rows(OWN)], dst_ref=lowbuf.at[rows(s)],
            send_sem=lsend.at[s], recv_sem=lrecv.at[s],
            device_id=(device,), device_id_type=MESH,
        )

    def back_copy(s, device):
        return pltpu.make_async_remote_copy(
            src_ref=rsend.at[s], dst_ref=rrecv.at[s],
            send_sem=rs_send.at[s], recv_sem=rs_recv.at[s],
            device_id=(device,), device_id_type=MESH,
        )

    direct = [(PARTNER, None, None, pt, pt), (SIDE, side_ok, side_ok, side, side)]
    direct += [(SLOT[d], valid(-d), valid(d), me + 2 * d, me - 2 * d) for d in SLOT]

    def guarded(cond, f):
        if cond is None:
            f()
        else:
            pl.when(cond)(f)

    def copy(kind, h, src, dst, device):
        return pltpu.make_async_remote_copy(
            src_ref=buf.at[h, :, rows(src)], dst_ref=buf.at[h, :, rows(dst)],
            send_sem=send_sem.at[kind, h], recv_sem=recv_sem.at[dst, h],
            device_id=(device,), device_id_type=MESH,
        )

    kinds = []

    def kind(cond, src, dst, device):
        kinds.append((cond, src, dst, device))
        return len(kinds) - 1

    mid = (x == 1) | (x == 2)

    def by_ring_up(xx, h):
        return (xx == 0) | (((xx == 1) | (xx == 2)) & (h % 2 == 0))

    def by_ring_down(xx, h):
        return (xx == 3) | (((xx == 1) | (xx == 2)) & (h % 2 == 1))

    def late(h):
        return (h // 2) % 2 == 0

    def up_here(h):
        return by_ring_up(x, h)

    def down_here(h):
        return by_ring_down(x, h)

    def always(cond):
        return lambda h: cond

    own = [
        kind(None, OWN, PARTNER, pt),
        kind(always(y < 3), OWN, SLOT[1], yp), kind(always(y > 0), OWN, SLOT[-1], ym),
        kind(always(x < 3), OWN, SLOT[4], xp), kind(always(x > 0), OWN, SLOT[-4], xm),
        kind(always(z < 3), OWN, SLOT[16], zp), kind(always(z > 0), OWN, SLOT[-16], zm),
        kind(always((z == 0) & (x == 0)), OWN, VIA_Z, zm),
        kind(always((z == 3) & (x == 3)), OWN, VIA_Z, zp),
    ]
    on = {}
    on[16] = [
        kind(always((z == 1) & (x != 0)), SLOT[16], SLOT[32], zp),
        kind(always(z == 3), SLOT[16], SLOT[-32], zp),
        kind(always((x == 3) & (z > 0)), SLOT[16], SLOT[4], xp),
    ]
    on[-16] = [
        kind(always((z == 2) & (x != 3)), SLOT[-16], SLOT[-32], zm),
        kind(always(z == 0), SLOT[-16], SLOT[32], zm),
        kind(always((x == 0) & (z < 3)), SLOT[-16], SLOT[-4], xm),
    ]
    on["z"] = [
        kind(always((z == 3) & (x == 0)), VIA_Z, SLOT[32], zm),
        kind(always((z == 0) & (x == 3)), VIA_Z, SLOT[-32], zp),
    ]
    on[4] = [
        kind(always((x < 2) & valid(4)), SLOT[4], SLOT[8], xp),
        kind(always(x == 3), SLOT[4], SLOT[-8], xp),
        kind(always((y == 3) & valid(4)), SLOT[4], SLOT[1], yp),
        kind(lambda h: (y == 2) & valid(4) & up_here(h), SLOT[4], VIA_Y, yp),
    ]
    on[-4] = [
        kind(always((x > 1) & valid(-4)), SLOT[-4], SLOT[-8], xm),
        kind(always(x == 0), SLOT[-4], SLOT[8], xm),
        kind(always((y == 0) & valid(-4)), SLOT[-4], SLOT[-1], ym),
        kind(lambda h: (y == 1) & valid(-4) & down_here(h), SLOT[-4], VIA_Y, ym),
    ]
    on[1] = [
        kind(lambda h: valid(1) & ((y < 2) | ((y == 2) & jnp.logical_not(up_here(h)))), SLOT[1], SLOT[2], yp),
        kind(lambda h: (y == 3) & jnp.logical_not(up_here(h)), SLOT[1], SLOT[-2], yp),
        kind(always((c == 1) & valid(1)), SLOT[1], SIDE, pt),
        kind(
            lambda h: (y == 3) & (x < 3) & jnp.logical_not(by_ring_up(x + 1, h)) & jnp.logical_not(late(h)),
            SLOT[1], VIA_Y, xp,
        ),
    ]
    on[-1] = [
        kind(lambda h: valid(-1) & ((y > 1) | ((y == 1) & up_here(h))), SLOT[-1], SLOT[-2], ym),
        kind(lambda h: (y == 0) & up_here(h), SLOT[-1], SLOT[2], ym),
        kind(always((c == 0) & valid(-1)), SLOT[-1], SIDE, pt),
        kind(
            lambda h: (y == 0) & (x > 0) & jnp.logical_not(by_ring_down(x - 1, h)) & jnp.logical_not(late(h)),
            SLOT[-1], VIA_Y, xm,
        ),
    ]

    def has_via_y(h):
        up = (y == 3) & ((z > 0) | (x > 0)) & (up_here(h) | jnp.logical_not(late(h)))
        down = (y == 0) & ((z < 3) | (x < 3)) & (down_here(h) | jnp.logical_not(late(h)))
        return up | down

    via_z = ((z == 3) & (x == 0)) | ((z == 0) & (x == 3))
    on["y"] = [
        kind(lambda h: (y == 3) & has_via_y(h), VIA_Y, SLOT[2], yp),
        kind(lambda h: (y == 0) & has_via_y(h), VIA_Y, SLOT[-2], ym),
    ]
    on[2] = [
        kind(lambda h: (y == 3) & (x > 0) & jnp.logical_not(by_ring_down(x - 1, h)) & late(h), SLOT[2], SLOT[-2], xm),
    ]
    on[-2] = [
        kind(lambda h: (y == 0) & (x < 3) & jnp.logical_not(by_ring_up(x + 1, h)) & late(h), SLOT[-2], SLOT[2], xp),
    ]
    on[8] = [kind(always((x == 3) & (z > 0)), SLOT[8], SLOT[-8], zm)]
    on[-8] = [kind(always((x == 0) & (z < 3)), SLOT[-8], SLOT[8], zp)]
    on[32] = []
    on[-32] = []

    def slot_of(d):
        return VIA_Y if d == "y" else VIA_Z if d == "z" else SLOT[d]

    def comes(d, h):
        return has_via_y(h) if d == "y" else via_z if d == "z" else valid(d)

    def lag(d):
        if d == "z":
            return 1
        if d == "y":
            return pick(((y == 3) & (x == 0)) | ((y == 0) & (x == 3)), 3, 2)
        return hops(d, z, x, y)

    def send(k, h):
        cond, src, dst, device = kinds[k]
        guarded(None if cond is None else cond(h), lambda: copy(k, h, src, dst, device).start())

    def arrived(s, h):
        copy(0, h, s, s, pt).wait_recv()

    def head(h):
        cols = pl.ds(pl.multiple_of(h * DH, DH), DH)
        q = q_ref[:, cols]
        g = g_ref[:, cols]
        top = None
        for t0, w in TILES:
            kt = buf[h, 0, pl.ds(t0, w), :]
            s = nt(q, kt) * (ROOT * math.log2(math.e)) + bias[0:1, t0:t0 + w]
            s_ref[:, t0:t0 + w] = s
            m = jnp.max(s, axis=1, keepdims=True)
            top = m if top is None else jnp.maximum(top, m)
        total = jnp.zeros((TOK, 1), jnp.float32)
        dot = jnp.zeros((TOK, 1), jnp.float32)
        for t0, w in TILES:
            e = jnp.exp2(s_ref[:, t0:t0 + w] - top)
            s_ref[:, t0:t0 + w] = e
            dp = nt(g, buf[h, 1, pl.ds(t0, w), :])
            d_ref[:, t0:t0 + w] = dp
            total = total + jnp.sum(e, axis=1, keepdims=True)
            dot = dot + jnp.sum(e * dp, axis=1, keepdims=True)
        inv = 1.0 / total
        dot = dot * inv
        qu = (nt(up_ref[1, :, cols], q) * ROOT).astype(jnp.bfloat16)
        gu = nt(up_ref[2, :, cols], g).astype(jnp.bfloat16)
        both = jnp.zeros((TOK, 2 * DH), jnp.float32)
        vlow = jnp.zeros((TOK, DH), jnp.float32)
        for t0, w in TILES:
            p = s_ref[:, t0:t0 + w] * inv
            pb = p.astype(jnp.bfloat16)
            ds = (p * (d_ref[:, t0:t0 + w] - dot)).astype(jnp.bfloat16)
            kt = buf[h, 0, pl.ds(t0, w), :]
            lt = lowbuf[pl.ds(t0, w), :]
            both = both + nn(ds, jnp.concatenate([kt, lt], axis=1))
            vlow = vlow + nn(pb, lt)
            acc[0:RANK, t0:t0 + w] += nn(qu, ds)
            acc[RANK:, t0:t0 + w] += nn(gu, pb)
        out0 = (both[:, 0:DH] * ROOT).astype(jnp.bfloat16)
        klow = both[:, DH:DH + RANK] * ROOT
        upart[0:RANK, cols] = (nn(lowt0[...], out0) * NORM).astype(jnp.bfloat16)
        back0[...] += nt(up_ref[0, :, cols], out0)
        lows = jnp.concatenate([klow, vlow[:, RANK:]], axis=1).T.astype(jnp.bfloat16)
        upart[RANK:2 * RANK, cols] = (nn(lows[0:RANK], q) * NORM).astype(jnp.bfloat16)
        upart[2 * RANK:, cols] = (nn(lows[RANK:], g) * NORM).astype(jnp.bfloat16)

    pl.semaphore_wait(barrier, 127)

    def send_own(h):
        for a in range(2):
            load(h, a).wait()
        for k in own:
            send(k, h)

    lax.fori_loop(0, LEAD, lambda h, _: (send_own(h), 0)[1], 0)
    for one in arrays():
        one.wait()

    every = [(d, SLOT[d]) for d in SLOT]
    for d, s in every:
        @pl.when(jnp.logical_not(valid(d)))
        def _(s=s):
            lowbuf[rows(s), :] = jnp.zeros((TOK, DH), jnp.bfloat16)
            rrecv[s] = jnp.zeros((2 * RANK, TOK), jnp.bfloat16)

            def zero(h, _):
                for a in range(2):
                    buf[h, a, rows(s), :] = jnp.zeros((TOK, DH), jnp.bfloat16)
                return 0

            lax.fori_loop(0, HEADS, zero, 0)

    @pl.when(jnp.logical_not(side_ok))
    def _():
        lowbuf[rows(SIDE), :] = jnp.zeros((TOK, DH), jnp.bfloat16)
        rrecv[SIDE] = jnp.zeros((2 * RANK, TOK), jnp.bfloat16)

        def zero(h, _):
            for a in range(2):
                buf[h, a, rows(SIDE), :] = jnp.zeros((TOK, DH), jnp.bfloat16)
            return 0

        lax.fori_loop(0, HEADS, zero, 0)

    lane = lax.broadcasted_iota(jnp.int32, (8, PAD), 1)
    total_bias = jnp.zeros((8, PAD), jnp.float32)
    for s, (block, ok) in enumerate(
        [(me, None), (pt, None), (side, side_ok)] + [(me - 2 * d, valid(d)) for d in SLOT]
    ):
        kept = mask_ref[me, jnp.clip(block, 0, 127)]
        value = jnp.where(kept > 0, 0.0, MASKED)
        if ok is not None:
            value = jnp.where(ok, value, MASKED)
        inside = (lane >= s * TOK) & (lane < (s + 1) * TOK)
        total_bias = jnp.where(inside, value, total_bias)
    bias[...] = total_bias

    low = nt(x_ref[...], down_ref[...]).astype(jnp.bfloat16)
    lowt0[...] = nt(down_ref[0:RANK, :], x_ref[...]).astype(jnp.bfloat16)
    lowbuf[rows(OWN), :] = low[:, RANK:]
    acc[...] = jnp.zeros_like(acc)
    back0[...] = jnp.zeros_like(back0)

    def pair_copy(n, src, dst):
        return pltpu.make_async_remote_copy(
            src_ref=src, dst_ref=dst, send_sem=pair_send.at[n], recv_sem=pair_recv.at[n],
            device_id=(pt,), device_id_type=MESH,
        )

    last = 4
    order = [16, -16, 4, -4, 1, -1, "z", "y", 8, -8, 2, -2, 32, -32]

    def step(r, _):
        @pl.when(r + LEAD < HEADS)
        def _():
            send_own(r + LEAD)

        for d in order:
            h = r - lag(d)

            @pl.when((h >= 0) & (h < HEADS) & comes(d, h))
            def _(d=d, h=h):
                arrived(slot_of(d), h)
                for k in on[d]:
                    send(k, h)

        @pl.when(r == 0)
        def _():
            for s, goes, _, to, _ in direct:
                guarded(goes, low_copy(s, to).start)
            pair_copy(0, x_ref, x2).start()

        @pl.when(r == last)
        def _():
            for s, _, comes_in, _, _ in direct:
                guarded(comes_in, low_copy(s, pt).wait_recv)

        h = r - last

        @pl.when((h >= 0) & (h < HEADS))
        def _():
            arrived(PARTNER, h)

            @pl.when(((c == 0) & valid(1)) | ((c == 1) & valid(-1)))
            def _():
                arrived(SIDE, h)

            head(h)

        return 0

    lax.fori_loop(0, HEADS + last, step, 0)

    for s, _, goes, _, to in direct:
        rsend[s] = acc[:, s * TOK:(s + 1) * TOK].astype(jnp.bfloat16)
        guarded(goes, back_copy(s, to).start)
    pair_copy(1, upart, upart2).start()
    backs[0:RANK, :] = back0[...].astype(jnp.bfloat16)
    pair_copy(2, backs.at[0:RANK], backs2.at[0:RANK]).start()
    pair_copy(0, x_ref, x2).wait_recv()
    pair_copy(1, upart, upart2).wait_recv()
    pair_copy(2, backs.at[0:RANK], backs2.at[0:RANK]).wait_recv()

    def both_up(p, lo, hi):
        r = slice(p * RANK, (p + 1) * RANK)
        return (upart[r, lo:hi].astype(jnp.float32) + upart2[r, lo:hi].astype(jnp.float32)).astype(jnp.bfloat16)

    def both_down(p, start):
        for t in range(0, WIDTH, 512):
            part = nn(backs[p * RANK:(p + 1) * RANK, :], x_ref[:, t:t + 512])
            part = part + nn(backs2[p * RANK:(p + 1) * RANK, :], x2[:, t:t + 512])
            terms[:, start + t:start + t + 512] = (part * NORM).astype(jnp.bfloat16)

    @pl.when(c == 0)
    def _():
        both_down(0, 0)
        terms[:, 3072:3840] = both_up(0, 0, 768)

    @pl.when(c == 1)
    def _():
        terms[:, 0:768] = both_up(0, 768, 1536)
        terms[:, 768:2304] = both_up(1, 0, 1536)
        terms[:, 2304:3840] = both_up(2, 0, 1536)

    here = (x, y, z)

    def peer(axis, at):
        return dev(*(z, at, y, c) if axis == 0 else (z, x, at, c) if axis == 1 else (at, x, y, c))

    def third(ref, k):
        return ref.at[:, k * THIRD:(k + 1) * THIRD]

    def rows16(ref, n):
        return ref.at[pl.ds(pl.multiple_of(n * 16, 16), 16), :]

    def ring_copies(stage, k):
        axis = (k + (0, 1, 2, 0)[stage]) % 3
        mine = here[axis]
        out = []
        for n in (1, 2, 3):
            to, source = (mine + n) % 4, (mine - n + 4) % 4
            if stage == 0:
                src, dst, got = rows16(third(terms, k), to), ring1.at[k, mine], ring1.at[k, source]
            elif stage == 3:
                src = part3.at[k]
                dst, got = rows16(third(result, k), mine), rows16(third(result, k), source)
            else:
                ring, part = ((ring2, part1), (ring3, part2))[stage - 1]
                src, dst, got = part.at[k], ring.at[k, mine], ring.at[k, source]
            slot = (stage * 3 + k) * 3 + n - 1
            out.append(tuple(
                pltpu.make_async_remote_copy(
                    src_ref=src, dst_ref=where, send_sem=ring_send.at[slot], recv_sem=ring_recv.at[slot],
                    device_id=(peer(axis, to),), device_id_type=MESH,
                )
                for where in (dst, got)
            ))
        return out

    def ring_start(stage):
        for k in range(3):
            mine = here[(k + (0, 1, 2, 0)[stage]) % 3]
            if stage == 0:
                ring1[k, mine] = rows16(third(terms, k), mine)[...]
            elif stage == 1:
                ring2[k, mine] = part1[k]
            elif stage == 2:
                ring3[k, mine] = part2[k]
            else:
                rows16(third(result, k), mine)[...] = part3[k]
            for out, _ in ring_copies(stage, k):
                out.start()

    def ring_finish(stage):
        for k in range(3):
            for _, got in ring_copies(stage, k):
                got.wait_recv()
            if stage < 3:
                ring, part = ((ring1, part1), (ring2, part2), (ring3, part3))[stage]
                total = ring[k, 0].astype(jnp.float32)
                for n in range(1, 4):
                    total = total + ring[k, n].astype(jnp.float32)
                part[k] = total.astype(jnp.bfloat16)

    def late_piece(o):
        oz, ox, oy = o // 16, (o // 4) % 4, o % 4
        t = (oy - ox - oz + 8) % 4
        return t < 3, (oz * 4 + ox) * 3 + t

    def place(ref, start, piece):
        return ref.at[
            pl.ds(pl.multiple_of((piece % 4) * 16, 16), 16),
            pl.ds(pl.multiple_of(start + (piece // 4) * 256, 256), 256),
        ]

    def reduce_start(j, of, start, landing):
        def one(n, _):
            o = (i + n) % CHIPS
            owns, piece = of(o)

            @pl.when(owns)
            def _():
                pltpu.make_async_remote_copy(
                    src_ref=place(terms, start, piece), dst_ref=landing.at[63 - n],
                    send_sem=red_send.at[j], recv_sem=red_recv.at[j],
                    device_id=(2 * o + c,), device_id_type=MESH,
                ).start()

            return 0

        lax.fori_loop(1, CHIPS, one, 0)

    def reduce_finish(j, of, start, landing, sums):
        owns, piece = of(i)

        @pl.when(owns)
        def _():
            pltpu.make_async_copy(landing, landing, red_recv.at[j]).wait()
            mine = place(terms, start, piece)[...].astype(jnp.float32)

            def add(n, total):
                return total + landing[n].astype(jnp.float32)

            sums[...] = lax.fori_loop(0, CHIPS - 1, add, mine).astype(jnp.bfloat16)
            pltpu.make_async_copy(sums, place(result, start, piece), gat_recv.at[j]).start()

            def one(n, _):
                o = (i + n) % CHIPS
                pltpu.make_async_remote_copy(
                    src_ref=sums, dst_ref=place(result, start, piece),
                    send_sem=gat_send.at[j], recv_sem=gat_recv.at[j],
                    device_id=(2 * o + c,), device_id_type=MESH,
                ).start()
                return 0

            lax.fori_loop(1, CHIPS, one, 0)

    def gathered(j, start, width):
        part = result.at[:, start:start + width]
        pltpu.make_async_copy(part, part, gat_recv.at[j]).wait()
        pair_copy(4 + j, part, result2.at[:, start:start + width]).start()

    def sent(j, of, landing, pieces):
        owns, _ = of(i)

        @pl.when(owns)
        def _():
            part = landing.at[0:pieces - 1]
            pltpu.make_async_copy(part, part, red_send.at[j]).wait()
            pltpu.make_async_copy(landing, landing, gat_send.at[j]).wait()

        @pl.when(jnp.logical_not(owns))
        def _():
            part = landing.at[0:pieces]
            pltpu.make_async_copy(part, part, red_send.at[j]).wait()

    ring_start(0)
    def drain(h, _):
        for k, (cond, src, dst, device) in enumerate(kinds):
            guarded(
                None if cond is None else cond(h),
                lambda: copy(k, h, src, dst, device).wait_send(),
            )
        return 0

    lax.fori_loop(0, HEADS, drain, 0)
    ring_finish(0)
    ring_start(1)

    total = acc[:, 0:TOK]
    for s, comes_in, _, _, _ in direct:
        guarded(comes_in, back_copy(s, pt).wait_recv)
        total = total + rrecv[s].astype(jnp.float32)
    backs[RANK:, :] = total.astype(jnp.bfloat16)
    pair_copy(3, backs.at[RANK:3 * RANK], backs2.at[RANK:3 * RANK]).start()
    pair_copy(3, backs.at[RANK:3 * RANK], backs2.at[RANK:3 * RANK]).wait_recv()

    @pl.when(c == 0)
    def _():
        both_down(1, EARLY)

    @pl.when(c == 1)
    def _():
        both_down(2, EARLY)

    reduce_start(1, late_piece, EARLY, late_in)
    ring_finish(1)
    ring_start(2)
    back = backs[...].T
    for t in range(0, WIDTH, 512):
        grad_out[:, t:t + 512] = nn(back, down_ref[:, t:t + 512]).astype(jnp.bfloat16)
    ring_finish(2)
    ring_start(3)
    reduce_finish(1, late_piece, EARLY, late_in, late_sum)
    ring_finish(3)
    pair_copy(4, result.at[:, 0:EARLY], result2.at[:, 0:EARLY]).start()
    gathered(1, EARLY, LATE)
    for j, (start, width) in enumerate([(0, EARLY), (EARLY, LATE)]):
        pair_copy(4 + j, result.at[:, start:start + width], result2.at[:, start:start + width]).wait_recv()

    def finish(a, b):
        down_out[0:RANK, :] = a[:, 0:3072]
        down_out[RANK:2 * RANK, :] = a[:, 3840:6912]
        down_out[2 * RANK:, :] = b[:, 3840:6912]
        up_out[0:RANK, 0:768] = a[:, 3072:3840]
        up_out[0:RANK, 768:1536] = b[:, 0:768]
        up_out[RANK:2 * RANK, :] = b[:, 768:2304]
        up_out[2 * RANK:, :] = b[:, 2304:3840]

    @pl.when(c == 0)
    def _():
        finish(result, result2)

    @pl.when(c == 1)
    def _():
        finish(result2, result)

    for stage in range(4):
        for k in range(3):
            for out, _ in ring_copies(stage, k):
                out.wait_send()
    sent(1, late_piece, late_in, 48)
    pair_copy(0, x_ref, x2).wait_send()
    pair_copy(1, upart, upart2).wait_send()
    pair_copy(2, backs.at[0:RANK], backs2.at[0:RANK]).wait_send()
    pair_copy(3, backs.at[RANK:3 * RANK], backs2.at[RANK:3 * RANK]).wait_send()
    for j, (start, width) in enumerate([(0, EARLY), (EARLY, LATE)]):
        pair_copy(4 + j, result.at[:, start:start + width], result2.at[:, start:start + width]).wait_send()
    for s, goes, returns, to, owner in direct:
        guarded(goes, low_copy(s, to).wait_send)
        guarded(returns, back_copy(s, owner).wait_send)


def attention(mask, inputs, queries, output_gradient, keys, values, down_t, up):
    vm = pl.BlockSpec(memory_space=pltpu.VMEM)
    dma = pltpu.SemaphoreType.DMA
    return pl.pallas_call(
        attention_kernel,
        out_shape=(
            jax.ShapeDtypeStruct((TOK, WIDTH), jnp.bfloat16),
            jax.ShapeDtypeStruct((3 * RANK, WIDTH), jnp.bfloat16),
            jax.ShapeDtypeStruct((3 * RANK, FEAT), jnp.bfloat16),
        ),
        in_specs=[pl.BlockSpec(memory_space=pltpu.SMEM)] + [pl.BlockSpec(memory_space=pl.ANY)] * 7,
        out_specs=(vm, vm, vm),
        scratch_shapes=[
            pltpu.VMEM((TOK, WIDTH), jnp.bfloat16),
            pltpu.VMEM((TOK, FEAT), jnp.bfloat16),
            pltpu.VMEM((TOK, FEAT), jnp.bfloat16),
            pltpu.VMEM((3 * RANK, WIDTH), jnp.bfloat16),
            pltpu.VMEM((3, RANK, FEAT), jnp.bfloat16),
            pltpu.VMEM((HEADS, 2, (SLOTS + 2) * TOK, DH), jnp.bfloat16),
            pltpu.VMEM((KEYS, DH), jnp.bfloat16),
            pltpu.VMEM((8, PAD), jnp.float32),
            pltpu.VMEM((TOK, PAD), jnp.float32),
            pltpu.VMEM((TOK, PAD), jnp.float32),
            pltpu.VMEM((2 * RANK, PAD), jnp.float32),
            pltpu.VMEM((RANK, TOK), jnp.float32),
            pltpu.VMEM((RANK, TOK), jnp.bfloat16),
            pltpu.VMEM((SLOTS, 2 * RANK, TOK), jnp.bfloat16),
            pltpu.VMEM((SLOTS, 2 * RANK, TOK), jnp.bfloat16),
            pltpu.VMEM((TOK, WIDTH), jnp.bfloat16),
            pltpu.VMEM((3 * RANK, FEAT), jnp.bfloat16),
            pltpu.VMEM((3 * RANK, FEAT), jnp.bfloat16),
            pltpu.VMEM((3 * RANK, TOK), jnp.bfloat16),
            pltpu.VMEM((3 * RANK, TOK), jnp.bfloat16),
            pltpu.VMEM((RANK, EARLY + LATE), jnp.bfloat16),
            pltpu.VMEM((RANK, EARLY + LATE), jnp.bfloat16),
            pltpu.VMEM((RANK, EARLY + LATE), jnp.bfloat16),
            pltpu.VMEM((CHIPS - 1, *PIECE), jnp.bfloat16),
            pltpu.VMEM(PIECE, jnp.bfloat16),
            pltpu.VMEM((3, 4, 16, THIRD), jnp.bfloat16),
            pltpu.VMEM((3, 4, 16, THIRD), jnp.bfloat16),
            pltpu.VMEM((3, 4, 16, THIRD), jnp.bfloat16),
            pltpu.VMEM((3, 16, THIRD), jnp.bfloat16),
            pltpu.VMEM((3, 16, THIRD), jnp.bfloat16),
            pltpu.VMEM((3, 16, THIRD), jnp.bfloat16),
            dma((5,)),
            dma((HEADS, 2)),
            dma((39, HEADS)),
            dma((SLOTS + 2, HEADS)),
            dma((SLOTS,)), dma((SLOTS,)), dma((SLOTS,)), dma((SLOTS,)),
            dma((6,)), dma((6,)), dma((2,)), dma((2,)), dma((2,)), dma((2,)), dma((36,)), dma((36,)),
        ],
        compiler_params=pltpu.CompilerParams(
            collective_id=0, has_side_effects=True, vmem_limit_bytes=56 * 2**20
        ),
        cost_estimate=pl.CostEstimate(flops=12 * 10**9, bytes_accessed=8 * 10**6, transcendentals=7 * 10**6),
        name="attention_gradients",
    )(mask, inputs, queries, output_gradient, keys, values, down_t, up)


def per_device(
    inputs, queries, keys, values, output_gradient, radial_block_mask,
    adapter_down_weight, adapter_up_weight,
):
    down_t = jnp.swapaxes(adapter_down_weight, 1, 2).reshape(3 * RANK, WIDTH)
    input_gradient, down, up = attention(
        radial_block_mask, inputs, queries, output_gradient, keys, values, down_t, adapter_up_weight
    )
    down = jnp.swapaxes(down.reshape(3, RANK, WIDTH), 1, 2).astype(jnp.float32)
    up = up.reshape(3, RANK, FEAT).astype(jnp.float32)
    return (input_gradient, down, up)


def solution(mesh):
    return jax.shard_map(
        per_device,
        mesh=mesh,
        in_specs=(P("frame", None),) * 5 + (P(), P(), P()),
        out_specs=(P("frame", None), P(), P()),
        check_vma=False,
    )
```

```python
import functools
import math

import jax
import jax.numpy as jnp
from jax import lax
from jax.experimental import pallas as pl
from jax.experimental.pallas import tpu as pltpu
from jax.sharding import PartitionSpec as P

MESH = pl.DeviceIdType.MESH
DH = 128
HEADS = 12
TOK = 192
RANK = 64
WIDTH = 3072
FEAT = HEADS * DH
OWN, PARTNER, SIDE = 0, 1, 2
SLOT = {1: 3, -1: 4, 2: 5, -2: 6, 4: 7, -4: 8, 8: 9, -8: 10, 16: 11, -16: 12, 32: 13, -32: 14}
SLOTS = 15
VIA_Y, VIA_Z = 15, 16
KEYS = SLOTS * TOK
PAD = 3072
TILES = [(0, 512), (512, 512), (1024, 512), (1536, 512), (2048, 512), (2560, 320)]
ROOT = 1.0 / math.sqrt(DH)
MASKED = -1e30
LEAD = 1
ITEMS = HEADS + 1
CHIPS = 64
NORM = 1.0 / math.sqrt(128 * TOK)
EARLY = 3840
THIRD = EARLY // 3
LATE = 3072
PIECE = (16, 256)


def nt(a, b):
    return lax.dot_general(a, b, (((1,), (1,)), ((), ())), preferred_element_type=jnp.float32)


def nn(a, b):
    return lax.dot_general(a, b, (((1,), (0,)), ((), ())), preferred_element_type=jnp.float32)


def pick(cond, a, b):
    return jnp.where(cond, a, b)


def hops(d, z, x, y):
    if abs(d) == 16:
        return 1
    if d == 4:
        return pick(x == 0, 2, 1)
    if d == -4:
        return pick(x == 3, 2, 1)
    if d == 1:
        return pick(y == 0, pick(x == 0, 3, 2), 1)
    if d == -1:
        return pick(y == 3, pick(x == 3, 3, 2), 1)
    if d == 8:
        return pick(x >= 2, 2, 3)
    if d == -8:
        return pick(x <= 1, 2, 3)
    if abs(d) == 32:
        return 2
    if d == 2:
        return pick(y >= 2, 2, pick(x == 0, 4, 3))
    return pick(y <= 1, 2, pick(x == 3, 4, 3))


def attention_kernel(
    mask_hbm, x_hbm, q_hbm, g_hbm, k_ref, v_ref, down_hbm, up_hbm,
    grad_out, down_out, up_out,
    mask_ref, x_ref, q_ref, g_ref, down_ref, up_ref,
    buf, lowbuf, bias, s_ref, d_ref, acc, back0, lowt0, rsend, rrecv,
    x2, upart, upart2, backs, backs2, terms, result, result2, late_in, late_sum, ring1, ring2, ring3, part1, part2, part3,
    in_sem, load_sem, send_sem, recv_sem, rs_send, rs_recv,
    pair_send, pair_recv, red_send, red_recv, gat_send, gat_recv, ring_send, ring_recv,
):
    me = lax.axis_index("frame")
    i = me // 2
    c = me % 2
    z = i // 16
    x = (i // 4) % 4
    y = i % 4

    def dev(zz, xx, yy, cc):
        return ((zz + 4) % 4) * 32 + ((xx + 4) % 4) * 8 + ((yy + 4) % 4) * 2 + cc

    yp, ym = dev(z, x, y + 1, c), dev(z, x, y - 1, c)
    xp, xm = dev(z, x + 1, y, c), dev(z, x - 1, y, c)
    zp, zm = dev(z + 1, x, y, c), dev(z - 1, x, y, c)
    pt = dev(z, x, y, 1 - c)
    side = pick(c == 0, me - 1, me + 1)
    side_ok = (side >= 0) & (side < 128)

    def valid(d):
        return (i - d >= 0) & (i - d < 64)

    def rows(s):
        return pl.ds(s * TOK, TOK)

    def load(h, a):
        ref = (k_ref, v_ref)[a]
        return pltpu.make_async_copy(
            ref.at[:, pl.ds(h * DH, DH)], buf.at[h, a, rows(OWN)], load_sem.at[h, a]
        )

    for h in range(HEADS):
        for a in range(2):
            load(h, a).start()

    def arrays():
        pairs = [(x_hbm, x_ref), (down_hbm, down_ref), (q_hbm, q_ref), (g_hbm, g_ref), (up_hbm, up_ref)]
        pairs += [(mask_hbm.at[pl.ds(me, 1), :], mask_ref)]
        return [pltpu.make_async_copy(src, dst, in_sem.at[n]) for n, (src, dst) in enumerate(pairs)]

    for one in arrays():
        one.start()

    barrier = pltpu.get_barrier_semaphore()

    def greet(n, _):
        pl.semaphore_signal(barrier, inc=1, device_id=((me + n) % 128,), device_id_type=MESH)
        return 0

    lax.fori_loop(1, 128, greet, 0)

    def back_copy(s, device):
        return pltpu.make_async_remote_copy(
            src_ref=rsend.at[s], dst_ref=rrecv.at[s],
            send_sem=rs_send.at[s], recv_sem=rs_recv.at[s],
            device_id=(device,), device_id_type=MESH,
        )

    direct = [(PARTNER, None, None, pt, pt), (SIDE, side_ok, side_ok, side, side)]
    direct += [(SLOT[d], valid(-d), valid(d), me + 2 * d, me - 2 * d) for d in SLOT]

    def guarded(cond, f):
        if cond is None:
            f()
        else:
            pl.when(cond)(f)

    def copy(act, kind, n, src, dst, device):
        def one(source, target):
            act(pltpu.make_async_remote_copy(
                src_ref=source, dst_ref=target,
                send_sem=send_sem.at[kind, n], recv_sem=recv_sem.at[dst, n],
                device_id=(device,), device_id_type=MESH,
            ))

        @pl.when(n == 1)
        def _():
            one(lowbuf.at[rows(src)], lowbuf.at[rows(dst)])

        @pl.when(n != 1)
        def _():
            h = jnp.maximum(n - 1, 0)
            one(buf.at[h, :, rows(src)], buf.at[h, :, rows(dst)])

    kinds = []

    def kind(cond, src, dst, device):
        kinds.append((cond, src, dst, device))
        return len(kinds) - 1

    mid = (x == 1) | (x == 2)

    def by_ring_up(xx, h):
        return (xx == 0) | (((xx == 1) | (xx == 2)) & (h % 2 == 0))

    def by_ring_down(xx, h):
        return (xx == 3) | (((xx == 1) | (xx == 2)) & (h % 2 == 1))

    def across_up(xx, h):
        return (xx == 3) | ((h // 2) % 2 == 0)

    def across_down(xx, h):
        return (xx == 0) | ((h // 2) % 2 == 0)

    def up_here(h):
        return by_ring_up(x, h)

    def down_here(h):
        return by_ring_down(x, h)

    def always(cond):
        return lambda h: cond

    own = [
        kind(None, OWN, PARTNER, pt),
        kind(always(y < 3), OWN, SLOT[1], yp), kind(always(y > 0), OWN, SLOT[-1], ym),
        kind(always(x < 3), OWN, SLOT[4], xp), kind(always(x > 0), OWN, SLOT[-4], xm),
        kind(always(z < 3), OWN, SLOT[16], zp), kind(always(z > 0), OWN, SLOT[-16], zm),
        kind(always((z == 0) & (x == 0)), OWN, VIA_Z, zm),
        kind(always((z == 3) & (x == 3)), OWN, VIA_Z, zp),
    ]
    on = {}
    on[16] = [
        kind(always((z == 1) & (x != 0)), SLOT[16], SLOT[32], zp),
        kind(always(z == 3), SLOT[16], SLOT[-32], zp),
        kind(always((x == 3) & (z > 0)), SLOT[16], SLOT[4], xp),
    ]
    on[-16] = [
        kind(always((z == 2) & (x != 3)), SLOT[-16], SLOT[-32], zm),
        kind(always(z == 0), SLOT[-16], SLOT[32], zm),
        kind(always((x == 0) & (z < 3)), SLOT[-16], SLOT[-4], xm),
    ]
    on["z"] = [
        kind(always((z == 3) & (x == 0)), VIA_Z, SLOT[32], zm),
        kind(always((z == 0) & (x == 3)), VIA_Z, SLOT[-32], zp),
    ]
    on[4] = [
        kind(always((x < 2) & valid(4)), SLOT[4], SLOT[8], xp),
        kind(always(x == 3), SLOT[4], SLOT[-8], xp),
        kind(always((y == 3) & valid(4)), SLOT[4], SLOT[1], yp),
        kind(lambda h: (y == 2) & valid(4) & up_here(h), SLOT[4], VIA_Y, yp),
    ]
    on[-4] = [
        kind(always((x > 1) & valid(-4)), SLOT[-4], SLOT[-8], xm),
        kind(always(x == 0), SLOT[-4], SLOT[8], xm),
        kind(always((y == 0) & valid(-4)), SLOT[-4], SLOT[-1], ym),
        kind(lambda h: (y == 1) & valid(-4) & down_here(h), SLOT[-4], VIA_Y, ym),
    ]
    on[1] = [
        kind(lambda h: valid(1) & ((y < 2) | ((y == 2) & jnp.logical_not(up_here(h)))), SLOT[1], SLOT[2], yp),
        kind(lambda h: (y == 3) & jnp.logical_not(up_here(h)), SLOT[1], SLOT[-2], yp),
        kind(always((c == 1) & valid(1)), SLOT[1], SIDE, pt),
        kind(
            lambda h: (y == 3) & (x < 3) & jnp.logical_not(by_ring_up(x + 1, h)) & jnp.logical_not(across_up(x + 1, h)),
            SLOT[1], VIA_Y, xp,
        ),
    ]
    on[-1] = [
        kind(lambda h: valid(-1) & ((y > 1) | ((y == 1) & up_here(h))), SLOT[-1], SLOT[-2], ym),
        kind(lambda h: (y == 0) & up_here(h), SLOT[-1], SLOT[2], ym),
        kind(always((c == 0) & valid(-1)), SLOT[-1], SIDE, pt),
        kind(
            lambda h: (y == 0) & (x > 0) & jnp.logical_not(by_ring_down(x - 1, h)) & jnp.logical_not(across_down(x - 1, h)),
            SLOT[-1], VIA_Y, xm,
        ),
    ]

    def has_via_y(h):
        up = (y == 3) & ((z > 0) | (x > 0)) & (up_here(h) | jnp.logical_not(across_up(x, h)))
        down = (y == 0) & ((z < 3) | (x < 3)) & (down_here(h) | jnp.logical_not(across_down(x, h)))
        return up | down

    via_z = ((z == 3) & (x == 0)) | ((z == 0) & (x == 3))
    on["y"] = [
        kind(lambda h: (y == 3) & has_via_y(h), VIA_Y, SLOT[2], yp),
        kind(lambda h: (y == 0) & has_via_y(h), VIA_Y, SLOT[-2], ym),
    ]
    on[2] = [
        kind(lambda h: (y == 3) & (x > 0) & jnp.logical_not(by_ring_down(x - 1, h)) & across_down(x - 1, h), SLOT[2], SLOT[-2], xm),
    ]
    on[-2] = [
        kind(lambda h: (y == 0) & (x < 3) & jnp.logical_not(by_ring_up(x + 1, h)) & across_up(x + 1, h), SLOT[-2], SLOT[2], xp),
    ]
    on[8] = [kind(always((x == 3) & (z > 0)), SLOT[8], SLOT[-8], zm)]
    on[-8] = [kind(always((x == 0) & (z < 3)), SLOT[-8], SLOT[8], zp)]
    on[32] = []
    on[-32] = []

    def slot_of(d):
        return VIA_Y if d == "y" else VIA_Z if d == "z" else SLOT[d]

    def comes(d, h):
        return has_via_y(h) if d == "y" else via_z if d == "z" else valid(d)

    def lag(d):
        if d == "z":
            return 1
        if d == "y":
            return pick(((y == 3) & (x == 0)) | ((y == 0) & (x == 3)), 3, 2)
        return hops(d, z, x, y)

    def send(k, h):
        cond, src, dst, device = kinds[k]
        guarded(
            None if cond is None else cond(h),
            lambda: copy(lambda one: one.start(), k, h, src, dst, device),
        )

    def arrived(s, h):
        copy(lambda one: one.wait_recv(), 0, h, s, s, pt)

    def head(h):
        cols = pl.ds(pl.multiple_of(h * DH, DH), DH)
        q = q_ref[:, cols]
        g = g_ref[:, cols]
        top = None
        for t0, w in TILES:
            kt = buf[h, 0, pl.ds(t0, w), :]
            s = nt(q, kt) * (ROOT * math.log2(math.e)) + bias[0:1, t0:t0 + w]
            s_ref[:, t0:t0 + w] = s
            m = jnp.max(s, axis=1, keepdims=True)
            top = m if top is None else jnp.maximum(top, m)
        total = jnp.zeros((TOK, 1), jnp.float32)
        dot = jnp.zeros((TOK, 1), jnp.float32)
        for t0, w in TILES:
            e = jnp.exp2(s_ref[:, t0:t0 + w] - top)
            s_ref[:, t0:t0 + w] = e
            dp = nt(g, buf[h, 1, pl.ds(t0, w), :])
            d_ref[:, t0:t0 + w] = dp
            total = total + jnp.sum(e, axis=1, keepdims=True)
            dot = dot + jnp.sum(e * dp, axis=1, keepdims=True)
        inv = 1.0 / total
        dot = dot * inv
        qu = (nt(up_ref[1, :, cols], q) * ROOT).astype(jnp.bfloat16)
        gu = nt(up_ref[2, :, cols], g).astype(jnp.bfloat16)
        both = jnp.zeros((TOK, 2 * DH), jnp.float32)
        vlow = jnp.zeros((TOK, DH), jnp.float32)
        for t0, w in TILES:
            p = s_ref[:, t0:t0 + w] * inv
            pb = p.astype(jnp.bfloat16)
            ds = (p * (d_ref[:, t0:t0 + w] - dot)).astype(jnp.bfloat16)
            kt = buf[h, 0, pl.ds(t0, w), :]
            lt = lowbuf[pl.ds(t0, w), :]
            both = both + nn(ds, jnp.concatenate([kt, lt], axis=1))
            vlow = vlow + nn(pb, lt)
            acc[0:RANK, t0:t0 + w] += nn(qu, ds)
            acc[RANK:, t0:t0 + w] += nn(gu, pb)
        out0 = (both[:, 0:DH] * ROOT).astype(jnp.bfloat16)
        klow = both[:, DH:DH + RANK] * ROOT
        upart[0:RANK, cols] = (nn(lowt0[...], out0) * NORM).astype(jnp.bfloat16)
        back0[...] += nt(up_ref[0, :, cols], out0)
        lows = jnp.concatenate([klow, vlow[:, RANK:]], axis=1).T.astype(jnp.bfloat16)
        upart[RANK:2 * RANK, cols] = (nn(lows[0:RANK], q) * NORM).astype(jnp.bfloat16)
        upart[2 * RANK:, cols] = (nn(lows[RANK:], g) * NORM).astype(jnp.bfloat16)

    pl.semaphore_wait(barrier, 127)

    def send_own(h):
        @pl.when(h != 1)
        def _():
            for a in range(2):
                load(jnp.maximum(h - 1, 0), a).wait()

        for k in own:
            send(k, h)

    send_own(jnp.int32(0))
    for one in arrays()[:2]:
        one.wait()

    low = nt(x_ref[...], down_ref[...]).astype(jnp.bfloat16)
    lowt0[...] = nt(down_ref[0:RANK, :], x_ref[...]).astype(jnp.bfloat16)
    lowbuf[rows(OWN), :] = low[:, RANK:]
    for one in arrays()[2:]:
        one.wait()

    every = [(d, SLOT[d]) for d in SLOT]
    for d, s in every:
        @pl.when(jnp.logical_not(valid(d)))
        def _(s=s):
            lowbuf[rows(s), :] = jnp.zeros((TOK, DH), jnp.bfloat16)
            rrecv[s] = jnp.zeros((TOK, DH), jnp.bfloat16)

            def zero(h, _):
                for a in range(2):
                    buf[h, a, rows(s), :] = jnp.zeros((TOK, DH), jnp.bfloat16)
                return 0

            lax.fori_loop(0, HEADS, zero, 0)

    @pl.when(jnp.logical_not(side_ok))
    def _():
        lowbuf[rows(SIDE), :] = jnp.zeros((TOK, DH), jnp.bfloat16)
        rrecv[SIDE] = jnp.zeros((TOK, DH), jnp.bfloat16)

        def zero(h, _):
            for a in range(2):
                buf[h, a, rows(SIDE), :] = jnp.zeros((TOK, DH), jnp.bfloat16)
            return 0

        lax.fori_loop(0, HEADS, zero, 0)

    lane = lax.broadcasted_iota(jnp.int32, (8, PAD), 1)
    total_bias = jnp.zeros((8, PAD), jnp.float32)
    for s, (block, ok) in enumerate(
        [(me, None), (pt, None), (side, side_ok)] + [(me - 2 * d, valid(d)) for d in SLOT]
    ):
        kept = mask_ref[0, jnp.clip(block, 0, 127)]
        value = jnp.where(kept > 0, 0.0, MASKED)
        if ok is not None:
            value = jnp.where(ok, value, MASKED)
        inside = (lane >= s * TOK) & (lane < (s + 1) * TOK)
        total_bias = jnp.where(inside, value, total_bias)
    bias[...] = total_bias

    acc[...] = jnp.zeros_like(acc)
    back0[...] = jnp.zeros_like(back0)

    def pair_copy(n, src, dst):
        return pltpu.make_async_remote_copy(
            src_ref=src, dst_ref=dst, send_sem=pair_send.at[n], recv_sem=pair_recv.at[n],
            device_id=(pt,), device_id_type=MESH,
        )

    last = 4
    order = [16, -16, 4, -4, 1, -1, "z", "y", 8, -8, 2, -2, 32, -32]

    def handle(slots, r):
        for d in slots:
            h = r - lag(d)

            @pl.when((h >= 0) & (h < ITEMS) & comes(d, h))
            def _(d=d, h=h):
                arrived(slot_of(d), h)
                for k in on[d]:
                    send(k, h)

    def step(r, _):
        @pl.when(r + LEAD < ITEMS)
        def _():
            send_own(r + LEAD)

        handle(order[:6], r)

        @pl.when((r >= last + 2) & (r <= HEADS + last + 1))
        def _():
            head(r - last - 2)

        handle(order[6:], r)

        @pl.when(r == 0)
        def _():
            pair_copy(0, x_ref, x2).start()

        h = r - last

        @pl.when((h >= 0) & (h < ITEMS))
        def _():
            arrived(PARTNER, h)

            @pl.when(((c == 0) & valid(1)) | ((c == 1) & valid(-1)))
            def _():
                arrived(SIDE, h)

        return 0

    lax.fori_loop(0, ITEMS + last + 1, step, 0)

    for s, _, goes, _, to in direct:
        part = acc[:, s * TOK:(s + 1) * TOK].astype(jnp.bfloat16)
        rsend[s, 0:DH, :] = part[:, 0:DH]
        rsend[s, DH:, :] = jnp.concatenate([part[0:RANK, DH:], part[RANK:, DH:]], axis=1)
        guarded(goes, back_copy(s, to).start)
    pair_copy(1, upart, upart2).start()
    backs[0:RANK, :] = back0[...].astype(jnp.bfloat16)
    pair_copy(2, backs.at[0:RANK], backs2.at[0:RANK]).start()
    pair_copy(0, x_ref, x2).wait_recv()
    pair_copy(1, upart, upart2).wait_recv()
    pair_copy(2, backs.at[0:RANK], backs2.at[0:RANK]).wait_recv()

    def both_up(p, lo, hi):
        r = slice(p * RANK, (p + 1) * RANK)
        return (upart[r, lo:hi].astype(jnp.float32) + upart2[r, lo:hi].astype(jnp.float32)).astype(jnp.bfloat16)

    def both_down(p, start):
        for t in range(0, WIDTH, 512):
            part = nn(backs[p * RANK:(p + 1) * RANK, :], x_ref[:, t:t + 512])
            part = part + nn(backs2[p * RANK:(p + 1) * RANK, :], x2[:, t:t + 512])
            terms[:, start + t:start + t + 512] = (part * NORM).astype(jnp.bfloat16)

    @pl.when(c == 0)
    def _():
        both_down(0, 0)
        terms[:, 3072:3840] = both_up(0, 0, 768)

    @pl.when(c == 1)
    def _():
        terms[:, 0:768] = both_up(0, 768, 1536)
        terms[:, 768:2304] = both_up(1, 0, 1536)
        terms[:, 2304:3840] = both_up(2, 0, 1536)

    here = (x, y, z)

    def peer(axis, at):
        return dev(*(z, at, y, c) if axis == 0 else (z, x, at, c) if axis == 1 else (at, x, y, c))

    def third(ref, k):
        return ref.at[:, k * THIRD:(k + 1) * THIRD]

    def rows16(ref, n):
        return ref.at[pl.ds(pl.multiple_of(n * 16, 16), 16), :]

    def ring_copies(stage, k):
        axis = (k + (0, 1, 2, 0)[stage]) % 3
        mine = here[axis]
        out = []
        for n in (1, 2, 3):
            to, source = (mine + n) % 4, (mine - n + 4) % 4
            if stage == 0:
                src, dst, got = rows16(third(terms, k), to), ring1.at[k, mine], ring1.at[k, source]
            elif stage == 3:
                src = part3.at[k]
                dst, got = rows16(third(result, k), mine), rows16(third(result, k), source)
            else:
                ring, part = ((ring2, part1), (ring3, part2))[stage - 1]
                src, dst, got = part.at[k], ring.at[k, mine], ring.at[k, source]
            slot = (stage * 3 + k) * 3 + n - 1
            out.append(tuple(
                pltpu.make_async_remote_copy(
                    src_ref=src, dst_ref=where, send_sem=ring_send.at[slot], recv_sem=ring_recv.at[slot],
                    device_id=(peer(axis, to),), device_id_type=MESH,
                )
                for where in (dst, got)
            ))
        return out

    def ring_start(stage):
        for k in range(3):
            mine = here[(k + (0, 1, 2, 0)[stage]) % 3]
            if stage == 0:
                ring1[k, mine] = rows16(third(terms, k), mine)[...]
            elif stage == 1:
                ring2[k, mine] = part1[k]
            elif stage == 2:
                ring3[k, mine] = part2[k]
            else:
                rows16(third(result, k), mine)[...] = part3[k]
            for out, _ in ring_copies(stage, k):
                out.start()

    def ring_finish(stage):
        for k in range(3):
            for _, got in ring_copies(stage, k):
                got.wait_recv()
            if stage < 3:
                ring, part = ((ring1, part1), (ring2, part2), (ring3, part3))[stage]
                total = ring[k, 0].astype(jnp.float32)
                for n in range(1, 4):
                    total = total + ring[k, n].astype(jnp.float32)
                part[k] = total.astype(jnp.bfloat16)

    def late_piece(o):
        oz, ox, oy = o // 16, (o // 4) % 4, o % 4
        t = (oy - ox - oz + 8) % 4
        return t < 3, (oz * 4 + ox) * 3 + t

    def place(ref, start, piece):
        return ref.at[
            pl.ds(pl.multiple_of((piece % 4) * 16, 16), 16),
            pl.ds(pl.multiple_of(start + (piece // 4) * 256, 256), 256),
        ]

    def reduce_start(j, of, start, landing):
        def one(n, _):
            o = (i + n) % CHIPS
            owns, piece = of(o)

            @pl.when(owns)
            def _():
                pltpu.make_async_remote_copy(
                    src_ref=place(terms, start, piece), dst_ref=landing.at[63 - n],
                    send_sem=red_send.at[j], recv_sem=red_recv.at[j],
                    device_id=(2 * o + c,), device_id_type=MESH,
                ).start()

            return 0

        lax.fori_loop(1, CHIPS, one, 0)

    def reduce_finish(j, of, start, landing, sums):
        owns, piece = of(i)

        @pl.when(owns)
        def _():
            pltpu.make_async_copy(landing, landing, red_recv.at[j]).wait()
            mine = place(terms, start, piece)[...].astype(jnp.float32)

            def add(n, total):
                return total + landing[n].astype(jnp.float32)

            sums[...] = lax.fori_loop(0, CHIPS - 1, add, mine).astype(jnp.bfloat16)
            pltpu.make_async_copy(sums, place(result, start, piece), gat_recv.at[j]).start()

            def one(n, _):
                o = (i + n) % CHIPS
                pltpu.make_async_remote_copy(
                    src_ref=sums, dst_ref=place(result, start, piece),
                    send_sem=gat_send.at[j], recv_sem=gat_recv.at[j],
                    device_id=(2 * o + c,), device_id_type=MESH,
                ).start()
                return 0

            lax.fori_loop(1, CHIPS, one, 0)

    def gathered(j, start, width):
        part = result.at[:, start:start + width]
        pltpu.make_async_copy(part, part, gat_recv.at[j]).wait()
        pair_copy(4 + j, part, result2.at[:, start:start + width]).start()

    def sent(j, of, landing, pieces):
        owns, _ = of(i)

        @pl.when(owns)
        def _():
            part = landing.at[0:pieces - 1]
            pltpu.make_async_copy(part, part, red_send.at[j]).wait()
            pltpu.make_async_copy(landing, landing, gat_send.at[j]).wait()

        @pl.when(jnp.logical_not(owns))
        def _():
            part = landing.at[0:pieces]
            pltpu.make_async_copy(part, part, red_send.at[j]).wait()

    ring_start(0)
    def drain(h, _):
        for k, (cond, src, dst, device) in enumerate(kinds):
            guarded(
                None if cond is None else cond(h),
                lambda: copy(lambda one: one.wait_send(), k, h, src, dst, device),
            )
        return 0

    lax.fori_loop(0, ITEMS, drain, 0)
    ring_finish(0)
    ring_start(1)

    total = jnp.zeros((TOK, DH), jnp.float32)
    for s, comes_in, _, _, _ in direct:
        guarded(comes_in, back_copy(s, pt).wait_recv)
        total = total + rrecv[s].astype(jnp.float32)
    rest = jnp.concatenate([total[DH:, 0:RANK], total[DH:, RANK:]], axis=0)
    backs[RANK:, :] = (acc[:, 0:TOK] + jnp.concatenate([total[0:DH], rest], axis=1)).astype(jnp.bfloat16)
    pair_copy(3, backs.at[RANK:3 * RANK], backs2.at[RANK:3 * RANK]).start()
    pair_copy(3, backs.at[RANK:3 * RANK], backs2.at[RANK:3 * RANK]).wait_recv()

    @pl.when(c == 0)
    def _():
        both_down(1, EARLY)

    @pl.when(c == 1)
    def _():
        both_down(2, EARLY)

    reduce_start(1, late_piece, EARLY, late_in)
    ring_finish(1)
    ring_start(2)
    back = backs[...].T
    for t in range(0, WIDTH, 512):
        grad_out[:, t:t + 512] = nn(back, down_ref[:, t:t + 512]).astype(jnp.bfloat16)
    ring_finish(2)
    ring_start(3)
    reduce_finish(1, late_piece, EARLY, late_in, late_sum)
    ring_finish(3)

    def early_pair():
        return pair_copy(4, result.at[:, 0:EARLY], result2.at[:, 0:EARLY])

    early_pair().start()
    early_pair().wait_recv()

    def finish_early(a, b):
        down_out[0:RANK, :] = a[:, 0:3072]
        up_out[0:RANK, 0:768] = a[:, 3072:3840]
        up_out[0:RANK, 768:1536] = b[:, 0:768]
        up_out[RANK:2 * RANK, :] = b[:, 768:2304]
        up_out[2 * RANK:, :] = b[:, 2304:3840]

    def finish_late(a, b):
        down_out[RANK:2 * RANK, :] = a[:, EARLY:]
        down_out[2 * RANK:, :] = b[:, EARLY:]

    def finish(f):
        @pl.when(c == 0)
        def _():
            f(result, result2)

        @pl.when(c == 1)
        def _():
            f(result2, result)

    finish(finish_early)
    gathered(1, EARLY, LATE)
    late_pair = pair_copy(5, result.at[:, EARLY:], result2.at[:, EARLY:])
    late_pair.wait_recv()
    finish(finish_late)

    for stage in range(4):
        for k in range(3):
            for out, _ in ring_copies(stage, k):
                out.wait_send()
    sent(1, late_piece, late_in, 48)
    pair_copy(0, x_ref, x2).wait_send()
    pair_copy(1, upart, upart2).wait_send()
    pair_copy(2, backs.at[0:RANK], backs2.at[0:RANK]).wait_send()
    pair_copy(3, backs.at[RANK:3 * RANK], backs2.at[RANK:3 * RANK]).wait_send()
    early_pair().wait_send()
    late_pair.wait_send()
    for s, goes, returns, to, owner in direct:
        guarded(returns, back_copy(s, owner).wait_send)


def attention(mask, inputs, queries, output_gradient, keys, values, down_t, up):
    vm = pl.BlockSpec(memory_space=pltpu.VMEM)
    dma = pltpu.SemaphoreType.DMA
    return pl.pallas_call(
        attention_kernel,
        out_shape=(
            jax.ShapeDtypeStruct((TOK, WIDTH), jnp.bfloat16),
            jax.ShapeDtypeStruct((3 * RANK, WIDTH), jnp.bfloat16),
            jax.ShapeDtypeStruct((3 * RANK, FEAT), jnp.bfloat16),
        ),
        in_specs=[pl.BlockSpec(memory_space=pl.ANY)] * 8,
        out_specs=(vm, vm, vm),
        scratch_shapes=[
            pltpu.SMEM((1, 128), jnp.int32),
            pltpu.VMEM((TOK, WIDTH), jnp.bfloat16),
            pltpu.VMEM((TOK, FEAT), jnp.bfloat16),
            pltpu.VMEM((TOK, FEAT), jnp.bfloat16),
            pltpu.VMEM((3 * RANK, WIDTH), jnp.bfloat16),
            pltpu.VMEM((3, RANK, FEAT), jnp.bfloat16),
            pltpu.VMEM((HEADS, 2, (SLOTS + 2) * TOK, DH), jnp.bfloat16),
            pltpu.VMEM((KEYS + 2 * TOK, DH), jnp.bfloat16),
            pltpu.VMEM((8, PAD), jnp.float32),
            pltpu.VMEM((TOK, PAD), jnp.float32),
            pltpu.VMEM((TOK, PAD), jnp.float32),
            pltpu.VMEM((2 * RANK, PAD), jnp.float32),
            pltpu.VMEM((RANK, TOK), jnp.float32),
            pltpu.VMEM((RANK, TOK), jnp.bfloat16),
            pltpu.VMEM((SLOTS, TOK, DH), jnp.bfloat16),
            pltpu.VMEM((SLOTS, TOK, DH), jnp.bfloat16),
            pltpu.VMEM((TOK, WIDTH), jnp.bfloat16),
            pltpu.VMEM((3 * RANK, FEAT), jnp.bfloat16),
            pltpu.VMEM((3 * RANK, FEAT), jnp.bfloat16),
            pltpu.VMEM((3 * RANK, TOK), jnp.bfloat16),
            pltpu.VMEM((3 * RANK, TOK), jnp.bfloat16),
            pltpu.VMEM((RANK, EARLY + LATE), jnp.bfloat16),
            pltpu.VMEM((RANK, EARLY + LATE), jnp.bfloat16),
            pltpu.VMEM((RANK, EARLY + LATE), jnp.bfloat16),
            pltpu.VMEM((CHIPS - 1, *PIECE), jnp.bfloat16),
            pltpu.VMEM(PIECE, jnp.bfloat16),
            pltpu.VMEM((3, 4, 16, THIRD), jnp.bfloat16),
            pltpu.VMEM((3, 4, 16, THIRD), jnp.bfloat16),
            pltpu.VMEM((3, 4, 16, THIRD), jnp.bfloat16),
            pltpu.VMEM((3, 16, THIRD), jnp.bfloat16),
            pltpu.VMEM((3, 16, THIRD), jnp.bfloat16),
            pltpu.VMEM((3, 16, THIRD), jnp.bfloat16),
            dma((6,)),
            dma((HEADS, 2)),
            dma((39, ITEMS)),
            dma((SLOTS + 2, ITEMS)),
            dma((SLOTS,)), dma((SLOTS,)),
            dma((6,)), dma((6,)), dma((2,)), dma((2,)), dma((2,)), dma((2,)), dma((36,)), dma((36,)),
        ],
        compiler_params=pltpu.CompilerParams(
            collective_id=0, has_side_effects=True, vmem_limit_bytes=56 * 2**20
        ),
        cost_estimate=pl.CostEstimate(flops=12 * 10**9, bytes_accessed=8 * 10**6, transcendentals=7 * 10**6),
        name="attention_gradients",
    )(mask, inputs, queries, output_gradient, keys, values, down_t, up)


def per_device(
    inputs, queries, keys, values, output_gradient, radial_block_mask,
    adapter_down_weight, adapter_up_weight,
):
    down_t = jnp.swapaxes(adapter_down_weight, 1, 2).reshape(3 * RANK, WIDTH)
    input_gradient, down, up = attention(
        radial_block_mask, inputs, queries, output_gradient, keys, values, down_t, adapter_up_weight
    )
    down = jnp.swapaxes(down.reshape(3, RANK, WIDTH), 1, 2).astype(jnp.float32)
    up = up.reshape(3, RANK, FEAT).astype(jnp.float32)
    return (input_gradient, down, up)


def solution(mesh):
    return jax.shard_map(
        per_device,
        mesh=mesh,
        in_specs=(P("frame", None),) * 5 + (P(), P(), P()),
        out_specs=(P("frame", None), P(), P()),
        check_vma=False,
    )
```

```python
import functools
import math

import jax
import jax.numpy as jnp
from jax import lax
from jax.experimental import pallas as pl
from jax.experimental.pallas import tpu as pltpu
from jax.sharding import PartitionSpec as P

MESH = pl.DeviceIdType.MESH
DH = 128
HEADS = 12
TOK = 192
RANK = 64
WIDTH = 3072
FEAT = HEADS * DH
OWN, PARTNER, SIDE = 0, 1, 2
SLOT = {1: 3, -1: 4, 2: 5, -2: 6, 4: 7, -4: 8, 8: 9, -8: 10, 16: 11, -16: 12, 32: 13, -32: 14}
SLOTS = 15
VIA_Y, VIA_Z = 15, 16
KEYS = SLOTS * TOK
PAD = 3072
TILES = [(0, 512), (512, 512), (1024, 512), (1536, 512), (2048, 512), (2560, 320)]
ROOT = 1.0 / math.sqrt(DH)
MASKED = -1e30
LEAD = 1
ITEMS = HEADS + 1
CHIPS = 64
NORM = 1.0 / math.sqrt(128 * TOK)
EARLY = 3840
THIRD = EARLY // 3
LATE = 3072
PIECE = (16, 256)


def nt(a, b):
    return lax.dot_general(a, b, (((1,), (1,)), ((), ())), preferred_element_type=jnp.float32)


def nn(a, b):
    return lax.dot_general(a, b, (((1,), (0,)), ((), ())), preferred_element_type=jnp.float32)


def pick(cond, a, b):
    return jnp.where(cond, a, b)


def hops(d, z, x, y):
    if abs(d) == 16:
        return 1
    if d == 4:
        return pick(x == 0, 2, 1)
    if d == -4:
        return pick(x == 3, 2, 1)
    if d == 1:
        return pick(y == 0, pick(x == 0, 3, 2), 1)
    if d == -1:
        return pick(y == 3, pick(x == 3, 3, 2), 1)
    if d == 8:
        return pick(x >= 2, 2, 3)
    if d == -8:
        return pick(x <= 1, 2, 3)
    if abs(d) == 32:
        return 2
    if d == 2:
        return pick(y >= 2, 2, pick(x == 0, 4, 3))
    return pick(y <= 1, 2, pick(x == 3, 4, 3))


def attention_kernel(
    mask_hbm, x_hbm, q_hbm, g_hbm, k_ref, v_ref, down_hbm, up_hbm,
    grad_out, down_out, up_out,
    mask_ref, x_ref, q_ref, g_ref, down_ref, up_ref,
    buf, lowbuf, bias, s_ref, d_ref, acc, back0, lowt0, rsend, rrecv,
    x2, upart, upart2, backs, backs2, terms, result, result2, late_in, late_sum, ring1, ring2, ring3, part1, part2, part3,
    in_sem, load_sem, send_sem, recv_sem, rs_send, rs_recv,
    pair_send, pair_recv, red_send, red_recv, gat_send, gat_recv, ring_send, ring_recv,
):
    me = lax.axis_index("frame")
    i = me // 2
    c = me % 2
    z = i // 16
    x = (i // 4) % 4
    y = i % 4

    def dev(zz, xx, yy, cc):
        return ((zz + 4) % 4) * 32 + ((xx + 4) % 4) * 8 + ((yy + 4) % 4) * 2 + cc

    yp, ym = dev(z, x, y + 1, c), dev(z, x, y - 1, c)
    xp, xm = dev(z, x + 1, y, c), dev(z, x - 1, y, c)
    zp, zm = dev(z + 1, x, y, c), dev(z - 1, x, y, c)
    pt = dev(z, x, y, 1 - c)
    side = pick(c == 0, me - 1, me + 1)
    side_ok = (side >= 0) & (side < 128)

    def valid(d):
        return (i - d >= 0) & (i - d < 64)

    def rows(s):
        return pl.ds(s * TOK, TOK)

    def load(h, a):
        ref = (k_ref, v_ref)[a]
        return pltpu.make_async_copy(
            ref.at[:, pl.ds(h * DH, DH)], buf.at[h, a, rows(OWN)], load_sem.at[h, a]
        )

    for h in range(HEADS):
        for a in range(2):
            load(h, a).start()

    def arrays():
        pairs = [(x_hbm, x_ref), (down_hbm, down_ref), (q_hbm, q_ref), (g_hbm, g_ref), (up_hbm, up_ref)]
        pairs += [(mask_hbm.at[pl.ds(me, 1), :], mask_ref)]
        return [pltpu.make_async_copy(src, dst, in_sem.at[n]) for n, (src, dst) in enumerate(pairs)]

    for one in arrays():
        one.start()

    barrier = pltpu.get_barrier_semaphore()

    def greet(n, _):
        pl.semaphore_signal(barrier, inc=1, device_id=((me + n) % 128,), device_id_type=MESH)
        return 0

    lax.fori_loop(1, 128, greet, 0)

    def back_copy(s, device):
        return pltpu.make_async_remote_copy(
            src_ref=rsend.at[s], dst_ref=rrecv.at[s],
            send_sem=rs_send.at[s], recv_sem=rs_recv.at[s],
            device_id=(device,), device_id_type=MESH,
        )

    direct = [(PARTNER, None, None, pt, pt), (SIDE, side_ok, side_ok, side, side)]
    direct += [(SLOT[d], valid(-d), valid(d), me + 2 * d, me - 2 * d) for d in SLOT]

    def guarded(cond, f):
        if cond is None:
            f()
        else:
            pl.when(cond)(f)

    def copy(act, kind, n, src, dst, device):
        def one(source, target):
            act(pltpu.make_async_remote_copy(
                src_ref=source, dst_ref=target,
                send_sem=send_sem.at[kind, n], recv_sem=recv_sem.at[dst, n],
                device_id=(device,), device_id_type=MESH,
            ))

        @pl.when(n == 1)
        def _():
            one(lowbuf.at[rows(src)], lowbuf.at[rows(dst)])

        @pl.when(n != 1)
        def _():
            h = jnp.maximum(n - 1, 0)
            one(buf.at[h, :, rows(src)], buf.at[h, :, rows(dst)])

    kinds = []

    def kind(cond, src, dst, device):
        kinds.append((cond, src, dst, device))
        return len(kinds) - 1

    mid = (x == 1) | (x == 2)

    def by_ring_up(xx, h):
        return (xx == 0) | (((xx == 1) | (xx == 2)) & (h % 2 == 0))

    def by_ring_down(xx, h):
        return (xx == 3) | (((xx == 1) | (xx == 2)) & (h % 2 == 1))

    def across_up(xx, h):
        return (xx == 3) | ((h // 2) % 2 == 0)

    def across_down(xx, h):
        return (xx == 0) | ((h // 2) % 2 == 0)

    def up_here(h):
        return by_ring_up(x, h)

    def down_here(h):
        return by_ring_down(x, h)

    def always(cond):
        return lambda h: cond

    own = [
        kind(None, OWN, PARTNER, pt),
        kind(always(y < 3), OWN, SLOT[1], yp), kind(always(y > 0), OWN, SLOT[-1], ym),
        kind(always(x < 3), OWN, SLOT[4], xp), kind(always(x > 0), OWN, SLOT[-4], xm),
        kind(always(z < 3), OWN, SLOT[16], zp), kind(always(z > 0), OWN, SLOT[-16], zm),
        kind(always((z == 0) & (x == 0)), OWN, VIA_Z, zm),
        kind(always((z == 3) & (x == 3)), OWN, VIA_Z, zp),
    ]
    on = {}
    on[16] = [
        kind(always((z == 1) & (x != 0)), SLOT[16], SLOT[32], zp),
        kind(always(z == 3), SLOT[16], SLOT[-32], zp),
        kind(always((x == 3) & (z > 0)), SLOT[16], SLOT[4], xp),
    ]
    on[-16] = [
        kind(always((z == 2) & (x != 3)), SLOT[-16], SLOT[-32], zm),
        kind(always(z == 0), SLOT[-16], SLOT[32], zm),
        kind(always((x == 0) & (z < 3)), SLOT[-16], SLOT[-4], xm),
    ]
    on["z"] = [
        kind(always((z == 3) & (x == 0)), VIA_Z, SLOT[32], zm),
        kind(always((z == 0) & (x == 3)), VIA_Z, SLOT[-32], zp),
    ]
    on[4] = [
        kind(always((x < 2) & valid(4)), SLOT[4], SLOT[8], xp),
        kind(always(x == 3), SLOT[4], SLOT[-8], xp),
        kind(always((y == 3) & valid(4)), SLOT[4], SLOT[1], yp),
        kind(lambda h: (y == 2) & valid(4) & up_here(h), SLOT[4], VIA_Y, yp),
    ]
    on[-4] = [
        kind(always((x > 1) & valid(-4)), SLOT[-4], SLOT[-8], xm),
        kind(always(x == 0), SLOT[-4], SLOT[8], xm),
        kind(always((y == 0) & valid(-4)), SLOT[-4], SLOT[-1], ym),
        kind(lambda h: (y == 1) & valid(-4) & down_here(h), SLOT[-4], VIA_Y, ym),
    ]
    on[1] = [
        kind(lambda h: valid(1) & ((y < 2) | ((y == 2) & jnp.logical_not(up_here(h)))), SLOT[1], SLOT[2], yp),
        kind(lambda h: (y == 3) & jnp.logical_not(up_here(h)), SLOT[1], SLOT[-2], yp),
        kind(always((c == 1) & valid(1)), SLOT[1], SIDE, pt),
        kind(
            lambda h: (y == 3) & (x < 3) & jnp.logical_not(by_ring_up(x + 1, h)) & jnp.logical_not(across_up(x + 1, h)),
            SLOT[1], VIA_Y, xp,
        ),
    ]
    on[-1] = [
        kind(lambda h: valid(-1) & ((y > 1) | ((y == 1) & up_here(h))), SLOT[-1], SLOT[-2], ym),
        kind(lambda h: (y == 0) & up_here(h), SLOT[-1], SLOT[2], ym),
        kind(always((c == 0) & valid(-1)), SLOT[-1], SIDE, pt),
        kind(
            lambda h: (y == 0) & (x > 0) & jnp.logical_not(by_ring_down(x - 1, h)) & jnp.logical_not(across_down(x - 1, h)),
            SLOT[-1], VIA_Y, xm,
        ),
    ]

    def has_via_y(h):
        up = (y == 3) & ((z > 0) | (x > 0)) & (up_here(h) | jnp.logical_not(across_up(x, h)))
        down = (y == 0) & ((z < 3) | (x < 3)) & (down_here(h) | jnp.logical_not(across_down(x, h)))
        return up | down

    via_z = ((z == 3) & (x == 0)) | ((z == 0) & (x == 3))
    on["y"] = [
        kind(lambda h: (y == 3) & has_via_y(h), VIA_Y, SLOT[2], yp),
        kind(lambda h: (y == 0) & has_via_y(h), VIA_Y, SLOT[-2], ym),
    ]
    on[2] = [
        kind(lambda h: (y == 3) & (x > 0) & jnp.logical_not(by_ring_down(x - 1, h)) & across_down(x - 1, h), SLOT[2], SLOT[-2], xm),
    ]
    on[-2] = [
        kind(lambda h: (y == 0) & (x < 3) & jnp.logical_not(by_ring_up(x + 1, h)) & across_up(x + 1, h), SLOT[-2], SLOT[2], xp),
    ]
    on[8] = [kind(always((x == 3) & (z > 0)), SLOT[8], SLOT[-8], zm)]
    on[-8] = [kind(always((x == 0) & (z < 3)), SLOT[-8], SLOT[8], zp)]
    on[32] = []
    on[-32] = []

    def slot_of(d):
        return VIA_Y if d == "y" else VIA_Z if d == "z" else SLOT[d]

    def comes(d, h):
        return has_via_y(h) if d == "y" else via_z if d == "z" else valid(d)

    def lag(d):
        if d == "z":
            return 1
        if d == "y":
            return pick(((y == 3) & (x == 0)) | ((y == 0) & (x == 3)), 3, 2)
        return hops(d, z, x, y)

    def send(k, h):
        cond, src, dst, device = kinds[k]
        guarded(
            None if cond is None else cond(h),
            lambda: copy(lambda one: one.start(), k, h, src, dst, device),
        )

    def arrived(s, h):
        copy(lambda one: one.wait_recv(), 0, h, s, s, pt)

    def head(h):
        cols = pl.ds(pl.multiple_of(h * DH, DH), DH)
        q = q_ref[:, cols]
        g = g_ref[:, cols]
        top = None
        for t0, w in TILES:
            kt = buf[h, 0, pl.ds(t0, w), :]
            s = nt(q, kt) * (ROOT * math.log2(math.e)) + bias[0:1, t0:t0 + w]
            s_ref[:, t0:t0 + w] = s
            m = jnp.max(s, axis=1, keepdims=True)
            top = m if top is None else jnp.maximum(top, m)
        total = jnp.zeros((TOK, 1), jnp.float32)
        dot = jnp.zeros((TOK, 1), jnp.float32)
        for t0, w in TILES:
            e = jnp.exp2(s_ref[:, t0:t0 + w] - top)
            s_ref[:, t0:t0 + w] = e
            dp = nt(g, buf[h, 1, pl.ds(t0, w), :])
            d_ref[:, t0:t0 + w] = dp
            total = total + jnp.sum(e, axis=1, keepdims=True)
            dot = dot + jnp.sum(e * dp, axis=1, keepdims=True)
        inv = 1.0 / total
        dot = dot * inv
        qu = (nt(up_ref[1, :, cols], q) * ROOT).astype(jnp.bfloat16)
        gu = nt(up_ref[2, :, cols], g).astype(jnp.bfloat16)
        both = jnp.zeros((TOK, 2 * DH), jnp.float32)
        vlow = jnp.zeros((TOK, DH), jnp.float32)
        for t0, w in TILES:
            p = s_ref[:, t0:t0 + w] * inv
            pb = p.astype(jnp.bfloat16)
            ds = (p * (d_ref[:, t0:t0 + w] - dot)).astype(jnp.bfloat16)
            kt = buf[h, 0, pl.ds(t0, w), :]
            lt = lowbuf[pl.ds(t0, w), :]
            both = both + nn(ds, jnp.concatenate([kt, lt], axis=1))
            vlow = vlow + nn(pb, lt)
            acc[0:RANK, t0:t0 + w] += nn(qu, ds)
            acc[RANK:, t0:t0 + w] += nn(gu, pb)
        out0 = (both[:, 0:DH] * ROOT).astype(jnp.bfloat16)
        klow = both[:, DH:DH + RANK] * ROOT
        upart[0:RANK, cols] = (nn(lowt0[...], out0) * NORM).astype(jnp.bfloat16)
        back0[...] += nt(up_ref[0, :, cols], out0)
        lows = jnp.concatenate([klow, vlow[:, RANK:]], axis=1).T.astype(jnp.bfloat16)
        upart[RANK:2 * RANK, cols] = (nn(lows[0:RANK], q) * NORM).astype(jnp.bfloat16)
        upart[2 * RANK:, cols] = (nn(lows[RANK:], g) * NORM).astype(jnp.bfloat16)

    pl.semaphore_wait(barrier, 127)

    def send_own(h):
        @pl.when(h != 1)
        def _():
            for a in range(2):
                load(jnp.maximum(h - 1, 0), a).wait()

        for k in own:
            send(k, h)

    send_own(jnp.int32(0))
    for one in arrays()[:2]:
        one.wait()

    low = nt(x_ref[...], down_ref[...]).astype(jnp.bfloat16)
    lowt0[...] = nt(down_ref[0:RANK, :], x_ref[...]).astype(jnp.bfloat16)
    lowbuf[rows(OWN), :] = low[:, RANK:]
    for one in arrays()[2:]:
        one.wait()

    every = [(d, SLOT[d]) for d in SLOT]
    for d, s in every:
        @pl.when(jnp.logical_not(valid(d)))
        def _(s=s):
            lowbuf[rows(s), :] = jnp.zeros((TOK, DH), jnp.bfloat16)
            rrecv[s] = jnp.zeros((TOK, DH), jnp.bfloat16)

            def zero(h, _):
                for a in range(2):
                    buf[h, a, rows(s), :] = jnp.zeros((TOK, DH), jnp.bfloat16)
                return 0

            lax.fori_loop(0, HEADS, zero, 0)

    @pl.when(jnp.logical_not(side_ok))
    def _():
        lowbuf[rows(SIDE), :] = jnp.zeros((TOK, DH), jnp.bfloat16)
        rrecv[SIDE] = jnp.zeros((TOK, DH), jnp.bfloat16)

        def zero(h, _):
            for a in range(2):
                buf[h, a, rows(SIDE), :] = jnp.zeros((TOK, DH), jnp.bfloat16)
            return 0

        lax.fori_loop(0, HEADS, zero, 0)

    lane = lax.broadcasted_iota(jnp.int32, (8, PAD), 1)
    total_bias = jnp.zeros((8, PAD), jnp.float32)
    for s, (block, ok) in enumerate(
        [(me, None), (pt, None), (side, side_ok)] + [(me - 2 * d, valid(d)) for d in SLOT]
    ):
        kept = mask_ref[0, jnp.clip(block, 0, 127)]
        value = jnp.where(kept > 0, 0.0, MASKED)
        if ok is not None:
            value = jnp.where(ok, value, MASKED)
        inside = (lane >= s * TOK) & (lane < (s + 1) * TOK)
        total_bias = jnp.where(inside, value, total_bias)
    bias[...] = total_bias

    acc[...] = jnp.zeros_like(acc)
    back0[...] = jnp.zeros_like(back0)

    def pair_copy(n, src, dst):
        return pltpu.make_async_remote_copy(
            src_ref=src, dst_ref=dst, send_sem=pair_send.at[n], recv_sem=pair_recv.at[n],
            device_id=(pt,), device_id_type=MESH,
        )

    last = 4
    order = [16, -16, 4, -4, 1, -1, "z", "y", 8, -8, 2, -2, 32, -32]

    def handle(slots, r):
        for d in slots:
            h = r - lag(d)

            @pl.when((h >= 0) & (h < ITEMS) & comes(d, h))
            def _(d=d, h=h):
                arrived(slot_of(d), h)
                for k in on[d]:
                    send(k, h)

    def step(r, _):
        @pl.when(r + LEAD < ITEMS)
        def _():
            send_own(r + LEAD)

        handle(order[:6], r)

        @pl.when((r >= last + 2) & (r <= HEADS + last + 1))
        def _():
            head(r - last - 2)

        handle(order[6:], r)

        @pl.when(r == 0)
        def _():
            pair_copy(0, x_ref, x2).start()

        h = r - last

        @pl.when((h >= 0) & (h < ITEMS))
        def _():
            arrived(PARTNER, h)

            @pl.when(((c == 0) & valid(1)) | ((c == 1) & valid(-1)))
            def _():
                arrived(SIDE, h)

        return 0

    lax.fori_loop(0, ITEMS + last + 1, step, 0)

    for s, _, goes, _, to in direct:
        part = acc[:, s * TOK:(s + 1) * TOK].astype(jnp.bfloat16)
        rsend[s, 0:DH, :] = part[:, 0:DH]
        rsend[s, DH:, :] = jnp.concatenate([part[0:RANK, DH:], part[RANK:, DH:]], axis=1)
        guarded(goes, back_copy(s, to).start)
    pair_copy(1, upart, upart2).start()
    backs[0:RANK, :] = back0[...].astype(jnp.bfloat16)
    pair_copy(2, backs.at[0:RANK], backs2.at[0:RANK]).start()
    pair_copy(0, x_ref, x2).wait_recv()
    pair_copy(1, upart, upart2).wait_recv()
    pair_copy(2, backs.at[0:RANK], backs2.at[0:RANK]).wait_recv()

    def both_up(p, lo, hi):
        r = slice(p * RANK, (p + 1) * RANK)
        return (upart[r, lo:hi].astype(jnp.float32) + upart2[r, lo:hi].astype(jnp.float32)).astype(jnp.bfloat16)

    def both_down(p, start):
        for t in range(0, WIDTH, 512):
            part = nn(backs[p * RANK:(p + 1) * RANK, :], x_ref[:, t:t + 512])
            part = part + nn(backs2[p * RANK:(p + 1) * RANK, :], x2[:, t:t + 512])
            terms[:, start + t:start + t + 512] = (part * NORM).astype(jnp.bfloat16)

    @pl.when(c == 0)
    def _():
        both_down(0, 0)
        terms[:, 3072:3840] = both_up(0, 0, 768)

    @pl.when(c == 1)
    def _():
        terms[:, 0:768] = both_up(0, 768, 1536)
        terms[:, 768:2304] = both_up(1, 0, 1536)
        terms[:, 2304:3840] = both_up(2, 0, 1536)

    here = (x, y, z)

    def peer(axis, at):
        return dev(*(z, at, y, c) if axis == 0 else (z, x, at, c) if axis == 1 else (at, x, y, c))

    def third(ref, k):
        return ref.at[:, k * THIRD:(k + 1) * THIRD]

    def rows16(ref, n):
        return ref.at[pl.ds(pl.multiple_of(n * 16, 16), 16), :]

    def ring_copies(stage, k):
        axis = (k + (0, 1, 2, 0)[stage]) % 3
        mine = here[axis]
        out = []
        for n in (1, 2, 3):
            to, source = (mine + n) % 4, (mine - n + 4) % 4
            if stage == 0:
                src, dst, got = rows16(third(terms, k), to), ring1.at[k, mine], ring1.at[k, source]
            elif stage == 3:
                src = part3.at[k]
                dst, got = rows16(third(result, k), mine), rows16(third(result, k), source)
            else:
                ring, part = ((ring2, part1), (ring3, part2))[stage - 1]
                src, dst, got = part.at[k], ring.at[k, mine], ring.at[k, source]
            slot = (stage * 3 + k) * 3 + n - 1
            out.append(tuple(
                pltpu.make_async_remote_copy(
                    src_ref=src, dst_ref=where, send_sem=ring_send.at[slot], recv_sem=ring_recv.at[slot],
                    device_id=(peer(axis, to),), device_id_type=MESH,
                )
                for where in (dst, got)
            ))
        return out

    def ring_start(stage):
        for k in range(3):
            mine = here[(k + (0, 1, 2, 0)[stage]) % 3]
            if stage == 0:
                ring1[k, mine] = rows16(third(terms, k), mine)[...]
            elif stage == 1:
                ring2[k, mine] = part1[k]
            elif stage == 2:
                ring3[k, mine] = part2[k]
            else:
                rows16(third(result, k), mine)[...] = part3[k]
            for out, _ in ring_copies(stage, k):
                out.start()

    def ring_finish(stage):
        for k in range(3):
            for _, got in ring_copies(stage, k):
                got.wait_recv()
            if stage < 3:
                ring, part = ((ring1, part1), (ring2, part2), (ring3, part3))[stage]
                total = ring[k, 0].astype(jnp.float32)
                for n in range(1, 4):
                    total = total + ring[k, n].astype(jnp.float32)
                part[k] = total.astype(jnp.bfloat16)

    def late_piece(o):
        oz, ox, oy = o // 16, (o // 4) % 4, o % 4
        t = (oy - ox - oz + 8) % 4
        return t < 3, (oz * 4 + ox) * 3 + t

    def place(ref, start, piece):
        return ref.at[
            pl.ds(pl.multiple_of((piece % 4) * 16, 16), 16),
            pl.ds(pl.multiple_of(start + (piece // 4) * 256, 256), 256),
        ]

    def reduce_start(j, of, start, landing):
        def one(n, _):
            o = (i + n) % CHIPS
            owns, piece = of(o)

            @pl.when(owns)
            def _():
                pltpu.make_async_remote_copy(
                    src_ref=place(terms, start, piece), dst_ref=landing.at[63 - n],
                    send_sem=red_send.at[j], recv_sem=red_recv.at[j],
                    device_id=(2 * o + c,), device_id_type=MESH,
                ).start()

            return 0

        lax.fori_loop(1, CHIPS, one, 0)

    def reduce_finish(j, of, start, landing, sums):
        owns, piece = of(i)

        @pl.when(owns)
        def _():
            pltpu.make_async_copy(landing, landing, red_recv.at[j]).wait()
            mine = place(terms, start, piece)[...].astype(jnp.float32)

            def add(n, total):
                return total + landing[n].astype(jnp.float32)

            sums[...] = lax.fori_loop(0, CHIPS - 1, add, mine).astype(jnp.bfloat16)
            pltpu.make_async_copy(sums, place(result, start, piece), gat_recv.at[j]).start()

            def one(n, _):
                o = (i + n) % CHIPS
                pltpu.make_async_remote_copy(
                    src_ref=sums, dst_ref=place(result, start, piece),
                    send_sem=gat_send.at[j], recv_sem=gat_recv.at[j],
                    device_id=(2 * o + c,), device_id_type=MESH,
                ).start()
                return 0

            lax.fori_loop(1, CHIPS, one, 0)

    def gathered(j, start, width):
        part = result.at[:, start:start + width]
        pltpu.make_async_copy(part, part, gat_recv.at[j]).wait()
        pair_copy(4 + j, part, result2.at[:, start:start + width]).start()

    def sent(j, of, landing, pieces):
        owns, _ = of(i)

        @pl.when(owns)
        def _():
            part = landing.at[0:pieces - 1]
            pltpu.make_async_copy(part, part, red_send.at[j]).wait()
            pltpu.make_async_copy(landing, landing, gat_send.at[j]).wait()

        @pl.when(jnp.logical_not(owns))
        def _():
            part = landing.at[0:pieces]
            pltpu.make_async_copy(part, part, red_send.at[j]).wait()

    ring_start(0)
    def drain(h, _):
        for k, (cond, src, dst, device) in enumerate(kinds):
            guarded(
                None if cond is None else cond(h),
                lambda: copy(lambda one: one.wait_send(), k, h, src, dst, device),
            )
        return 0

    lax.fori_loop(0, ITEMS, drain, 0)
    ring_finish(0)
    ring_start(1)

    total = jnp.zeros((TOK, DH), jnp.float32)
    for s, comes_in, _, _, _ in direct:
        guarded(comes_in, back_copy(s, pt).wait_recv)
        total = total + rrecv[s].astype(jnp.float32)
    rest = jnp.concatenate([total[DH:, 0:RANK], total[DH:, RANK:]], axis=0)
    backs[RANK:, :] = (acc[:, 0:TOK] + jnp.concatenate([total[0:DH], rest], axis=1)).astype(jnp.bfloat16)
    pair_copy(3, backs.at[RANK:3 * RANK], backs2.at[RANK:3 * RANK]).start()
    pair_copy(3, backs.at[RANK:3 * RANK], backs2.at[RANK:3 * RANK]).wait_recv()

    @pl.when(c == 0)
    def _():
        both_down(1, EARLY)

    @pl.when(c == 1)
    def _():
        both_down(2, EARLY)

    reduce_start(1, late_piece, EARLY, late_in)
    ring_finish(1)
    ring_start(2)
    back = backs[...].T
    for t in range(0, WIDTH, 512):
        grad_out[:, t:t + 512] = nn(back, down_ref[:, t:t + 512]).astype(jnp.bfloat16)
    ring_finish(2)
    ring_start(3)
    reduce_finish(1, late_piece, EARLY, late_in, late_sum)
    ring_finish(3)

    def early_pair():
        return pair_copy(4, result.at[:, 0:EARLY], result2.at[:, 0:EARLY])

    early_pair().start()
    early_pair().wait_recv()

    def finish_early(a, b):
        down_out[0:RANK, :] = a[:, 0:3072]
        up_out[0:RANK, 0:768] = a[:, 3072:3840]
        up_out[0:RANK, 768:1536] = b[:, 0:768]
        up_out[RANK:2 * RANK, :] = b[:, 768:2304]
        up_out[2 * RANK:, :] = b[:, 2304:3840]

    def finish_late(a, b):
        down_out[RANK:2 * RANK, :] = a[:, EARLY:]
        down_out[2 * RANK:, :] = b[:, EARLY:]

    def finish(f):
        @pl.when(c == 0)
        def _():
            f(result, result2)

        @pl.when(c == 1)
        def _():
            f(result2, result)

    finish(finish_early)
    gathered(1, EARLY, LATE)
    late_pair = pair_copy(5, result.at[:, EARLY:], result2.at[:, EARLY:])
    late_pair.wait_recv()
    finish(finish_late)

    for stage in range(4):
        for k in range(3):
            for out, _ in ring_copies(stage, k):
                out.wait_send()
    sent(1, late_piece, late_in, 48)
    pair_copy(0, x_ref, x2).wait_send()
    pair_copy(1, upart, upart2).wait_send()
    pair_copy(2, backs.at[0:RANK], backs2.at[0:RANK]).wait_send()
    pair_copy(3, backs.at[RANK:3 * RANK], backs2.at[RANK:3 * RANK]).wait_send()
    early_pair().wait_send()
    late_pair.wait_send()
    for s, goes, returns, to, owner in direct:
        guarded(returns, back_copy(s, owner).wait_send)


def attention(mask, inputs, queries, output_gradient, keys, values, down_t, up):
    vm = pl.BlockSpec(memory_space=pltpu.VMEM)
    dma = pltpu.SemaphoreType.DMA
    return pl.pallas_call(
        attention_kernel,
        out_shape=(
            jax.ShapeDtypeStruct((TOK, WIDTH), jnp.bfloat16),
            jax.ShapeDtypeStruct((3 * RANK, WIDTH), jnp.bfloat16),
            jax.ShapeDtypeStruct((3 * RANK, FEAT), jnp.bfloat16),
        ),
        in_specs=[pl.BlockSpec(memory_space=pl.ANY)] * 8,
        out_specs=(vm, vm, vm),
        scratch_shapes=[
            pltpu.SMEM((1, 128), jnp.int32),
            pltpu.VMEM((TOK, WIDTH), jnp.bfloat16),
            pltpu.VMEM((TOK, FEAT), jnp.bfloat16),
            pltpu.VMEM((TOK, FEAT), jnp.bfloat16),
            pltpu.VMEM((3 * RANK, WIDTH), jnp.bfloat16),
            pltpu.VMEM((3, RANK, FEAT), jnp.bfloat16),
            pltpu.VMEM((HEADS, 2, (SLOTS + 2) * TOK, DH), jnp.bfloat16),
            pltpu.VMEM((KEYS + 2 * TOK, DH), jnp.bfloat16),
            pltpu.VMEM((8, PAD), jnp.float32),
            pltpu.VMEM((TOK, PAD), jnp.float32),
            pltpu.VMEM((TOK, PAD), jnp.float32),
            pltpu.VMEM((2 * RANK, PAD), jnp.float32),
            pltpu.VMEM((RANK, TOK), jnp.float32),
            pltpu.VMEM((RANK, TOK), jnp.bfloat16),
            pltpu.VMEM((SLOTS, TOK, DH), jnp.bfloat16),
            pltpu.VMEM((SLOTS, TOK, DH), jnp.bfloat16),
            pltpu.VMEM((TOK, WIDTH), jnp.bfloat16),
            pltpu.VMEM((3 * RANK, FEAT), jnp.bfloat16),
            pltpu.VMEM((3 * RANK, FEAT), jnp.bfloat16),
            pltpu.VMEM((3 * RANK, TOK), jnp.bfloat16),
            pltpu.VMEM((3 * RANK, TOK), jnp.bfloat16),
            pltpu.VMEM((RANK, EARLY + LATE), jnp.bfloat16),
            pltpu.VMEM((RANK, EARLY + LATE), jnp.bfloat16),
            pltpu.VMEM((RANK, EARLY + LATE), jnp.bfloat16),
            pltpu.VMEM((CHIPS - 1, *PIECE), jnp.bfloat16),
            pltpu.VMEM(PIECE, jnp.bfloat16),
            pltpu.VMEM((3, 4, 16, THIRD), jnp.bfloat16),
            pltpu.VMEM((3, 4, 16, THIRD), jnp.bfloat16),
            pltpu.VMEM((3, 4, 16, THIRD), jnp.bfloat16),
            pltpu.VMEM((3, 16, THIRD), jnp.bfloat16),
            pltpu.VMEM((3, 16, THIRD), jnp.bfloat16),
            pltpu.VMEM((3, 16, THIRD), jnp.bfloat16),
            dma((6,)),
            dma((HEADS, 2)),
            dma((39, ITEMS)),
            dma((SLOTS + 2, ITEMS)),
            dma((SLOTS,)), dma((SLOTS,)),
            dma((6,)), dma((6,)), dma((2,)), dma((2,)), dma((2,)), dma((2,)), dma((36,)), dma((36,)),
        ],
        compiler_params=pltpu.CompilerParams(
            collective_id=0, has_side_effects=True, vmem_limit_bytes=56 * 2**20
        ),
        cost_estimate=pl.CostEstimate(flops=12 * 10**9, bytes_accessed=8 * 10**6, transcendentals=7 * 10**6),
        name="attention_gradients",
    )(mask, inputs, queries, output_gradient, keys, values, down_t, up)


def finish_kernel(grad_in, down_in, up_in, grad, down, up):
    grad[...] = grad_in[...]
    down[...] = down_in[...].astype(jnp.float32)
    up[...] = up_in[...].astype(jnp.float32)


def finished(grad, down, up):
    parts = 3

    def block(width):
        return pl.BlockSpec((TOK, width // parts), lambda n: (0, n))

    specs = [block(WIDTH), block(WIDTH), block(FEAT)]
    return pl.pallas_call(
        finish_kernel,
        grid=(parts,),
        out_shape=(
            jax.ShapeDtypeStruct(grad.shape, grad.dtype),
            jax.ShapeDtypeStruct(down.shape, jnp.float32),
            jax.ShapeDtypeStruct(up.shape, jnp.float32),
        ),
        in_specs=specs,
        out_specs=specs,
        name="final_types",
    )(grad, down, up)


def per_device(
    inputs, queries, keys, values, output_gradient, radial_block_mask,
    adapter_down_weight, adapter_up_weight,
):
    down_t = jnp.swapaxes(adapter_down_weight, 1, 2).reshape(3 * RANK, WIDTH)
    input_gradient, down, up = finished(*attention(
        radial_block_mask, inputs, queries, output_gradient, keys, values, down_t, adapter_up_weight
    ))
    down = jnp.swapaxes(down.reshape(3, RANK, WIDTH), 1, 2)
    return (input_gradient, down, up.reshape(3, RANK, FEAT))


def solution(mesh):
    return jax.shard_map(
        per_device,
        mesh=mesh,
        in_specs=(P("frame", None),) * 5 + (P(), P(), P()),
        out_specs=(P("frame", None), P(), P()),
        check_vma=False,
    )
```

```python
import functools
import math

import jax
import jax.numpy as jnp
from jax import lax
from jax.experimental import pallas as pl
from jax.experimental.pallas import tpu as pltpu
from jax.sharding import PartitionSpec as P

MESH = pl.DeviceIdType.MESH
DH = 128
HEADS = 12
TOK = 192
RANK = 64
WIDTH = 3072
FEAT = HEADS * DH
OWN, PARTNER, SIDE = 0, 1, 2
SLOT = {1: 3, -1: 4, 2: 5, -2: 6, 4: 7, -4: 8, 8: 9, -8: 10, 16: 11, -16: 12, 32: 13, -32: 14}
SLOTS = 15
VIA_Y, VIA_Z = 15, 16
KEYS = SLOTS * TOK
PAD = 3072
TILES = [(0, 512), (512, 512), (1024, 512), (1536, 512), (2048, 512), (2560, 320)]
ROOT = 1.0 / math.sqrt(DH)
MASKED = -1e30
LEAD = 1
ITEMS = HEADS + 1
CHIPS = 64
NORM = 1.0 / math.sqrt(128 * TOK)
EARLY = 3840
THIRD = EARLY // 3
LATE = 3072
PIECE = (16, 256)


def nt(a, b):
    return lax.dot_general(a, b, (((1,), (1,)), ((), ())), preferred_element_type=jnp.float32)


def nn(a, b):
    return lax.dot_general(a, b, (((1,), (0,)), ((), ())), preferred_element_type=jnp.float32)


def pick(cond, a, b):
    return jnp.where(cond, a, b)


def hops(d, z, x, y):
    if abs(d) == 16:
        return 1
    if d == 4:
        return pick(x == 0, 2, 1)
    if d == -4:
        return pick(x == 3, 2, 1)
    if d == 1:
        return pick(y == 0, pick(x == 0, 3, 2), 1)
    if d == -1:
        return pick(y == 3, pick(x == 3, 3, 2), 1)
    if d == 8:
        return pick(x >= 2, 2, 3)
    if d == -8:
        return pick(x <= 1, 2, 3)
    if abs(d) == 32:
        return 2
    if d == 2:
        return pick(y >= 2, 2, pick(x == 0, 4, 3))
    return pick(y <= 1, 2, pick(x == 3, 4, 3))


def attention_kernel(
    mask_hbm, x_hbm, q_hbm, g_hbm, k_ref, v_ref, down_hbm, up_hbm,
    grad_hbm, down_out, up_out,
    grad_out, grad_sem, mask_ref, x_ref, q_ref, g_ref, down_ref, up_ref,
    buf, lowbuf, bias, s_ref, d_ref, acc, back0, lowt0, rsend, rrecv,
    x2, upart, upart2, backs, backs2, terms, result, result2, late_in, late_sum, ring1, ring2, ring3, part1, part2, part3,
    in_sem, load_sem, send_sem, recv_sem, rs_send, rs_recv,
    pair_send, pair_recv, red_send, red_recv, gat_send, gat_recv, ring_send, ring_recv,
):
    me = lax.axis_index("frame")
    i = me // 2
    c = me % 2
    z = i // 16
    x = (i // 4) % 4
    y = i % 4

    def dev(zz, xx, yy, cc):
        return ((zz + 4) % 4) * 32 + ((xx + 4) % 4) * 8 + ((yy + 4) % 4) * 2 + cc

    yp, ym = dev(z, x, y + 1, c), dev(z, x, y - 1, c)
    xp, xm = dev(z, x + 1, y, c), dev(z, x - 1, y, c)
    zp, zm = dev(z + 1, x, y, c), dev(z - 1, x, y, c)
    pt = dev(z, x, y, 1 - c)
    side = pick(c == 0, me - 1, me + 1)
    side_ok = (side >= 0) & (side < 128)

    def valid(d):
        return (i - d >= 0) & (i - d < 64)

    def rows(s):
        return pl.ds(s * TOK, TOK)

    def load(h, a):
        ref = (k_ref, v_ref)[a]
        return pltpu.make_async_copy(
            ref.at[:, pl.ds(h * DH, DH)], buf.at[h, a, rows(OWN)], load_sem.at[h, a]
        )

    for h in range(HEADS):
        for a in range(2):
            load(h, a).start()

    def arrays():
        pairs = [(x_hbm, x_ref), (down_hbm, down_ref), (q_hbm, q_ref), (g_hbm, g_ref), (up_hbm, up_ref)]
        pairs += [(mask_hbm.at[pl.ds(me, 1), :], mask_ref)]
        return [pltpu.make_async_copy(src, dst, in_sem.at[n]) for n, (src, dst) in enumerate(pairs)]

    for one in arrays():
        one.start()

    barrier = pltpu.get_barrier_semaphore()

    def greet(n, _):
        pl.semaphore_signal(barrier, inc=1, device_id=((me + n) % 128,), device_id_type=MESH)
        return 0

    lax.fori_loop(1, 128, greet, 0, unroll=True)

    def back_copy(s, device):
        return pltpu.make_async_remote_copy(
            src_ref=rsend.at[s], dst_ref=rrecv.at[s],
            send_sem=rs_send.at[s], recv_sem=rs_recv.at[s],
            device_id=(device,), device_id_type=MESH,
        )

    direct = [(PARTNER, None, None, pt, pt), (SIDE, side_ok, side_ok, side, side)]
    direct += [(SLOT[d], valid(-d), valid(d), me + 2 * d, me - 2 * d) for d in SLOT]

    def guarded(cond, f):
        if cond is None:
            f()
        else:
            pl.when(cond)(f)

    def copy(act, kind, n, src, dst, device):
        def one(source, target):
            act(pltpu.make_async_remote_copy(
                src_ref=source, dst_ref=target,
                send_sem=send_sem.at[kind, n], recv_sem=recv_sem.at[dst, n],
                device_id=(device,), device_id_type=MESH,
            ))

        @pl.when(n == 1)
        def _():
            one(lowbuf.at[rows(src)], lowbuf.at[rows(dst)])

        @pl.when(n != 1)
        def _():
            h = jnp.maximum(n - 1, 0)
            one(buf.at[h, :, rows(src)], buf.at[h, :, rows(dst)])

    kinds = []

    def kind(cond, src, dst, device):
        kinds.append((cond, src, dst, device))
        return len(kinds) - 1

    mid = (x == 1) | (x == 2)

    def by_ring_up(xx, h):
        return (xx == 0) | (((xx == 1) | (xx == 2)) & (h % 2 == 0))

    def by_ring_down(xx, h):
        return (xx == 3) | (((xx == 1) | (xx == 2)) & (h % 2 == 1))

    def across_up(xx, h):
        return (xx == 3) | ((h // 2) % 2 == 0)

    def across_down(xx, h):
        return (xx == 0) | ((h // 2) % 2 == 0)

    def up_here(h):
        return by_ring_up(x, h)

    def down_here(h):
        return by_ring_down(x, h)

    def always(cond):
        return lambda h: cond

    own = [
        kind(None, OWN, PARTNER, pt),
        kind(always(y < 3), OWN, SLOT[1], yp), kind(always(y > 0), OWN, SLOT[-1], ym),
        kind(always(x < 3), OWN, SLOT[4], xp), kind(always(x > 0), OWN, SLOT[-4], xm),
        kind(always(z < 3), OWN, SLOT[16], zp), kind(always(z > 0), OWN, SLOT[-16], zm),
        kind(always((z == 0) & (x == 0)), OWN, VIA_Z, zm),
        kind(always((z == 3) & (x == 3)), OWN, VIA_Z, zp),
    ]
    on = {}
    on[16] = [
        kind(always((z == 1) & (x != 0)), SLOT[16], SLOT[32], zp),
        kind(always(z == 3), SLOT[16], SLOT[-32], zp),
        kind(always((x == 3) & (z > 0)), SLOT[16], SLOT[4], xp),
    ]
    on[-16] = [
        kind(always((z == 2) & (x != 3)), SLOT[-16], SLOT[-32], zm),
        kind(always(z == 0), SLOT[-16], SLOT[32], zm),
        kind(always((x == 0) & (z < 3)), SLOT[-16], SLOT[-4], xm),
    ]
    on["z"] = [
        kind(always((z == 3) & (x == 0)), VIA_Z, SLOT[32], zm),
        kind(always((z == 0) & (x == 3)), VIA_Z, SLOT[-32], zp),
    ]
    on[4] = [
        kind(always((x < 2) & valid(4)), SLOT[4], SLOT[8], xp),
        kind(always(x == 3), SLOT[4], SLOT[-8], xp),
        kind(always((y == 3) & valid(4)), SLOT[4], SLOT[1], yp),
        kind(lambda h: (y == 2) & valid(4) & up_here(h), SLOT[4], VIA_Y, yp),
    ]
    on[-4] = [
        kind(always((x > 1) & valid(-4)), SLOT[-4], SLOT[-8], xm),
        kind(always(x == 0), SLOT[-4], SLOT[8], xm),
        kind(always((y == 0) & valid(-4)), SLOT[-4], SLOT[-1], ym),
        kind(lambda h: (y == 1) & valid(-4) & down_here(h), SLOT[-4], VIA_Y, ym),
    ]
    on[1] = [
        kind(lambda h: valid(1) & ((y < 2) | ((y == 2) & jnp.logical_not(up_here(h)))), SLOT[1], SLOT[2], yp),
        kind(lambda h: (y == 3) & jnp.logical_not(up_here(h)), SLOT[1], SLOT[-2], yp),
        kind(always((c == 1) & valid(1)), SLOT[1], SIDE, pt),
        kind(
            lambda h: (y == 3) & (x < 3) & jnp.logical_not(by_ring_up(x + 1, h)) & jnp.logical_not(across_up(x + 1, h)),
            SLOT[1], VIA_Y, xp,
        ),
    ]
    on[-1] = [
        kind(lambda h: valid(-1) & ((y > 1) | ((y == 1) & up_here(h))), SLOT[-1], SLOT[-2], ym),
        kind(lambda h: (y == 0) & up_here(h), SLOT[-1], SLOT[2], ym),
        kind(always((c == 0) & valid(-1)), SLOT[-1], SIDE, pt),
        kind(
            lambda h: (y == 0) & (x > 0) & jnp.logical_not(by_ring_down(x - 1, h)) & jnp.logical_not(across_down(x - 1, h)),
            SLOT[-1], VIA_Y, xm,
        ),
    ]

    def has_via_y(h):
        up = (y == 3) & ((z > 0) | (x > 0)) & (up_here(h) | jnp.logical_not(across_up(x, h)))
        down = (y == 0) & ((z < 3) | (x < 3)) & (down_here(h) | jnp.logical_not(across_down(x, h)))
        return up | down

    via_z = ((z == 3) & (x == 0)) | ((z == 0) & (x == 3))
    on["y"] = [
        kind(lambda h: (y == 3) & has_via_y(h), VIA_Y, SLOT[2], yp),
        kind(lambda h: (y == 0) & has_via_y(h), VIA_Y, SLOT[-2], ym),
    ]
    on[2] = [
        kind(lambda h: (y == 3) & (x > 0) & jnp.logical_not(by_ring_down(x - 1, h)) & across_down(x - 1, h), SLOT[2], SLOT[-2], xm),
    ]
    on[-2] = [
        kind(lambda h: (y == 0) & (x < 3) & jnp.logical_not(by_ring_up(x + 1, h)) & across_up(x + 1, h), SLOT[-2], SLOT[2], xp),
    ]
    on[8] = [kind(always((x == 3) & (z > 0)), SLOT[8], SLOT[-8], zm)]
    on[-8] = [kind(always((x == 0) & (z < 3)), SLOT[-8], SLOT[8], zp)]
    on[32] = []
    on[-32] = []

    def slot_of(d):
        return VIA_Y if d == "y" else VIA_Z if d == "z" else SLOT[d]

    def comes(d, h):
        return has_via_y(h) if d == "y" else via_z if d == "z" else valid(d)

    def lag(d):
        if d == "z":
            return 1
        if d == "y":
            return pick(((y == 3) & (x == 0)) | ((y == 0) & (x == 3)), 3, 2)
        return hops(d, z, x, y)

    def send(k, h):
        cond, src, dst, device = kinds[k]
        guarded(
            None if cond is None else cond(h),
            lambda: copy(lambda one: one.start(), k, h, src, dst, device),
        )

    def arrived(s, h):
        copy(lambda one: one.wait_recv(), 0, h, s, s, pt)

    def head(h):
        cols = pl.ds(pl.multiple_of(h * DH, DH), DH)
        q = q_ref[:, cols]
        g = g_ref[:, cols]
        top = None
        for t0, w in TILES:
            kt = buf[h, 0, pl.ds(t0, w), :]
            s = nt(q, kt) * (ROOT * math.log2(math.e)) + bias[0:1, t0:t0 + w]
            s_ref[:, t0:t0 + w] = s
            m = jnp.max(s, axis=1, keepdims=True)
            top = m if top is None else jnp.maximum(top, m)
        total = jnp.zeros((TOK, 1), jnp.float32)
        dot = jnp.zeros((TOK, 1), jnp.float32)
        for t0, w in TILES:
            e = jnp.exp2(s_ref[:, t0:t0 + w] - top)
            s_ref[:, t0:t0 + w] = e
            dp = nt(g, buf[h, 1, pl.ds(t0, w), :])
            d_ref[:, t0:t0 + w] = dp
            total = total + jnp.sum(e, axis=1, keepdims=True)
            dot = dot + jnp.sum(e * dp, axis=1, keepdims=True)
        inv = 1.0 / total
        dot = dot * inv
        qu = (nt(up_ref[1, :, cols], q) * ROOT).astype(jnp.bfloat16)
        gu = nt(up_ref[2, :, cols], g).astype(jnp.bfloat16)
        both = jnp.zeros((TOK, 2 * DH), jnp.float32)
        vlow = jnp.zeros((TOK, DH), jnp.float32)
        for t0, w in TILES:
            p = s_ref[:, t0:t0 + w] * inv
            pb = p.astype(jnp.bfloat16)
            ds = (p * (d_ref[:, t0:t0 + w] - dot)).astype(jnp.bfloat16)
            kt = buf[h, 0, pl.ds(t0, w), :]
            lt = lowbuf[pl.ds(t0, w), :]
            both = both + nn(ds, jnp.concatenate([kt, lt], axis=1))
            vlow = vlow + nn(pb, lt)
            acc[0:RANK, t0:t0 + w] += nn(qu, ds)
            acc[RANK:, t0:t0 + w] += nn(gu, pb)
        out0 = (both[:, 0:DH] * ROOT).astype(jnp.bfloat16)
        klow = both[:, DH:DH + RANK] * ROOT
        upart[0:RANK, cols] = (nn(lowt0[...], out0) * NORM).astype(jnp.bfloat16)
        back0[...] += nt(up_ref[0, :, cols], out0)
        lows = jnp.concatenate([klow, vlow[:, RANK:]], axis=1).T.astype(jnp.bfloat16)
        upart[RANK:2 * RANK, cols] = (nn(lows[0:RANK], q) * NORM).astype(jnp.bfloat16)
        upart[2 * RANK:, cols] = (nn(lows[RANK:], g) * NORM).astype(jnp.bfloat16)

    pl.semaphore_wait(barrier, 127)

    def send_own(h):
        @pl.when(h != 1)
        def _():
            for a in range(2):
                load(jnp.maximum(h - 1, 0), a).wait()

        for k in own:
            send(k, h)

    send_own(jnp.int32(0))
    for one in arrays()[:2]:
        one.wait()

    low = nt(x_ref[...], down_ref[...]).astype(jnp.bfloat16)
    lowt0[...] = nt(down_ref[0:RANK, :], x_ref[...]).astype(jnp.bfloat16)
    lowbuf[rows(OWN), :] = low[:, RANK:]
    for one in arrays()[2:]:
        one.wait()

    every = [(d, SLOT[d]) for d in SLOT]
    for d, s in every:
        @pl.when(jnp.logical_not(valid(d)))
        def _(s=s):
            lowbuf[rows(s), :] = jnp.zeros((TOK, DH), jnp.bfloat16)
            rrecv[s] = jnp.zeros((TOK, DH), jnp.bfloat16)

            def zero(h, _):
                for a in range(2):
                    buf[h, a, rows(s), :] = jnp.zeros((TOK, DH), jnp.bfloat16)
                return 0

            lax.fori_loop(0, HEADS, zero, 0)

    @pl.when(jnp.logical_not(side_ok))
    def _():
        lowbuf[rows(SIDE), :] = jnp.zeros((TOK, DH), jnp.bfloat16)
        rrecv[SIDE] = jnp.zeros((TOK, DH), jnp.bfloat16)

        def zero(h, _):
            for a in range(2):
                buf[h, a, rows(SIDE), :] = jnp.zeros((TOK, DH), jnp.bfloat16)
            return 0

        lax.fori_loop(0, HEADS, zero, 0)

    lane = lax.broadcasted_iota(jnp.int32, (8, PAD), 1)
    total_bias = jnp.zeros((8, PAD), jnp.float32)
    for s, (block, ok) in enumerate(
        [(me, None), (pt, None), (side, side_ok)] + [(me - 2 * d, valid(d)) for d in SLOT]
    ):
        kept = mask_ref[0, jnp.clip(block, 0, 127)]
        value = jnp.where(kept > 0, 0.0, MASKED)
        if ok is not None:
            value = jnp.where(ok, value, MASKED)
        inside = (lane >= s * TOK) & (lane < (s + 1) * TOK)
        total_bias = jnp.where(inside, value, total_bias)
    bias[...] = total_bias

    acc[...] = jnp.zeros_like(acc)
    back0[...] = jnp.zeros_like(back0)

    def pair_copy(n, src, dst):
        return pltpu.make_async_remote_copy(
            src_ref=src, dst_ref=dst, send_sem=pair_send.at[n], recv_sem=pair_recv.at[n],
            device_id=(pt,), device_id_type=MESH,
        )

    last = 4
    order = [16, -16, 4, -4, 1, -1, "z", "y", 8, -8, 2, -2, 32, -32]

    def handle(slots, r):
        for d in slots:
            h = r - lag(d)

            @pl.when((h >= 0) & (h < ITEMS) & comes(d, h))
            def _(d=d, h=h):
                arrived(slot_of(d), h)
                for k in on[d]:
                    send(k, h)

    def step(r, _):
        @pl.when(r + LEAD < ITEMS)
        def _():
            send_own(r + LEAD)

        handle(order[:6], r)

        @pl.when((r >= last + 2) & (r <= HEADS + last + 1))
        def _():
            head(r - last - 2)

        handle(order[6:], r)

        @pl.when(r == 0)
        def _():
            pair_copy(0, x_ref, x2).start()

        h = r - last

        @pl.when((h >= 0) & (h < ITEMS))
        def _():
            arrived(PARTNER, h)

            @pl.when(((c == 0) & valid(1)) | ((c == 1) & valid(-1)))
            def _():
                arrived(SIDE, h)

        return 0

    lax.fori_loop(0, ITEMS + last + 1, step, 0)

    for s, _, goes, _, to in direct:
        part = acc[:, s * TOK:(s + 1) * TOK].astype(jnp.bfloat16)
        rsend[s, 0:DH, :] = part[:, 0:DH]
        rsend[s, DH:, :] = jnp.concatenate([part[0:RANK, DH:], part[RANK:, DH:]], axis=1)
        guarded(goes, back_copy(s, to).start)
    pair_copy(1, upart, upart2).start()
    backs[0:RANK, :] = back0[...].astype(jnp.bfloat16)
    pair_copy(2, backs.at[0:RANK], backs2.at[0:RANK]).start()
    pair_copy(0, x_ref, x2).wait_recv()
    pair_copy(1, upart, upart2).wait_recv()
    pair_copy(2, backs.at[0:RANK], backs2.at[0:RANK]).wait_recv()

    def both_up(p, lo, hi):
        r = slice(p * RANK, (p + 1) * RANK)
        return (upart[r, lo:hi].astype(jnp.float32) + upart2[r, lo:hi].astype(jnp.float32)).astype(jnp.bfloat16)

    def both_down(p, start):
        for t in range(0, WIDTH, 512):
            part = nn(backs[p * RANK:(p + 1) * RANK, :], x_ref[:, t:t + 512])
            part = part + nn(backs2[p * RANK:(p + 1) * RANK, :], x2[:, t:t + 512])
            terms[:, start + t:start + t + 512] = (part * NORM).astype(jnp.bfloat16)

    @pl.when(c == 0)
    def _():
        both_down(0, 0)
        terms[:, 3072:3840] = both_up(0, 0, 768)

    @pl.when(c == 1)
    def _():
        terms[:, 0:768] = both_up(0, 768, 1536)
        terms[:, 768:2304] = both_up(1, 0, 1536)
        terms[:, 2304:3840] = both_up(2, 0, 1536)

    here = (x, y, z)

    def peer(axis, at):
        return dev(*(z, at, y, c) if axis == 0 else (z, x, at, c) if axis == 1 else (at, x, y, c))

    def third(ref, k):
        return ref.at[:, k * THIRD:(k + 1) * THIRD]

    def rows16(ref, n):
        return ref.at[pl.ds(pl.multiple_of(n * 16, 16), 16), :]

    def ring_copies(stage, k):
        axis = (k + (0, 1, 2, 0)[stage]) % 3
        mine = here[axis]
        out = []
        for n in (1, 2, 3):
            to, source = (mine + n) % 4, (mine - n + 4) % 4
            if stage == 0:
                src, dst, got = rows16(third(terms, k), to), ring1.at[k, mine], ring1.at[k, source]
            elif stage == 3:
                src = part3.at[k]
                dst, got = rows16(third(result, k), mine), rows16(third(result, k), source)
            else:
                ring, part = ((ring2, part1), (ring3, part2))[stage - 1]
                src, dst, got = part.at[k], ring.at[k, mine], ring.at[k, source]
            slot = (stage * 3 + k) * 3 + n - 1
            out.append(tuple(
                pltpu.make_async_remote_copy(
                    src_ref=src, dst_ref=where, send_sem=ring_send.at[slot], recv_sem=ring_recv.at[slot],
                    device_id=(peer(axis, to),), device_id_type=MESH,
                )
                for where in (dst, got)
            ))
        return out

    def ring_start(stage):
        for k in range(3):
            mine = here[(k + (0, 1, 2, 0)[stage]) % 3]
            if stage == 0:
                ring1[k, mine] = rows16(third(terms, k), mine)[...]
            elif stage == 1:
                ring2[k, mine] = part1[k]
            elif stage == 2:
                ring3[k, mine] = part2[k]
            else:
                rows16(third(result, k), mine)[...] = part3[k]
            for out, _ in ring_copies(stage, k):
                out.start()

    def ring_finish(stage):
        for k in range(3):
            for _, got in ring_copies(stage, k):
                got.wait_recv()
            if stage < 3:
                ring, part = ((ring1, part1), (ring2, part2), (ring3, part3))[stage]
                total = ring[k, 0].astype(jnp.float32)
                for n in range(1, 4):
                    total = total + ring[k, n].astype(jnp.float32)
                part[k] = total.astype(jnp.bfloat16)

    def late_piece(o):
        oz, ox, oy = o // 16, (o // 4) % 4, o % 4
        t = (oy - ox - oz + 8) % 4
        return t < 3, (oz * 4 + ox) * 3 + t

    def place(ref, start, piece):
        return ref.at[
            pl.ds(pl.multiple_of((piece % 4) * 16, 16), 16),
            pl.ds(pl.multiple_of(start + (piece // 4) * 256, 256), 256),
        ]

    def reduce_start(j, of, start, landing):
        def one(n, _):
            o = (i + n) % CHIPS
            owns, piece = of(o)

            @pl.when(owns)
            def _():
                pltpu.make_async_remote_copy(
                    src_ref=place(terms, start, piece), dst_ref=landing.at[63 - n],
                    send_sem=red_send.at[j], recv_sem=red_recv.at[j],
                    device_id=(2 * o + c,), device_id_type=MESH,
                ).start()

            return 0

        lax.fori_loop(1, CHIPS, one, 0)

    def reduce_finish(j, of, start, landing, sums):
        owns, piece = of(i)

        @pl.when(owns)
        def _():
            pltpu.make_async_copy(landing, landing, red_recv.at[j]).wait()
            mine = place(terms, start, piece)[...].astype(jnp.float32)

            def add(n, total):
                return total + landing[n].astype(jnp.float32)

            sums[...] = lax.fori_loop(0, CHIPS - 1, add, mine).astype(jnp.bfloat16)
            pltpu.make_async_copy(sums, place(result, start, piece), gat_recv.at[j]).start()

            def one(n, _):
                o = (i + n) % CHIPS
                pltpu.make_async_remote_copy(
                    src_ref=sums, dst_ref=place(result, start, piece),
                    send_sem=gat_send.at[j], recv_sem=gat_recv.at[j],
                    device_id=(2 * o + c,), device_id_type=MESH,
                ).start()
                return 0

            lax.fori_loop(1, CHIPS, one, 0)

    def gathered(j, start, width):
        part = result.at[:, start:start + width]
        pltpu.make_async_copy(part, part, gat_recv.at[j]).wait()
        pair_copy(4 + j, part, result2.at[:, start:start + width]).start()

    def sent(j, of, landing, pieces):
        owns, _ = of(i)

        @pl.when(owns)
        def _():
            part = landing.at[0:pieces - 1]
            pltpu.make_async_copy(part, part, red_send.at[j]).wait()
            pltpu.make_async_copy(landing, landing, gat_send.at[j]).wait()

        @pl.when(jnp.logical_not(owns))
        def _():
            part = landing.at[0:pieces]
            pltpu.make_async_copy(part, part, red_send.at[j]).wait()

    ring_start(0)
    def drain(h, _):
        for k, (cond, src, dst, device) in enumerate(kinds):
            guarded(
                None if cond is None else cond(h),
                lambda: copy(lambda one: one.wait_send(), k, h, src, dst, device),
            )
        return 0

    lax.fori_loop(0, ITEMS, drain, 0)
    ring_finish(0)
    ring_start(1)

    total = jnp.zeros((TOK, DH), jnp.float32)
    for s, comes_in, _, _, _ in direct:
        guarded(comes_in, back_copy(s, pt).wait_recv)
        total = total + rrecv[s].astype(jnp.float32)
    rest = jnp.concatenate([total[DH:, 0:RANK], total[DH:, RANK:]], axis=0)
    backs[RANK:, :] = (acc[:, 0:TOK] + jnp.concatenate([total[0:DH], rest], axis=1)).astype(jnp.bfloat16)
    pair_copy(3, backs.at[RANK:3 * RANK], backs2.at[RANK:3 * RANK]).start()
    pair_copy(3, backs.at[RANK:3 * RANK], backs2.at[RANK:3 * RANK]).wait_recv()

    @pl.when(c == 0)
    def _():
        both_down(1, EARLY)

    @pl.when(c == 1)
    def _():
        both_down(2, EARLY)

    reduce_start(1, late_piece, EARLY, late_in)
    ring_finish(1)
    ring_start(2)
    back = backs[...].T
    for t in range(0, WIDTH, 512):
        grad_out[:, t:t + 512] = nn(back, down_ref[:, t:t + 512]).astype(jnp.bfloat16)
    leave = pltpu.make_async_copy(grad_out, grad_hbm, grad_sem)
    leave.start()
    ring_finish(2)
    ring_start(3)
    reduce_finish(1, late_piece, EARLY, late_in, late_sum)
    ring_finish(3)

    def early_pair():
        return pair_copy(4, result.at[:, 0:EARLY], result2.at[:, 0:EARLY])

    early_pair().start()
    early_pair().wait_recv()

    def finish_early(a, b):
        down_out[0:RANK, :] = a[:, 0:3072]
        up_out[0:RANK, 0:768] = a[:, 3072:3840]
        up_out[0:RANK, 768:1536] = b[:, 0:768]
        up_out[RANK:2 * RANK, :] = b[:, 768:2304]
        up_out[2 * RANK:, :] = b[:, 2304:3840]

    def finish_late(a, b):
        down_out[RANK:2 * RANK, :] = a[:, EARLY:]
        down_out[2 * RANK:, :] = b[:, EARLY:]

    def finish(f):
        @pl.when(c == 0)
        def _():
            f(result, result2)

        @pl.when(c == 1)
        def _():
            f(result2, result)

    finish(finish_early)
    gathered(1, EARLY, LATE)
    late_pair = pair_copy(5, result.at[:, EARLY:], result2.at[:, EARLY:])
    late_pair.wait_recv()
    finish(finish_late)

    for stage in range(4):
        for k in range(3):
            for out, _ in ring_copies(stage, k):
                out.wait_send()
    sent(1, late_piece, late_in, 48)
    pair_copy(0, x_ref, x2).wait_send()
    pair_copy(1, upart, upart2).wait_send()
    pair_copy(2, backs.at[0:RANK], backs2.at[0:RANK]).wait_send()
    pair_copy(3, backs.at[RANK:3 * RANK], backs2.at[RANK:3 * RANK]).wait_send()
    leave.wait()
    early_pair().wait_send()
    late_pair.wait_send()
    for s, goes, returns, to, owner in direct:
        guarded(returns, back_copy(s, owner).wait_send)


def attention(mask, inputs, queries, output_gradient, keys, values, down_t, up):
    vm = pl.BlockSpec(memory_space=pltpu.VMEM)
    dma = pltpu.SemaphoreType.DMA
    return pl.pallas_call(
        attention_kernel,
        out_shape=(
            jax.ShapeDtypeStruct((TOK, WIDTH), jnp.bfloat16),
            jax.ShapeDtypeStruct((3 * RANK, WIDTH), jnp.bfloat16),
            jax.ShapeDtypeStruct((3 * RANK, FEAT), jnp.bfloat16),
        ),
        in_specs=[pl.BlockSpec(memory_space=pl.ANY)] * 8,
        out_specs=(pl.BlockSpec(memory_space=pl.ANY), vm, vm),
        scratch_shapes=[
            pltpu.VMEM((TOK, WIDTH), jnp.bfloat16),
            dma,
            pltpu.SMEM((1, 128), jnp.int32),
            pltpu.VMEM((TOK, WIDTH), jnp.bfloat16),
            pltpu.VMEM((TOK, FEAT), jnp.bfloat16),
            pltpu.VMEM((TOK, FEAT), jnp.bfloat16),
            pltpu.VMEM((3 * RANK, WIDTH), jnp.bfloat16),
            pltpu.VMEM((3, RANK, FEAT), jnp.bfloat16),
            pltpu.VMEM((HEADS, 2, (SLOTS + 2) * TOK, DH), jnp.bfloat16),
            pltpu.VMEM((KEYS + 2 * TOK, DH), jnp.bfloat16),
            pltpu.VMEM((8, PAD), jnp.float32),
            pltpu.VMEM((TOK, PAD), jnp.float32),
            pltpu.VMEM((TOK, PAD), jnp.float32),
            pltpu.VMEM((2 * RANK, PAD), jnp.float32),
            pltpu.VMEM((RANK, TOK), jnp.float32),
            pltpu.VMEM((RANK, TOK), jnp.bfloat16),
            pltpu.VMEM((SLOTS, TOK, DH), jnp.bfloat16),
            pltpu.VMEM((SLOTS, TOK, DH), jnp.bfloat16),
            pltpu.VMEM((TOK, WIDTH), jnp.bfloat16),
            pltpu.VMEM((3 * RANK, FEAT), jnp.bfloat16),
            pltpu.VMEM((3 * RANK, FEAT), jnp.bfloat16),
            pltpu.VMEM((3 * RANK, TOK), jnp.bfloat16),
            pltpu.VMEM((3 * RANK, TOK), jnp.bfloat16),
            pltpu.VMEM((RANK, EARLY + LATE), jnp.bfloat16),
            pltpu.VMEM((RANK, EARLY + LATE), jnp.bfloat16),
            pltpu.VMEM((RANK, EARLY + LATE), jnp.bfloat16),
            pltpu.VMEM((CHIPS - 1, *PIECE), jnp.bfloat16),
            pltpu.VMEM(PIECE, jnp.bfloat16),
            pltpu.VMEM((3, 4, 16, THIRD), jnp.bfloat16),
            pltpu.VMEM((3, 4, 16, THIRD), jnp.bfloat16),
            pltpu.VMEM((3, 4, 16, THIRD), jnp.bfloat16),
            pltpu.VMEM((3, 16, THIRD), jnp.bfloat16),
            pltpu.VMEM((3, 16, THIRD), jnp.bfloat16),
            pltpu.VMEM((3, 16, THIRD), jnp.bfloat16),
            dma((6,)),
            dma((HEADS, 2)),
            dma((39, ITEMS)),
            dma((SLOTS + 2, ITEMS)),
            dma((SLOTS,)), dma((SLOTS,)),
            dma((6,)), dma((6,)), dma((2,)), dma((2,)), dma((2,)), dma((2,)), dma((36,)), dma((36,)),
        ],
        compiler_params=pltpu.CompilerParams(
            collective_id=0, has_side_effects=True, vmem_limit_bytes=56 * 2**20
        ),
        cost_estimate=pl.CostEstimate(flops=12 * 10**9, bytes_accessed=8 * 10**6, transcendentals=7 * 10**6),
        name="attention_gradients",
    )(mask, inputs, queries, output_gradient, keys, values, down_t, up)


def finish_kernel(grad_in, down_in, up_in, grad, down, up):
    grad[...] = grad_in[...]
    down[...] = down_in[...].astype(jnp.float32)
    up[...] = up_in[...].astype(jnp.float32)


def finished(grad, down, up):
    parts = 3

    def block(width):
        return pl.BlockSpec((TOK, width // parts), lambda n: (0, n))

    specs = [block(WIDTH), block(WIDTH), block(FEAT)]
    return pl.pallas_call(
        finish_kernel,
        grid=(parts,),
        out_shape=(
            jax.ShapeDtypeStruct(grad.shape, grad.dtype),
            jax.ShapeDtypeStruct(down.shape, jnp.float32),
            jax.ShapeDtypeStruct(up.shape, jnp.float32),
        ),
        in_specs=specs,
        out_specs=specs,
        name="final_types",
    )(grad, down, up)


def per_device(
    inputs, queries, keys, values, output_gradient, radial_block_mask,
    adapter_down_weight, adapter_up_weight,
):
    down_t = jnp.swapaxes(adapter_down_weight, 1, 2).reshape(3 * RANK, WIDTH)
    input_gradient, down, up = finished(*attention(
        radial_block_mask, inputs, queries, output_gradient, keys, values, down_t, adapter_up_weight
    ))
    down = jnp.swapaxes(down.reshape(3, RANK, WIDTH), 1, 2)
    return (input_gradient, down, up.reshape(3, RANK, FEAT))


def solution(mesh):
    return jax.shard_map(
        per_device,
        mesh=mesh,
        in_specs=(P("frame", None),) * 5 + (P(), P(), P()),
        out_specs=(P("frame", None), P(), P()),
        check_vma=False,
    )
```

```python
import functools
import math

import jax
import jax.numpy as jnp
from jax import lax
from jax.experimental import pallas as pl
from jax.experimental.pallas import tpu as pltpu
from jax.sharding import PartitionSpec as P

MESH = pl.DeviceIdType.MESH
DH = 128
HEADS = 12
TOK = 192
RANK = 64
WIDTH = 3072
FEAT = HEADS * DH
OWN, PARTNER, SIDE = 0, 1, 2
SLOT = {1: 3, -1: 4, 2: 5, -2: 6, 4: 7, -4: 8, 8: 9, -8: 10, 16: 11, -16: 12, 32: 13, -32: 14}
SLOTS = 15
VIA_Y, VIA_Z = 15, 16
KEYS = SLOTS * TOK
PAD = 3072
TILES = [(0, 512), (512, 512), (1024, 512), (1536, 512), (2048, 512), (2560, 320)]
ROOT = 1.0 / math.sqrt(DH)
MASKED = -1e30
LEAD = 1
ITEMS = HEADS + 1
CHIPS = 64
NORM = 1.0 / math.sqrt(128 * TOK)
EARLY = 3840
THIRD = EARLY // 3
LATE = 3072
PIECE = (16, 256)


def nt(a, b):
    return lax.dot_general(a, b, (((1,), (1,)), ((), ())), preferred_element_type=jnp.float32)


def nn(a, b):
    return lax.dot_general(a, b, (((1,), (0,)), ((), ())), preferred_element_type=jnp.float32)


def pick(cond, a, b):
    return jnp.where(cond, a, b)


def hops(d, z, x, y):
    if abs(d) == 16:
        return 1
    if d == 4:
        return pick(x == 0, 2, 1)
    if d == -4:
        return pick(x == 3, 2, 1)
    if d == 1:
        return pick(y == 0, pick(x == 0, 3, 2), 1)
    if d == -1:
        return pick(y == 3, pick(x == 3, 3, 2), 1)
    if d == 8:
        return pick(x >= 2, 2, 3)
    if d == -8:
        return pick(x <= 1, 2, 3)
    if abs(d) == 32:
        return 2
    if d == 2:
        return pick(y >= 2, 2, pick(x == 0, 4, 3))
    return pick(y <= 1, 2, pick(x == 3, 4, 3))


def attention_kernel(
    mask_hbm, x_hbm, q_hbm, g_hbm, k_ref, v_ref, down_hbm, up_hbm,
    grad_hbm, down_out, up_out,
    grad_out, grad_sem, mask_ref, x_ref, q_ref, g_ref, down_ref, up_ref,
    buf, lowbuf, bias, s_ref, d_ref, acc, back0, lowt0, rsend, rrecv,
    x2, upart, upart2, backs, backs2, terms, result, result2, late_in, late_sum, ring1, ring2, ring3, part1, part2, part3,
    in_sem, load_sem, send_sem, recv_sem, rs_send, rs_recv,
    pair_send, pair_recv, red_send, red_recv, gat_send, gat_recv, ring_send, ring_recv,
):
    me = lax.axis_index("frame")
    i = me // 2
    c = me % 2
    z = i // 16
    x = (i // 4) % 4
    y = i % 4

    def dev(zz, xx, yy, cc):
        return ((zz + 4) % 4) * 32 + ((xx + 4) % 4) * 8 + ((yy + 4) % 4) * 2 + cc

    yp, ym = dev(z, x, y + 1, c), dev(z, x, y - 1, c)
    xp, xm = dev(z, x + 1, y, c), dev(z, x - 1, y, c)
    zp, zm = dev(z + 1, x, y, c), dev(z - 1, x, y, c)
    pt = dev(z, x, y, 1 - c)
    side = pick(c == 0, me - 1, me + 1)
    side_ok = (side >= 0) & (side < 128)

    def valid(d):
        return (i - d >= 0) & (i - d < 64)

    def rows(s):
        return pl.ds(s * TOK, TOK)

    def load(h, a):
        ref = (k_ref, v_ref)[a]
        return pltpu.make_async_copy(
            ref.at[:, pl.ds(h * DH, DH)], buf.at[h, a, rows(OWN)], load_sem.at[h, a]
        )

    for h in range(HEADS):
        for a in range(2):
            load(h, a).start()

    def arrays():
        pairs = [(x_hbm, x_ref), (down_hbm, down_ref), (q_hbm, q_ref), (g_hbm, g_ref), (up_hbm, up_ref)]
        pairs += [(mask_hbm.at[pl.ds(me, 1), :], mask_ref)]
        return [pltpu.make_async_copy(src, dst, in_sem.at[n]) for n, (src, dst) in enumerate(pairs)]

    for one in arrays():
        one.start()

    barrier = pltpu.get_barrier_semaphore()

    def greet(n, _):
        pl.semaphore_signal(barrier, inc=1, device_id=((me + n) % 128,), device_id_type=MESH)
        return 0

    lax.fori_loop(1, 128, greet, 0, unroll=True)

    def back_copy(s, device):
        return pltpu.make_async_remote_copy(
            src_ref=rsend.at[s], dst_ref=rrecv.at[s],
            send_sem=rs_send.at[s], recv_sem=rs_recv.at[s],
            device_id=(device,), device_id_type=MESH,
        )

    direct = [(PARTNER, None, None, pt, pt), (SIDE, side_ok, side_ok, side, side)]
    direct += [(SLOT[d], valid(-d), valid(d), me + 2 * d, me - 2 * d) for d in SLOT]

    def guarded(cond, f):
        if cond is None:
            f()
        else:
            pl.when(cond)(f)

    def copy(act, kind, n, src, dst, device):
        def one(source, target):
            act(pltpu.make_async_remote_copy(
                src_ref=source, dst_ref=target,
                send_sem=send_sem.at[kind, n], recv_sem=recv_sem.at[dst, n],
                device_id=(device,), device_id_type=MESH,
            ))

        @pl.when(n == 1)
        def _():
            one(lowbuf.at[rows(src)], lowbuf.at[rows(dst)])

        @pl.when(n != 1)
        def _():
            h = jnp.maximum(n - 1, 0)
            one(buf.at[h, :, rows(src)], buf.at[h, :, rows(dst)])

    kinds = []

    def kind(cond, src, dst, device):
        kinds.append((cond, src, dst, device))
        return len(kinds) - 1

    mid = (x == 1) | (x == 2)

    def by_ring_up(xx, h):
        return (xx == 0) | (((xx == 1) | (xx == 2)) & (h % 2 == 0))

    def by_ring_down(xx, h):
        return (xx == 3) | (((xx == 1) | (xx == 2)) & (h % 2 == 1))

    def across_up(xx, h):
        return (xx == 3) | ((h // 2) % 2 == 0)

    def across_down(xx, h):
        return (xx == 0) | ((h // 2) % 2 == 0)

    def up_here(h):
        return by_ring_up(x, h)

    def down_here(h):
        return by_ring_down(x, h)

    def always(cond):
        return lambda h: cond

    own = [
        kind(None, OWN, PARTNER, pt),
        kind(always(y < 3), OWN, SLOT[1], yp), kind(always(y > 0), OWN, SLOT[-1], ym),
        kind(always(x < 3), OWN, SLOT[4], xp), kind(always(x > 0), OWN, SLOT[-4], xm),
        kind(always(z < 3), OWN, SLOT[16], zp), kind(always(z > 0), OWN, SLOT[-16], zm),
        kind(always((z == 0) & (x == 0)), OWN, VIA_Z, zm),
        kind(always((z == 3) & (x == 3)), OWN, VIA_Z, zp),
    ]
    on = {}
    on[16] = [
        kind(always((z == 1) & (x != 0)), SLOT[16], SLOT[32], zp),
        kind(always(z == 3), SLOT[16], SLOT[-32], zp),
        kind(always((x == 3) & (z > 0)), SLOT[16], SLOT[4], xp),
    ]
    on[-16] = [
        kind(always((z == 2) & (x != 3)), SLOT[-16], SLOT[-32], zm),
        kind(always(z == 0), SLOT[-16], SLOT[32], zm),
        kind(always((x == 0) & (z < 3)), SLOT[-16], SLOT[-4], xm),
    ]
    on["z"] = [
        kind(always((z == 3) & (x == 0)), VIA_Z, SLOT[32], zm),
        kind(always((z == 0) & (x == 3)), VIA_Z, SLOT[-32], zp),
    ]
    on[4] = [
        kind(always((x < 2) & valid(4)), SLOT[4], SLOT[8], xp),
        kind(always(x == 3), SLOT[4], SLOT[-8], xp),
        kind(always((y == 3) & valid(4)), SLOT[4], SLOT[1], yp),
        kind(lambda h: (y == 2) & valid(4) & up_here(h), SLOT[4], VIA_Y, yp),
    ]
    on[-4] = [
        kind(always((x > 1) & valid(-4)), SLOT[-4], SLOT[-8], xm),
        kind(always(x == 0), SLOT[-4], SLOT[8], xm),
        kind(always((y == 0) & valid(-4)), SLOT[-4], SLOT[-1], ym),
        kind(lambda h: (y == 1) & valid(-4) & down_here(h), SLOT[-4], VIA_Y, ym),
    ]
    on[1] = [
        kind(lambda h: valid(1) & ((y < 2) | ((y == 2) & jnp.logical_not(up_here(h)))), SLOT[1], SLOT[2], yp),
        kind(lambda h: (y == 3) & jnp.logical_not(up_here(h)), SLOT[1], SLOT[-2], yp),
        kind(always((c == 1) & valid(1)), SLOT[1], SIDE, pt),
        kind(
            lambda h: (y == 3) & (x < 3) & jnp.logical_not(by_ring_up(x + 1, h)) & jnp.logical_not(across_up(x + 1, h)),
            SLOT[1], VIA_Y, xp,
        ),
    ]
    on[-1] = [
        kind(lambda h: valid(-1) & ((y > 1) | ((y == 1) & up_here(h))), SLOT[-1], SLOT[-2], ym),
        kind(lambda h: (y == 0) & up_here(h), SLOT[-1], SLOT[2], ym),
        kind(always((c == 0) & valid(-1)), SLOT[-1], SIDE, pt),
        kind(
            lambda h: (y == 0) & (x > 0) & jnp.logical_not(by_ring_down(x - 1, h)) & jnp.logical_not(across_down(x - 1, h)),
            SLOT[-1], VIA_Y, xm,
        ),
    ]

    def has_via_y(h):
        up = (y == 3) & ((z > 0) | (x > 0)) & (up_here(h) | jnp.logical_not(across_up(x, h)))
        down = (y == 0) & ((z < 3) | (x < 3)) & (down_here(h) | jnp.logical_not(across_down(x, h)))
        return up | down

    via_z = ((z == 3) & (x == 0)) | ((z == 0) & (x == 3))
    on["y"] = [
        kind(lambda h: (y == 3) & has_via_y(h), VIA_Y, SLOT[2], yp),
        kind(lambda h: (y == 0) & has_via_y(h), VIA_Y, SLOT[-2], ym),
    ]
    on[2] = [
        kind(lambda h: (y == 3) & (x > 0) & jnp.logical_not(by_ring_down(x - 1, h)) & across_down(x - 1, h), SLOT[2], SLOT[-2], xm),
    ]
    on[-2] = [
        kind(lambda h: (y == 0) & (x < 3) & jnp.logical_not(by_ring_up(x + 1, h)) & across_up(x + 1, h), SLOT[-2], SLOT[2], xp),
    ]
    on[8] = [kind(always((x == 3) & (z > 0)), SLOT[8], SLOT[-8], zm)]
    on[-8] = [kind(always((x == 0) & (z < 3)), SLOT[-8], SLOT[8], zp)]
    on[32] = []
    on[-32] = []

    def slot_of(d):
        return VIA_Y if d == "y" else VIA_Z if d == "z" else SLOT[d]

    def comes(d, h):
        return has_via_y(h) if d == "y" else via_z if d == "z" else valid(d)

    def lag(d):
        if d == "z":
            return 1
        if d == "y":
            return pick(((y == 3) & (x == 0)) | ((y == 0) & (x == 3)), 3, 2)
        return hops(d, z, x, y)

    def send(k, h):
        cond, src, dst, device = kinds[k]
        guarded(
            None if cond is None else cond(h),
            lambda: copy(lambda one: one.start(), k, h, src, dst, device),
        )

    def arrived(s, h):
        copy(lambda one: one.wait_recv(), 0, h, s, s, pt)

    def head(h):
        cols = pl.ds(pl.multiple_of(h * DH, DH), DH)
        q = q_ref[:, cols]
        g = g_ref[:, cols]
        top = None
        for t0, w in TILES:
            kt = buf[h, 0, pl.ds(t0, w), :]
            s = nt(q, kt) * (ROOT * math.log2(math.e)) + bias[0:1, t0:t0 + w]
            s_ref[:, t0:t0 + w] = s
            m = jnp.max(s, axis=1, keepdims=True)
            top = m if top is None else jnp.maximum(top, m)
        total = jnp.zeros((TOK, 1), jnp.float32)
        dot = jnp.zeros((TOK, 1), jnp.float32)
        for t0, w in TILES:
            e = jnp.exp2(s_ref[:, t0:t0 + w] - top)
            s_ref[:, t0:t0 + w] = e
            dp = nt(g, buf[h, 1, pl.ds(t0, w), :])
            d_ref[:, t0:t0 + w] = dp
            total = total + jnp.sum(e, axis=1, keepdims=True)
            dot = dot + jnp.sum(e * dp, axis=1, keepdims=True)
        inv = 1.0 / total
        dot = dot * inv
        qu = (nt(up_ref[1, :, cols], q) * ROOT).astype(jnp.bfloat16)
        gu = nt(up_ref[2, :, cols], g).astype(jnp.bfloat16)
        both = jnp.zeros((TOK, 2 * DH), jnp.float32)
        vlow = jnp.zeros((TOK, DH), jnp.float32)
        for t0, w in TILES:
            p = s_ref[:, t0:t0 + w] * inv
            pb = p.astype(jnp.bfloat16)
            ds = (p * (d_ref[:, t0:t0 + w] - dot)).astype(jnp.bfloat16)
            kt = buf[h, 0, pl.ds(t0, w), :]
            lt = lowbuf[pl.ds(t0, w), :]
            both = both + nn(ds, jnp.concatenate([kt, lt], axis=1))
            vlow = vlow + nn(pb, lt)
            acc[0:RANK, t0:t0 + w] += nn(qu, ds)
            acc[RANK:, t0:t0 + w] += nn(gu, pb)
        out0 = (both[:, 0:DH] * ROOT).astype(jnp.bfloat16)
        klow = both[:, DH:DH + RANK] * ROOT
        upart[0:RANK, cols] = (nn(lowt0[...], out0) * NORM).astype(jnp.bfloat16)
        back0[...] += nt(up_ref[0, :, cols], out0)
        lows = jnp.concatenate([klow, vlow[:, RANK:]], axis=1).T.astype(jnp.bfloat16)
        upart[RANK:2 * RANK, cols] = (nn(lows[0:RANK], q) * NORM).astype(jnp.bfloat16)
        upart[2 * RANK:, cols] = (nn(lows[RANK:], g) * NORM).astype(jnp.bfloat16)

    pl.semaphore_wait(barrier, 127)

    def send_own(h):
        @pl.when(h != 1)
        def _():
            for a in range(2):
                load(jnp.maximum(h - 1, 0), a).wait()

        for k in own:
            send(k, h)

    send_own(jnp.int32(0))
    for one in arrays()[:2]:
        one.wait()

    low = nt(x_ref[...], down_ref[...]).astype(jnp.bfloat16)
    lowt0[...] = nt(down_ref[0:RANK, :], x_ref[...]).astype(jnp.bfloat16)
    lowbuf[rows(OWN), :] = low[:, RANK:]
    for one in arrays()[2:]:
        one.wait()

    every = [(d, SLOT[d]) for d in SLOT]
    for d, s in every:
        @pl.when(jnp.logical_not(valid(d)))
        def _(s=s):
            lowbuf[rows(s), :] = jnp.zeros((TOK, DH), jnp.bfloat16)
            rrecv[s] = jnp.zeros((TOK, DH), jnp.bfloat16)

            def zero(h, _):
                for a in range(2):
                    buf[h, a, rows(s), :] = jnp.zeros((TOK, DH), jnp.bfloat16)
                return 0

            lax.fori_loop(0, HEADS, zero, 0)

    @pl.when(jnp.logical_not(side_ok))
    def _():
        lowbuf[rows(SIDE), :] = jnp.zeros((TOK, DH), jnp.bfloat16)
        rrecv[SIDE] = jnp.zeros((TOK, DH), jnp.bfloat16)

        def zero(h, _):
            for a in range(2):
                buf[h, a, rows(SIDE), :] = jnp.zeros((TOK, DH), jnp.bfloat16)
            return 0

        lax.fori_loop(0, HEADS, zero, 0)

    lane = lax.broadcasted_iota(jnp.int32, (8, PAD), 1)
    total_bias = jnp.zeros((8, PAD), jnp.float32)
    for s, (block, ok) in enumerate(
        [(me, None), (pt, None), (side, side_ok)] + [(me - 2 * d, valid(d)) for d in SLOT]
    ):
        kept = mask_ref[0, jnp.clip(block, 0, 127)]
        value = jnp.where(kept > 0, 0.0, MASKED)
        if ok is not None:
            value = jnp.where(ok, value, MASKED)
        inside = (lane >= s * TOK) & (lane < (s + 1) * TOK)
        total_bias = jnp.where(inside, value, total_bias)
    bias[...] = total_bias

    acc[...] = jnp.zeros_like(acc)
    back0[...] = jnp.zeros_like(back0)

    def pair_copy(n, src, dst):
        return pltpu.make_async_remote_copy(
            src_ref=src, dst_ref=dst, send_sem=pair_send.at[n], recv_sem=pair_recv.at[n],
            device_id=(pt,), device_id_type=MESH,
        )

    last = 4
    order = [16, -16, 4, -4, 1, -1, "z", "y", 8, -8, 2, -2, 32, -32]

    def handle(slots, r):
        for d in slots:
            h = r - lag(d)

            @pl.when((h >= 0) & (h < ITEMS) & comes(d, h))
            def _(d=d, h=h):
                arrived(slot_of(d), h)
                for k in on[d]:
                    send(k, h)

    def step(r, _):
        @pl.when(r + LEAD < ITEMS)
        def _():
            send_own(r + LEAD)

        handle(order[:6], r)

        @pl.when((r >= last + 2) & (r <= HEADS + last + 1))
        def _():
            head(r - last - 2)

        handle(order[6:], r)

        @pl.when(r == 0)
        def _():
            pair_copy(0, x_ref, x2).start()

        h = r - last

        @pl.when((h >= 0) & (h < ITEMS))
        def _():
            arrived(PARTNER, h)

            @pl.when(((c == 0) & valid(1)) | ((c == 1) & valid(-1)))
            def _():
                arrived(SIDE, h)

        return 0

    lax.fori_loop(0, ITEMS + last + 1, step, 0)

    for s, _, goes, _, to in direct:
        part = acc[:, s * TOK:(s + 1) * TOK].astype(jnp.bfloat16)
        rsend[s, 0:DH, :] = part[:, 0:DH]
        rsend[s, DH:, :] = jnp.concatenate([part[0:RANK, DH:], part[RANK:, DH:]], axis=1)
        guarded(goes, back_copy(s, to).start)
    pair_copy(1, upart, upart2).start()
    backs[0:RANK, :] = back0[...].astype(jnp.bfloat16)
    pair_copy(2, backs.at[0:RANK], backs2.at[0:RANK]).start()
    pair_copy(0, x_ref, x2).wait_recv()
    pair_copy(1, upart, upart2).wait_recv()
    pair_copy(2, backs.at[0:RANK], backs2.at[0:RANK]).wait_recv()

    def both_up(p, lo, hi):
        r = slice(p * RANK, (p + 1) * RANK)
        return (upart[r, lo:hi].astype(jnp.float32) + upart2[r, lo:hi].astype(jnp.float32)).astype(jnp.bfloat16)

    def own_down(p):
        for t in range(0, WIDTH, 512):
            s_ref[0:RANK, t:t + 512] = nn(backs[p * RANK:(p + 1) * RANK, :], x_ref[:, t:t + 512])

    def both_down(p, start):
        for t in range(0, WIDTH, 512):
            part = s_ref[0:RANK, t:t + 512] + nn(backs2[p * RANK:(p + 1) * RANK, :], x2[:, t:t + 512])
            terms[:, start + t:start + t + 512] = (part * NORM).astype(jnp.bfloat16)

    @pl.when(c == 0)
    def _():
        own_down(0)
        both_down(0, 0)
        terms[:, 3072:3840] = both_up(0, 0, 768)

    @pl.when(c == 1)
    def _():
        terms[:, 0:768] = both_up(0, 768, 1536)
        terms[:, 768:2304] = both_up(1, 0, 1536)
        terms[:, 2304:3840] = both_up(2, 0, 1536)

    here = (x, y, z)

    def peer(axis, at):
        return dev(*(z, at, y, c) if axis == 0 else (z, x, at, c) if axis == 1 else (at, x, y, c))

    def third(ref, k):
        return ref.at[:, k * THIRD:(k + 1) * THIRD]

    def rows16(ref, n):
        return ref.at[pl.ds(pl.multiple_of(n * 16, 16), 16), :]

    def ring_copies(stage, k):
        axis = (k + (0, 1, 2, 0)[stage]) % 3
        mine = here[axis]
        out = []
        for n in (1, 2, 3):
            to, source = (mine + n) % 4, (mine - n + 4) % 4
            if stage == 0:
                src, dst, got = rows16(third(terms, k), to), ring1.at[k, mine], ring1.at[k, source]
            elif stage == 3:
                src = part3.at[k]
                dst, got = rows16(third(result, k), mine), rows16(third(result, k), source)
            else:
                ring, part = ((ring2, part1), (ring3, part2))[stage - 1]
                src, dst, got = part.at[k], ring.at[k, mine], ring.at[k, source]
            slot = (stage * 3 + k) * 3 + n - 1
            out.append(tuple(
                pltpu.make_async_remote_copy(
                    src_ref=src, dst_ref=where, send_sem=ring_send.at[slot], recv_sem=ring_recv.at[slot],
                    device_id=(peer(axis, to),), device_id_type=MESH,
                )
                for where in (dst, got)
            ))
        return out

    def ring_start(stage):
        for k in range(3):
            mine = here[(k + (0, 1, 2, 0)[stage]) % 3]
            if stage == 0:
                ring1[k, mine] = rows16(third(terms, k), mine)[...]
            elif stage == 1:
                ring2[k, mine] = part1[k]
            elif stage == 2:
                ring3[k, mine] = part2[k]
            else:
                rows16(third(result, k), mine)[...] = part3[k]
            for out, _ in ring_copies(stage, k):
                out.start()

    def ring_finish(stage):
        for k in range(3):
            for _, got in ring_copies(stage, k):
                got.wait_recv()
            if stage < 3:
                ring, part = ((ring1, part1), (ring2, part2), (ring3, part3))[stage]
                total = ring[k, 0].astype(jnp.float32)
                for n in range(1, 4):
                    total = total + ring[k, n].astype(jnp.float32)
                part[k] = total.astype(jnp.bfloat16)

    def late_piece(o):
        oz, ox, oy = o // 16, (o // 4) % 4, o % 4
        t = (oy - ox - oz + 8) % 4
        return t < 3, (oz * 4 + ox) * 3 + t

    def place(ref, start, piece):
        return ref.at[
            pl.ds(pl.multiple_of((piece % 4) * 16, 16), 16),
            pl.ds(pl.multiple_of(start + (piece // 4) * 256, 256), 256),
        ]

    def reduce_start(j, of, start, landing):
        def one(n, _):
            o = (i + n) % CHIPS
            owns, piece = of(o)

            @pl.when(owns)
            def _():
                pltpu.make_async_remote_copy(
                    src_ref=place(terms, start, piece), dst_ref=landing.at[63 - n],
                    send_sem=red_send.at[j], recv_sem=red_recv.at[j],
                    device_id=(2 * o + c,), device_id_type=MESH,
                ).start()

            return 0

        lax.fori_loop(1, CHIPS, one, 0)

    def reduce_finish(j, of, start, landing, sums):
        owns, piece = of(i)

        @pl.when(owns)
        def _():
            pltpu.make_async_copy(landing, landing, red_recv.at[j]).wait()
            mine = place(terms, start, piece)[...].astype(jnp.float32)

            def add(n, total):
                return total + landing[n].astype(jnp.float32)

            sums[...] = lax.fori_loop(0, CHIPS - 1, add, mine, unroll=9).astype(jnp.bfloat16)
            pltpu.make_async_copy(sums, place(result, start, piece), gat_recv.at[j]).start()

            def one(n, _):
                o = (i + n) % CHIPS
                pltpu.make_async_remote_copy(
                    src_ref=sums, dst_ref=place(result, start, piece),
                    send_sem=gat_send.at[j], recv_sem=gat_recv.at[j],
                    device_id=(2 * o + c,), device_id_type=MESH,
                ).start()
                return 0

            lax.fori_loop(1, CHIPS, one, 0)

    def gathered(j, start, width):
        part = result.at[:, start:start + width]
        pltpu.make_async_copy(part, part, gat_recv.at[j]).wait()
        pair_copy(4 + j, part, result2.at[:, start:start + width]).start()

    def sent(j, of, landing, pieces):
        owns, _ = of(i)

        @pl.when(owns)
        def _():
            part = landing.at[0:pieces - 1]
            pltpu.make_async_copy(part, part, red_send.at[j]).wait()
            pltpu.make_async_copy(landing, landing, gat_send.at[j]).wait()

        @pl.when(jnp.logical_not(owns))
        def _():
            part = landing.at[0:pieces]
            pltpu.make_async_copy(part, part, red_send.at[j]).wait()

    ring_start(0)
    def drain(h, _):
        for k, (cond, src, dst, device) in enumerate(kinds):
            guarded(
                None if cond is None else cond(h),
                lambda: copy(lambda one: one.wait_send(), k, h, src, dst, device),
            )
        return 0

    lax.fori_loop(0, ITEMS, drain, 0)
    ring_finish(0)
    ring_start(1)

    total = jnp.zeros((TOK, DH), jnp.float32)
    for s, comes_in, _, _, _ in direct:
        guarded(comes_in, back_copy(s, pt).wait_recv)
        total = total + rrecv[s].astype(jnp.float32)
    rest = jnp.concatenate([total[DH:, 0:RANK], total[DH:, RANK:]], axis=0)
    backs[RANK:, :] = (acc[:, 0:TOK] + jnp.concatenate([total[0:DH], rest], axis=1)).astype(jnp.bfloat16)
    pair_copy(3, backs.at[RANK:3 * RANK], backs2.at[RANK:3 * RANK]).start()

    @pl.when(c == 0)
    def _():
        own_down(1)

    @pl.when(c == 1)
    def _():
        own_down(2)

    pair_copy(3, backs.at[RANK:3 * RANK], backs2.at[RANK:3 * RANK]).wait_recv()

    @pl.when(c == 0)
    def _():
        both_down(1, EARLY)

    @pl.when(c == 1)
    def _():
        both_down(2, EARLY)

    reduce_start(1, late_piece, EARLY, late_in)
    ring_finish(1)
    ring_start(2)
    back = backs[...].T
    for t in range(0, WIDTH, 512):
        grad_out[:, t:t + 512] = nn(back, down_ref[:, t:t + 512]).astype(jnp.bfloat16)
    leave = pltpu.make_async_copy(grad_out, grad_hbm, grad_sem)
    leave.start()
    ring_finish(2)
    ring_start(3)
    reduce_finish(1, late_piece, EARLY, late_in, late_sum)
    ring_finish(3)

    def early_pair():
        return pair_copy(4, result.at[:, 0:EARLY], result2.at[:, 0:EARLY])

    early_pair().start()
    early_pair().wait_recv()

    def finish_early(a, b):
        down_out[0:RANK, :] = a[:, 0:3072]
        up_out[0:RANK, 0:768] = a[:, 3072:3840]
        up_out[0:RANK, 768:1536] = b[:, 0:768]
        up_out[RANK:2 * RANK, :] = b[:, 768:2304]
        up_out[2 * RANK:, :] = b[:, 2304:3840]

    def finish_late(a, b):
        down_out[RANK:2 * RANK, :] = a[:, EARLY:]
        down_out[2 * RANK:, :] = b[:, EARLY:]

    def finish(f):
        @pl.when(c == 0)
        def _():
            f(result, result2)

        @pl.when(c == 1)
        def _():
            f(result2, result)

    finish(finish_early)
    gathered(1, EARLY, LATE)
    late_pair = pair_copy(5, result.at[:, EARLY:], result2.at[:, EARLY:])
    late_pair.wait_recv()
    finish(finish_late)

    for stage in range(4):
        for k in range(3):
            for out, _ in ring_copies(stage, k):
                out.wait_send()
    sent(1, late_piece, late_in, 48)
    pair_copy(0, x_ref, x2).wait_send()
    pair_copy(1, upart, upart2).wait_send()
    pair_copy(2, backs.at[0:RANK], backs2.at[0:RANK]).wait_send()
    pair_copy(3, backs.at[RANK:3 * RANK], backs2.at[RANK:3 * RANK]).wait_send()
    leave.wait()
    early_pair().wait_send()
    late_pair.wait_send()
    for s, goes, returns, to, owner in direct:
        guarded(returns, back_copy(s, owner).wait_send)


def attention(mask, inputs, queries, output_gradient, keys, values, down_t, up):
    vm = pl.BlockSpec(memory_space=pltpu.VMEM)
    dma = pltpu.SemaphoreType.DMA
    return pl.pallas_call(
        attention_kernel,
        out_shape=(
            jax.ShapeDtypeStruct((TOK, WIDTH), jnp.bfloat16),
            jax.ShapeDtypeStruct((3 * RANK, WIDTH), jnp.bfloat16),
            jax.ShapeDtypeStruct((3 * RANK, FEAT), jnp.bfloat16),
        ),
        in_specs=[pl.BlockSpec(memory_space=pl.ANY)] * 8,
        out_specs=(pl.BlockSpec(memory_space=pl.ANY), vm, vm),
        scratch_shapes=[
            pltpu.VMEM((TOK, WIDTH), jnp.bfloat16),
            dma,
            pltpu.SMEM((1, 128), jnp.int32),
            pltpu.VMEM((TOK, WIDTH), jnp.bfloat16),
            pltpu.VMEM((TOK, FEAT), jnp.bfloat16),
            pltpu.VMEM((TOK, FEAT), jnp.bfloat16),
            pltpu.VMEM((3 * RANK, WIDTH), jnp.bfloat16),
            pltpu.VMEM((3, RANK, FEAT), jnp.bfloat16),
            pltpu.VMEM((HEADS, 2, (SLOTS + 2) * TOK, DH), jnp.bfloat16),
            pltpu.VMEM((KEYS + 2 * TOK, DH), jnp.bfloat16),
            pltpu.VMEM((8, PAD), jnp.float32),
            pltpu.VMEM((TOK, PAD), jnp.float32),
            pltpu.VMEM((TOK, PAD), jnp.float32),
            pltpu.VMEM((2 * RANK, PAD), jnp.float32),
            pltpu.VMEM((RANK, TOK), jnp.float32),
            pltpu.VMEM((RANK, TOK), jnp.bfloat16),
            pltpu.VMEM((SLOTS, TOK, DH), jnp.bfloat16),
            pltpu.VMEM((SLOTS, TOK, DH), jnp.bfloat16),
            pltpu.VMEM((TOK, WIDTH), jnp.bfloat16),
            pltpu.VMEM((3 * RANK, FEAT), jnp.bfloat16),
            pltpu.VMEM((3 * RANK, FEAT), jnp.bfloat16),
            pltpu.VMEM((3 * RANK, TOK), jnp.bfloat16),
            pltpu.VMEM((3 * RANK, TOK), jnp.bfloat16),
            pltpu.VMEM((RANK, EARLY + LATE), jnp.bfloat16),
            pltpu.VMEM((RANK, EARLY + LATE), jnp.bfloat16),
            pltpu.VMEM((RANK, EARLY + LATE), jnp.bfloat16),
            pltpu.VMEM((CHIPS - 1, *PIECE), jnp.bfloat16),
            pltpu.VMEM(PIECE, jnp.bfloat16),
            pltpu.VMEM((3, 4, 16, THIRD), jnp.bfloat16),
            pltpu.VMEM((3, 4, 16, THIRD), jnp.bfloat16),
            pltpu.VMEM((3, 4, 16, THIRD), jnp.bfloat16),
            pltpu.VMEM((3, 16, THIRD), jnp.bfloat16),
            pltpu.VMEM((3, 16, THIRD), jnp.bfloat16),
            pltpu.VMEM((3, 16, THIRD), jnp.bfloat16),
            dma((6,)),
            dma((HEADS, 2)),
            dma((39, ITEMS)),
            dma((SLOTS + 2, ITEMS)),
            dma((SLOTS,)), dma((SLOTS,)),
            dma((6,)), dma((6,)), dma((2,)), dma((2,)), dma((2,)), dma((2,)), dma((36,)), dma((36,)),
        ],
        compiler_params=pltpu.CompilerParams(
            collective_id=0, has_side_effects=True, vmem_limit_bytes=56 * 2**20
        ),
        cost_estimate=pl.CostEstimate(flops=12 * 10**9, bytes_accessed=8 * 10**6, transcendentals=7 * 10**6),
        name="attention_gradients",
    )(mask, inputs, queries, output_gradient, keys, values, down_t, up)


def finish_kernel(grad_in, down_in, up_in, grad, down, up):
    grad[...] = grad_in[...]
    down[...] = down_in[...].astype(jnp.float32)
    up[...] = up_in[...].astype(jnp.float32)


def finished(grad, down, up):
    parts = 3

    def block(width):
        return pl.BlockSpec((TOK, width // parts), lambda n: (0, n))

    specs = [block(WIDTH), block(WIDTH), block(FEAT)]
    return pl.pallas_call(
        finish_kernel,
        grid=(parts,),
        out_shape=(
            jax.ShapeDtypeStruct(grad.shape, grad.dtype),
            jax.ShapeDtypeStruct(down.shape, jnp.float32),
            jax.ShapeDtypeStruct(up.shape, jnp.float32),
        ),
        in_specs=specs,
        out_specs=specs,
        name="final_types",
    )(grad, down, up)


def per_device(
    inputs, queries, keys, values, output_gradient, radial_block_mask,
    adapter_down_weight, adapter_up_weight,
):
    down_t = jnp.swapaxes(adapter_down_weight, 1, 2).reshape(3 * RANK, WIDTH)
    input_gradient, down, up = finished(*attention(
        radial_block_mask, inputs, queries, output_gradient, keys, values, down_t, adapter_up_weight
    ))
    down = jnp.swapaxes(down.reshape(3, RANK, WIDTH), 1, 2)
    return (input_gradient, down, up.reshape(3, RANK, FEAT))


def solution(mesh):
    return jax.shard_map(
        per_device,
        mesh=mesh,
        in_specs=(P("frame", None),) * 5 + (P(), P(), P()),
        out_specs=(P("frame", None), P(), P()),
        check_vma=False,
    )
```
